32 devices in a mesh: bx: 8 (over z, x), by: 2 (over y), cores: 2 (over core).
Axes of the slice: x: 2, y: 2, z: 4, core: 2. Of those that a mesh axis runs over, the one named last changes fastest.
Arguments:
- weights: float32 [16, 2, 2, 16, 16, 1024], P(('bx', 'cores'), 'by'), may hold values from -6 to 6
- speed_modes: float32 [4, 4], replicated, may hold values from -0.05 to 0.05
Outputs:
- radon_weights: float32 [16, 2, 2, 16, 16, 1024], P(('bx', 'cores'), 'by')
The draws below stay inside these ranges and needn't reach their ends.
All inputs are finite; a program needn't handle non-finite values.
Results may differ from the reference program's by a relative error of at most 0.02.
Values sent between devices are 32-bit elements; how exact they have to be, the bound alone decides.
No kernel may reach another device: no remote copies, remote signals or barrier semaphores. Data moves between devices by JAX's collectives and lax.ppermute only.
A program may use at most 128 MiB of HBM per device.

```python
import math
from functools import partial
import jax
import jax.numpy as jnp
import numpy as np
from jax import lax

N = 8192
Q = 16
MODES = 4
TGT = 32
PAIRS = 1024
SBX = 16
SBY = 2
XB = 3
YB = 1


def shard_levels(rng, dims, cuts, least, top_value):
    gain = 1.0
    for dim, shards_of in cuts:
        heights = jax.random.uniform(jax.random.fold_in(jax.random.fold_in(rng, 6), dim), (shards_of,), jnp.float32, least / len(cuts), top_value / len(cuts))
        gain = gain * jnp.repeat(jnp.exp(heights), dims[dim] // shards_of).reshape((-1,) + (1,) * (len(dims) - 1 - dim))
    return gain


def bell_draw(own_key, shape, width, most, cuts=(), kind=jnp.bfloat16):
    drawn = jax.random.normal(own_key, shape, jnp.float32) * width
    if len(cuts) > 0:
        drawn = shard_levels(own_key, shape, cuts, -0.22, 0.18) * drawn
    return jnp.clip(drawn, min=-most, max=most).astype(kind)


def setup_inputs(seed: int = 0) -> dict:
    key_list = jax.random.split(jax.random.key(seed), 3)
    return {
        "weights": bell_draw(key_list[0], (SBX, SBY, 2, Q, Q, PAIRS), 1.0, 6.0, ((0, 16), (1, 2)), jnp.float32),
        "speed_modes": jnp.clip(jax.random.uniform(key_list[1], (MODES, MODES), jnp.float32, -0.05, 0.05), -0.05, 0.05),
    }


def cheb_nodes(degree):
    return np.cos(np.pi * (2 * np.arange(degree) + 1) / (2 * degree))

def lagrange_table(degree):
    points = cheb_nodes(degree)
    result = np.ones((degree, 2 * degree))
    for child_side in range(2):
        inside = (points + 2 * child_side - 1) / 2
        for node_row in range(degree):
            for node_other in range(degree):
                if node_other != node_row:
                    result[node_row, child_side * degree:(child_side + 1) * degree] *= (inside - points[node_other]) / (points[node_row] - points[node_other])
    return result

def speed_of(speed_modes, target_one, target_two):
    mode_count = speed_modes.shape[0]
    frequencies = jnp.arange(mode_count).astype(jnp.float32) * math.pi
    along_one = jnp.cos(frequencies[:, None] * target_one[None, :])
    along_two = jnp.cos(frequencies[:, None] * target_two[None, :])
    blended = jnp.dot(speed_modes, along_two, preferred_element_type=jnp.float32, precision=lax.Precision.HIGHEST)
    return 1.0 + lax.optimization_barrier(jnp.sum(blended * along_one, axis=0))

def rotation(target_one, target_two, speed_value, wave_one, wave_two):
    phase = target_one * wave_one + target_two * wave_two + speed_value * jnp.sqrt(wave_one * wave_one + wave_two * wave_two)
    phase = phase - jnp.floor(phase)
    angle = 2.0 * math.pi * phase
    return (jnp.cos(angle), jnp.sin(angle))

def node_phase(layout, speed_value, center, half_width, degree):
    target_one, target_two, merge_dim, centers, child_half, other_center, other_half = layout
    points = jnp.asarray(cheb_nodes(degree), jnp.float32)
    merged = center[None, :] + half_width * points[:, None]
    across = other_center[None, :] + other_half * points[:, None]
    if merge_dim == 0:
        return rotation(target_one, target_two, speed_value, merged[:, None, :], across[None, :, :])
    return rotation(target_one, target_two, speed_value, across[:, None, :], merged[None, :, :])

def merge_children(child_low, child_high, layout, speed_modes):
    target_one, target_two, merge_dim, centers, child_half, other_center, other_half = layout
    degree = child_low.shape[1]
    speed_value = speed_of(speed_modes, target_one, target_two)
    lagrange = jnp.asarray(lagrange_table(degree), jnp.float32)
    pieces = []
    for child, center in ((child_low, centers[0]), (child_high, centers[1])):
        cosine, sine_part = node_phase(layout, speed_value, center, child_half, degree)
        real_part = child[0] * cosine + child[1] * sine_part
        imag_part = child[1] * cosine - child[0] * sine_part
        pieces.append(jnp.stack([real_part, imag_part]))
    stacked = jnp.concatenate(pieces, axis=1 + merge_dim)
    if merge_dim == 0:
        blended = jnp.einsum('ij,rjks->riks', lagrange, stacked, precision=lax.Precision.HIGHEST)
    else:
        blended = jnp.einsum('kj,rijs->riks', lagrange, stacked, precision=lax.Precision.HIGHEST)
    cosine, sine_part = node_phase(layout, speed_value, centers[2], 2.0 * child_half, degree)
    return jnp.stack([blended[0] * cosine - blended[1] * sine_part, blended[0] * sine_part + blended[1] * cosine])

def reversed_bits(box_code, bit_count):
    result = jnp.zeros_like(box_code)
    for bit_place in range(bit_count):
        result = result + box_code // 2 ** bit_place % 2 * 2 ** (bit_count - 1 - bit_place)
    return result

def x_layout(level_index, box_code, targets, y_box, geometry):
    extent, side_count, src_x, src_y = geometry
    span_size = 2 ** (level_index + 1)
    row_index = targets // side_count * span_size + reversed_bits(box_code, level_index + 1)
    target_one = (row_index.astype(jnp.float32) + 0.5) / (side_count * span_size)
    target_two = ((targets % side_count).astype(jnp.float32) + 0.5) / side_count
    parent = (box_code // span_size).astype(jnp.float32)
    child_width = extent * 2 ** level_index / src_x
    low_center = -extent / 2 + (2.0 * parent + 0.5) * child_width
    high_center = low_center + child_width
    parent_center = -extent / 2 + (parent + 0.5) * (2.0 * child_width)
    other_center = jnp.zeros_like(target_one) + (-extent / 2 + (jnp.asarray(y_box).astype(jnp.float32) + 0.5) * (extent / src_y))
    return (target_one, target_two, 0, (low_center, high_center, parent_center), child_width / 2, other_center, extent / (2 * src_y))

def y_layout(level_index, box_code, targets, x_code, x_bits, geometry):
    extent, side_count, src_x, src_y = geometry
    span_size = 2 ** (level_index + 1)
    col_index = targets % side_count * span_size + reversed_bits(box_code, level_index + 1)
    target_two = (col_index.astype(jnp.float32) + 0.5) / (side_count * span_size)
    row_index = targets // side_count * src_x + reversed_bits(x_code, x_bits)
    target_one = (row_index.astype(jnp.float32) + 0.5) / (side_count * src_x)
    parent = (box_code // span_size).astype(jnp.float32)
    child_width = extent * 2 ** level_index / src_y
    low_center = -extent / 2 + (2.0 * parent + 0.5) * child_width
    high_center = low_center + child_width
    parent_center = -extent / 2 + (parent + 0.5) * (2.0 * child_width)
    other_center = jnp.zeros_like(target_one)
    return (target_one, target_two, 1, (low_center, high_center, parent_center), child_width / 2, other_center, extent / 2)

def tree_level(packed_block, level_index, box_count, targets, layout_fn, speed_modes):
    degree = packed_block.shape[1]
    pieces = targets.shape[0]
    groups = box_count // 2 ** (level_index + 1)
    inner_size = 2 ** level_index * pieces
    shaped = packed_block.reshape(2, degree, degree, groups, 2, inner_size)
    child_low = shaped[:, :, :, :, 0, :].reshape(2, degree, degree, groups * inner_size)
    child_high = shaped[:, :, :, :, 1, :].reshape(2, degree, degree, groups * inner_size)
    slot_index = jnp.arange(groups * inner_size, dtype=jnp.int32)
    outer_index = slot_index // inner_size
    inner_index = slot_index % inner_size
    tiled_pairs = jnp.tile(targets, groups * 2 ** level_index)
    results = []
    for own_bit in range(2):
        box_codes = outer_index * 2 ** (level_index + 1) + own_bit * 2 ** level_index + inner_index // pieces
        merged = merge_children(child_low, child_high, layout_fn(level_index, box_codes, tiled_pairs), speed_modes)
        results.append(merged.reshape(2, degree, degree, groups, inner_size))
    return jnp.stack(results, axis=4).reshape(2, degree, degree, box_count * pieces)

def reference(weights, speed_modes):
    x_bits = XB + 1
    geometry = (float(N), TGT, SBX, SBY)
    targets = jnp.arange(PAIRS, dtype=jnp.int32)
    by_rows = jnp.transpose(weights, (1, 2, 3, 4, 0, 5)).reshape(SBY, 2, Q, Q, SBX * PAIRS)

    def x_phase(packed):
        y_box, packed_block = packed
        for level_index in range(x_bits):
            packed_block = tree_level(packed_block, level_index, SBX, targets, partial(x_layout, y_box=y_box, geometry=geometry), speed_modes)
        return packed_block
    after_first = lax.map(x_phase, (jnp.arange(SBY, dtype=jnp.int32), by_rows))
    by_cols = jnp.transpose(after_first.reshape(SBY, 2, Q, Q, SBX, PAIRS), (4, 1, 2, 3, 0, 5)).reshape(SBX, 2, Q, Q, SBY * PAIRS)

    def y_phase(packed):
        x_code, packed_block = packed
        for level_index in range(YB):
            packed_block = tree_level(packed_block, level_index, SBY, targets, partial(y_layout, x_code=x_code, x_bits=x_bits, geometry=geometry), speed_modes)
        return packed_block
    after_second = lax.map(y_phase, (jnp.arange(SBX, dtype=jnp.int32), by_cols))
    return jnp.transpose(after_second.reshape(SBX, 2, Q, Q, SBY, PAIRS), (0, 4, 1, 2, 3, 5))
```

```python
from functools import partial
import math

import jax
import jax.numpy as jnp
import numpy as np
from jax import lax
from jax.experimental import pallas as pl
from jax.experimental.pallas import tpu as pltpu
from jax.sharding import PartitionSpec as P

N = 8192
TGT = 32


def partner_2(value, axis, apart):
    mask = 2**apart
    pairs = [(source, source ^ mask) for source in range(lax.axis_size(axis))]
    return lax.ppermute(value, axis, pairs)


def cheb_nodes(degree):
    return np.cos(np.pi * (2 * np.arange(degree) + 1) / (2 * degree))


def lagrange_table(degree):
    points = cheb_nodes(degree)
    result = np.ones((degree, 2 * degree))
    for child_side in range(2):
        inside = (points + 2 * child_side - 1) / 2
        for node_row in range(degree):
            for node_other in range(degree):
                if node_other != node_row:
                    result[node_row, child_side * degree : (child_side + 1) * degree] *= (
                        inside - points[node_other]
                    ) / (points[node_row] - points[node_other])
    return result


def speed_of(speed_modes, target_one, target_two):
    mode_count = speed_modes.shape[0]
    frequencies = jnp.arange(mode_count).astype(jnp.float32) * math.pi
    along_one = jnp.cos(frequencies[:, None] * target_one[None, :])
    along_two = jnp.cos(frequencies[:, None] * target_two[None, :])
    blended = jnp.dot(
        speed_modes, along_two, preferred_element_type=jnp.float32, precision=lax.Precision.HIGHEST
    )
    return 1.0 + jnp.sum(blended * along_one, axis=0)


def rotation(target_one, target_two, speed_value, wave_one, wave_two):
    phase = (
        target_one * wave_one
        + target_two * wave_two
        + speed_value * jnp.sqrt(wave_one * wave_one + wave_two * wave_two)
    )
    phase = phase - jnp.floor(phase)
    angle = 2.0 * math.pi * phase
    return (jnp.cos(angle), jnp.sin(angle))


def node_phase(layout, speed_value, center, half_width, degree):
    target_one, target_two, merge_dim, centers, child_half, other_center, other_half = layout
    points = jnp.asarray(cheb_nodes(degree), jnp.float32)
    merged = center[None, :] + half_width * points[:, None]
    across = other_center[None, :] + other_half * points[:, None]
    if merge_dim == 0:
        return rotation(target_one, target_two, speed_value, merged[:, None, :], across[None, :, :])
    return rotation(target_one, target_two, speed_value, across[:, None, :], merged[None, :, :])


def merge_children(child_low, child_high, layout, speed_modes):
    target_one, target_two, merge_dim, centers, child_half, other_center, other_half = layout
    degree = child_low.shape[1]
    speed_value = speed_of(speed_modes, target_one, target_two)
    lagrange = jnp.asarray(lagrange_table(degree), jnp.float32)
    pieces = []
    for child, center in ((child_low, centers[0]), (child_high, centers[1])):
        cosine, sine_part = node_phase(layout, speed_value, center, child_half, degree)
        real_part = child[0] * cosine + child[1] * sine_part
        imag_part = child[1] * cosine - child[0] * sine_part
        pieces.append(jnp.stack([real_part, imag_part]))
    stacked = jnp.concatenate(pieces, axis=1 + merge_dim)
    if merge_dim == 0:
        blended = jnp.einsum("ij,rjks->riks", lagrange, stacked, precision=lax.Precision.HIGHEST)
    else:
        blended = jnp.einsum("kj,rijs->riks", lagrange, stacked, precision=lax.Precision.HIGHEST)
    cosine, sine_part = node_phase(layout, speed_value, centers[2], 2.0 * child_half, degree)
    return jnp.stack(
        [blended[0] * cosine - blended[1] * sine_part, blended[0] * sine_part + blended[1] * cosine]
    )


def reversed_bits(box_code, bit_count):
    result = jnp.zeros_like(box_code)
    for bit_place in range(bit_count):
        result = result + box_code // 2**bit_place % 2 * 2 ** (bit_count - 1 - bit_place)
    return result


def x_layout(level_index, box_code, targets, y_box, geometry):
    extent, side_count, src_x, src_y = geometry
    span_size = 2 ** (level_index + 1)
    row_index = targets // side_count * span_size + reversed_bits(box_code, level_index + 1)
    target_one = (row_index.astype(jnp.float32) + 0.5) / (side_count * span_size)
    target_two = ((targets % side_count).astype(jnp.float32) + 0.5) / side_count
    parent = (box_code // span_size).astype(jnp.float32)
    child_width = extent * 2**level_index / src_x
    low_center = -extent / 2 + (2.0 * parent + 0.5) * child_width
    high_center = low_center + child_width
    parent_center = -extent / 2 + (parent + 0.5) * (2.0 * child_width)
    other_center = jnp.zeros_like(target_one) + (
        -extent / 2 + (jnp.asarray(y_box).astype(jnp.float32) + 0.5) * (extent / src_y)
    )
    return (
        target_one,
        target_two,
        0,
        (low_center, high_center, parent_center),
        child_width / 2,
        other_center,
        extent / (2 * src_y),
    )


def y_layout(level_index, box_code, targets, x_code, x_bits, geometry):
    extent, side_count, src_x, src_y = geometry
    span_size = 2 ** (level_index + 1)
    col_index = targets % side_count * span_size + reversed_bits(box_code, level_index + 1)
    target_two = (col_index.astype(jnp.float32) + 0.5) / (side_count * span_size)
    row_index = targets // side_count * src_x + reversed_bits(x_code, x_bits)
    target_one = (row_index.astype(jnp.float32) + 0.5) / (side_count * src_x)
    parent = (box_code // span_size).astype(jnp.float32)
    child_width = extent * 2**level_index / src_y
    low_center = -extent / 2 + (2.0 * parent + 0.5) * child_width
    high_center = low_center + child_width
    parent_center = -extent / 2 + (parent + 0.5) * (2.0 * child_width)
    other_center = jnp.zeros_like(target_one)
    return (
        target_one,
        target_two,
        1,
        (low_center, high_center, parent_center),
        child_width / 2,
        other_center,
        extent / 2,
    )


def pair_level(current, partner, level_index, box_code, targets, layout_fn, speed_modes):
    own_bit = box_code // 2**level_index % 2
    child_low = jnp.where(own_bit == 0, current, partner)
    child_high = jnp.where(own_bit == 0, partner, current)
    box_codes = jnp.zeros_like(targets) + box_code
    return merge_children(
        child_low, child_high, layout_fn(level_index, box_codes, targets), speed_modes
    )


def on_device(weights, speed_modes):
    current = weights.reshape(weights.shape[2:])
    pair_count = current.shape[3]
    core_count = lax.axis_size("cores")
    src_x = lax.axis_size("bx") * core_count
    src_y = lax.axis_size("by")
    x_bits = src_x.bit_length() - 1
    y_bits = src_y.bit_length() - 1
    x_code = lax.axis_index("bx") * core_count + lax.axis_index("cores")
    y_box = lax.axis_index("by")
    geometry = (float(N), TGT, src_x, src_y)
    targets = jnp.arange(pair_count, dtype=jnp.int32)
    first_layout = partial(x_layout, y_box=y_box, geometry=geometry)
    second_layout = partial(y_layout, x_code=x_code, x_bits=x_bits, geometry=geometry)
    for level_index in range(x_bits):
        if level_index == 0:
            partner = partner_2(current, "cores", 0)
        else:
            partner = partner_2(current, "bx", level_index - 1)
        current = pair_level(
            current, partner, level_index, x_code, targets, first_layout, speed_modes
        )
    for level_index in range(y_bits):
        partner = partner_2(current, "by", level_index)
        current = pair_level(
            current, partner, level_index, y_box, targets, second_layout, speed_modes
        )
    return current.reshape(weights.shape)


SIN_HALF = (4.442879586386342, -7.3078180422392816, 3.597788667381583, -0.7912380409231197)
COS_HALF = (
    1.4142134965636117,
    -6.978850988059019,
    5.739461167077472,
    -1.883562964211867,
    0.3106981455985473,
)
CHUNKS = 2
PIECES = 16
LEVEL_ROWS = (0, 256, 384, 448, 480)
VMEM_LIMIT = 48 * 2**20


def node_tables():
    points = cheb_nodes(16).astype(np.float32)
    nodes = []
    for level_index in range(5):
        width = np.float32(N * 2**level_index / 16)
        for box in range(16 >> level_index):
            center = np.float32(-N / 2 + (box + 0.5) * width)
            nodes.append(center + (width / 2) * points)
    nodes = np.concatenate(nodes).astype(np.float32)
    sub = np.arange(8)
    lane = np.arange(128)
    half = (sub // 4)[:, None] + 0 * lane[None, :]
    second = (lane // 32 * 4)[None, :] + (sub % 4)[:, None]
    wave_two = (-N / 2 + (half + 0.5) * (N / 2)).astype(np.float32) + np.float32(N / 4) * points[second]
    wave_two = wave_two.astype(np.float32)
    lengths = np.sqrt(nodes[:, None, None] * nodes[:, None, None] + wave_two * wave_two)
    return nodes, wave_two, lengths.astype(np.float32)


def final_tables():
    points = cheb_nodes(16).astype(np.float32) * np.float32(N / 2)
    lane = np.arange(128)
    one = np.broadcast_to(points.reshape(2, 8, 1), (2, 8, 128)).astype(np.float32)
    two = np.stack([np.broadcast_to(points[lane // 32 * 4 + a], (8, 128)) for a in range(4)])
    two = two.astype(np.float32)
    lengths = np.sqrt((one * one)[:, None] + (two * two)[None, :]).astype(np.float32)
    return np.array(one), two, lengths


def second_weights():
    table = lagrange_table(16)
    result = np.zeros((8, 4, 32, 4, 4, 32), np.float32)
    same = np.eye(32, dtype=np.float32)
    for half in range(2):
        for a in range(4):
            for b in range(4):
                for out_a in range(4):
                    for out_b in range(4):
                        weight = table[4 * out_b + out_a, half * 16 + 4 * b + a]
                        result[half * 4 + a, b, :, out_a, out_b, :] = np.float32(weight) * same
    return result.reshape(8, 128, 512)


def folded_table():
    table = lagrange_table(16)[:, :16]
    even = (table[:8] + table[::-1][:8]) / 2
    odd = (table[:8] - table[::-1][:8]) / 2
    return even, odd


def turn(phase):
    part = phase - jnp.round(phase)
    square = part * part
    sine = SIN_HALF[3]
    for coefficient in SIN_HALF[2::-1]:
        sine = sine * square + coefficient
    sine = sine * part
    cosine = COS_HALF[4]
    for coefficient in COS_HALF[3::-1]:
        cosine = cosine * square + coefficient
    return 1.0 - sine * sine, sine * cosine


def swap_lanes(values):
    lane = lax.broadcasted_iota(jnp.int32, (8, 128), 1)
    low = lane < 64
    even = lane // 32 % 2 == 0
    half = [None] * 4
    for b in range(2):
        half[b] = jnp.where(low, values[b], pltpu.roll(values[b + 2], 64, 1))
        half[b + 2] = jnp.where(low, pltpu.roll(values[b], 64, 1), values[b + 2])
    full = [None] * 4
    for j in (0, 2):
        full[j] = jnp.where(even, half[j], pltpu.roll(half[j + 1], 32, 1))
        full[j + 1] = jnp.where(even, pltpu.roll(half[j], 96, 1), half[j + 1])
    return full


def pack_kernel(in_ref, out_ref):
    upper = lax.broadcasted_iota(jnp.int32, (8, 128), 0) < 4
    for t1 in range(16):
        groups = [None] * 4
        for high in range(2):
            real = in_ref[0, t1, 8 * high : 8 * high + 8, :]
            imag = in_ref[1, t1, 8 * high : 8 * high + 8, :]
            groups[2 * high] = jnp.where(upper, real, pltpu.roll(imag, 4, 0))
            groups[2 * high + 1] = jnp.where(upper, pltpu.roll(real, 4, 0), imag)
        for j, tile in enumerate(swap_lanes(groups)):
            out_ref[j, t1] = tile


def pack(weights, chunk):
    return pl.pallas_call(
        pack_kernel,
        grid=(4,),
        in_specs=[pl.BlockSpec((2, 16, 16, 128), lambda i: (0, 0, 0, 4 * chunk + i))],
        out_specs=pl.BlockSpec((4, 16, 8, 128), lambda i: (i, 0, 0, 0)),
        out_shape=jax.ShapeDtypeStruct((PIECES, 16, 8, 128), jnp.float32),
        cost_estimate=pl.CostEstimate(flops=10**6, bytes_accessed=2**21, transcendentals=0),
        name="pack",
    )(weights)


def join_kernel(in_ref, out_ref):
    upper = lax.broadcasted_iota(jnp.int32, (8, 128), 0) < 4

    def step(box, carry):
        for t1 in range(16):
            low = in_ref[2 * box, t1]
            high = in_ref[2 * box + 1, t1]
            out_ref[box, 0, t1] = jnp.where(upper, low, pltpu.roll(high, 4, 0))
            out_ref[box, 1, t1] = jnp.where(upper, pltpu.roll(low, 4, 0), high)
        return carry

    lax.fori_loop(0, 8, step, 0)


def join(received):
    return pl.pallas_call(
        join_kernel,
        in_specs=[pl.BlockSpec(memory_space=pltpu.VMEM)],
        out_specs=pl.BlockSpec(memory_space=pltpu.VMEM),
        out_shape=jax.ShapeDtypeStruct((8, 2, 16, 8, 128), jnp.float32),
        compiler_params=pltpu.CompilerParams(vmem_limit_bytes=VMEM_LIMIT),
        cost_estimate=pl.CostEstimate(flops=10**6, bytes_accessed=2**21, transcendentals=0),
        name="join",
    )(received)


def levels_kernel(
    chunk, ids, nodes, own, other, speeds, waves, lengths, last_one, last_two, last_lengths,
    weights, out, boxes_a, boxes_b, sums, turned, mixed,
):
    even, odd = folded_table()
    row = (chunk * PIECES + ids[0]).astype(jnp.float32)
    core = ids[1]
    core_float = core.astype(jnp.float32)
    wave_two = waves[...]
    lane = lax.broadcasted_iota(jnp.int32, (8, 128), 1)
    along_two = ((lane % 32).astype(jnp.float32) + 0.5) * (1.0 / 32)
    second_phase = along_two * wave_two

    def first_point(level_index, low_code):
        span = 2.0 ** (level_index + 1)
        code = core_float * 2.0**level_index + low_code
        return (row * span + code + 0.5) * (1.0 / (32 * span))

    def speed_row(level_index, low_code):
        return jnp.broadcast_to(speeds[pl.ds(2**level_index - 1 + low_code, 1), :], (8, 128))

    def blend(copies, target, boxes):
        for i_half in range(2):
            totals = {}
            for parity, table in ((0, even), (1, odd)):
                for j in range(16):
                    piece = sums[parity, j, :copies]
                    for i in range(4 * i_half, 4 * i_half + 4):
                        term = piece * float(table[i, j])
                        key = (parity, i)
                        totals[key] = term if j == 0 else totals[key] + term
            for i in range(4 * i_half, 4 * i_half + 4):
                plus = totals[0, i] + totals[1, i]
                minus = totals[0, i] - totals[1, i]
                for n, box in enumerate(boxes):
                    for part in range(2):
                        target[box, part, i] = plus[2 * n + part]
                        target[box, part, 15 - i] = minus[2 * n + part]

    sign = 1.0 - 2.0 * core_float

    def first_level(box, carry):
        point = first_point(0, 0.0)
        speed = speed_row(0, 0)
        for j in range(16):
            own_node = jnp.where(core == 0, j, 15 - j)
            pieces = []
            for source, node, box_code in (
                (own, own_node, 2 * box + core),
                (other, 15 - own_node, 2 * box + 1 - core),
            ):
                entry = box_code * 16 + node
                phase = (point * nodes[entry] + second_phase) + speed * lengths[entry]
                cosine, sine = turn(phase)
                real = source[box, 0, node]
                imag = source[box, 1, node]
                pieces.append((real * cosine + imag * sine, imag * cosine - real * sine))
            for part in range(2):
                sums[0, j, part] = pieces[0][part] + pieces[1][part]
                sums[1, j, part] = (pieces[0][part] - pieces[1][part]) * sign
        blend(2, boxes_a, [box])
        return carry

    lax.fori_loop(0, 8, first_level, 0)

    def later_level(level_index, source, target):
        low_bits = level_index - 1
        stride = 2**low_bits

        def group(index, carry):
            parent = index // stride
            low = index % stride
            code = 0
            for bit in range(low_bits):
                code = code + low // 2**bit % 2 * 2 ** (low_bits - 1 - bit)
            code = jnp.int32(0) + code
            before = first_point(level_index - 1, code.astype(jnp.float32))
            before_speed = speed_row(level_index - 1, code)
            points = [first_point(level_index, (2 * code + b).astype(jnp.float32)) for b in range(2)]
            point_speeds = [speed_row(level_index, 2 * code + b) for b in range(2)]
            first_box = parent * (2 * stride) + low
            for j in range(16):
                pieces = []
                for child in range(2):
                    node = j if child == 0 else 15 - j
                    entry = LEVEL_ROWS[level_index] + (2 * parent + child) * 16 + node
                    length = lengths[entry]
                    wave = nodes[entry]
                    real = source[first_box + child * stride, 0, node]
                    imag = source[first_box + child * stride, 1, node]
                    old = (before * wave + second_phase) + before_speed * length
                    for b in range(2):
                        new = (points[b] * wave + second_phase) + point_speeds[b] * length
                        cosine, sine = turn(new - old)
                        pieces.append((real * cosine + imag * sine, imag * cosine - real * sine))
                for b in range(2):
                    for part in range(2):
                        sums[0, j, 2 * b + part] = pieces[b][part] + pieces[2 + b][part]
                        sums[1, j, 2 * b + part] = pieces[b][part] - pieces[2 + b][part]
            blend(4, target, [first_box, first_box + stride])
            return carry

        lax.fori_loop(0, 4, group, 0)

    later_level(1, boxes_a, boxes_b)
    later_level(2, boxes_b, boxes_a)
    later_level(3, boxes_a, boxes_b)

    fine_two = [((lane % 32).astype(jnp.float32) * 2.0 + (e + 0.5)) * (1.0 / 64) for e in range(2)]
    fine_phase = [fine_two[e] * wave_two for e in range(2)]

    def reversed_code(box):
        return box % 2 * 4 + box // 2 % 2 * 2 + box // 4

    def fine_speed(code, e):
        return jnp.broadcast_to(speeds[pl.ds(15 + 2 * code + e, 1), :], (8, 128))

    def rotate_box(box, carry):
        code = reversed_code(box)
        point = first_point(3, code.astype(jnp.float32))
        old_speed = speed_row(3, code)
        new_speeds = [fine_speed(code, e) for e in range(2)]
        for t1 in range(16):
            entry = LEVEL_ROWS[4] + t1
            length = lengths[entry]
            across = point * nodes[entry]
            real = boxes_b[box, 0, t1]
            imag = boxes_b[box, 1, t1]
            old = (across + second_phase) + old_speed * length
            for e in range(2):
                new = (across + fine_phase[e]) + new_speeds[e] * length
                cosine, sine = turn(new - old)
                first = pl.multiple_of((box * 32 + t1) * 8, 8)
                turned[e, pl.ds(first, 8), :] = real * cosine + imag * sine
                turned[e, pl.ds(first + 128, 8), :] = imag * cosine - real * sine
        return carry

    lax.fori_loop(0, 8, rotate_box, 0)

    for e in range(2):
        total = None
        for j in range(8):
            rows = turned[e, pl.ds(j, 256, stride=8), :]
            term = jnp.dot(
                rows, weights[j], preferred_element_type=jnp.float32, precision=lax.Precision.HIGHEST
            )
            total = term if total is None else total + term
        mixed[e] = total

    last_phase = [[fine_two[e] * last_two[a] for a in range(4)] for e in range(2)]

    def finish_box(box, carry):
        code = reversed_code(box)
        point = first_point(3, code.astype(jnp.float32))
        for e in range(2):
            speed = fine_speed(code, e)
            for high in range(2):
                across = point * last_one[high]
                first = pl.multiple_of(box * 32 + high * 8, 8)
                for a in range(4):
                    phase = (across + last_phase[e][a]) + speed * last_lengths[high, a]
                    cosine, sine = turn(phase)
                    real = mixed[e, pl.ds(first, 8), 128 * a : 128 * a + 128]
                    imag = mixed[e, pl.ds(first + 16, 8), 128 * a : 128 * a + 128]
                    out[2 * box + e, high * 4 + a] = real * cosine - imag * sine
                    out[2 * box + e, 8 + high * 4 + a] = real * sine + imag * cosine
        return carry

    lax.fori_loop(0, 8, finish_box, 0)


def levels(chunk, ids, own, other, speeds):
    nodes, waves, lengths = node_tables()
    last_one, last_two, last_lengths = final_tables()
    in_vmem = pl.BlockSpec(memory_space=pltpu.VMEM)
    in_smem = pl.BlockSpec(memory_space=pltpu.SMEM)
    return pl.pallas_call(
        partial(levels_kernel, chunk),
        in_specs=[in_smem, in_smem] + [in_vmem] * 9,
        out_specs=in_vmem,
        out_shape=jax.ShapeDtypeStruct((PIECES, 16, 8, 128), jnp.float32),
        scratch_shapes=[
            pltpu.VMEM((8, 2, 16, 8, 128), jnp.float32),
            pltpu.VMEM((8, 2, 16, 8, 128), jnp.float32),
            pltpu.VMEM((2, 16, 4, 8, 128), jnp.float32),
            pltpu.VMEM((2, 2048, 128), jnp.float32),
            pltpu.VMEM((2, 256, 512), jnp.float32),
        ],
        compiler_params=pltpu.CompilerParams(vmem_limit_bytes=VMEM_LIMIT),
        cost_estimate=pl.CostEstimate(flops=10**8, bytes_accessed=2**23, transcendentals=0),
        name="levels",
    )(
        ids, jnp.asarray(nodes), own, other, speeds, jnp.asarray(waves), jnp.asarray(lengths),
        jnp.asarray(last_one), jnp.asarray(last_two), jnp.asarray(last_lengths),
        jnp.asarray(second_weights()),
    )


def unpack_kernel(*refs):
    in_ref, out_ref, rows = refs[0], refs[-2], refs[-1]
    for part in range(2):
        for high in range(2):
            for a in range(4):
                tiles = [in_ref[j, part * 8 + high * 4 + a] for j in range(4)]
                for b, tile in enumerate(swap_lanes(tiles)):
                    t2 = 4 * b + a
                    rows[part * 2 + high, 8 * t2 : 8 * t2 + 8, :] = tile
            for t1 in range(8):
                out_ref[part, high * 8 + t1] = rows[part * 2 + high, pl.ds(t1, 16, stride=8), :]


def unpack(received, chunk, earlier):
    operands = [received]
    in_specs = [pl.BlockSpec((4, 16, 8, 128), lambda i: (i, 0, 0, 0))]
    aliases = {}
    if earlier is not None:
        operands.append(earlier)
        in_specs.append(pl.BlockSpec(memory_space=pl.ANY))
        aliases = {1: 0}
    return pl.pallas_call(
        unpack_kernel,
        grid=(4,),
        in_specs=in_specs,
        out_specs=pl.BlockSpec((2, 16, 16, 128), lambda i: (0, 0, 0, 4 * chunk + i)),
        out_shape=jax.ShapeDtypeStruct((2, 16, 16, 1024), jnp.float32),
        scratch_shapes=[pltpu.VMEM((4, 128, 128), jnp.float32)],
        input_output_aliases=aliases,
        cost_estimate=pl.CostEstimate(flops=10**6, bytes_accessed=2**21, transcendentals=0),
        name="unpack",
    )(*operands)


def speed_tables(speed_modes, core):
    numerators, spans = [], []
    for level_index in range(4):
        for code in range(2**level_index):
            numerators.append(core * 2**level_index + code)
            spans.append(2 ** (level_index + 1))
    for code in range(8):
        for e in range(2):
            numerators.append(core * 8 + code)
            spans.append(16)
    codes = jnp.stack(numerators).astype(jnp.float32)
    spans = jnp.asarray(np.array(spans), jnp.float32)
    me = lax.axis_index("bx") * 2 + lax.axis_index("by")
    rows = (jnp.arange(CHUNKS) * PIECES + me).astype(jnp.float32)
    target_one = (rows[:, None] * spans + codes + 0.5) / (TGT * spans)
    columns = jnp.arange(32).astype(jnp.float32)
    coarse = jnp.broadcast_to((columns + 0.5) / TGT, (15, 32))
    fine = jnp.stack([(2 * columns + e + 0.5) / (2 * TGT) for e in range(2)])
    target_two = jnp.concatenate([coarse, jnp.tile(fine, (8, 1))])
    target_one = jnp.broadcast_to(target_one[:, :, None], (CHUNKS, 31, 32))
    target_two = jnp.broadcast_to(target_two[None], (CHUNKS, 31, 32))
    speed = speed_of(speed_modes, target_one.reshape(-1), target_two.reshape(-1))
    return jnp.tile(speed.reshape(CHUNKS, 31, 32), (1, 1, 4))


def on_device_dealt(weights, speed_modes):
    local = weights.reshape(weights.shape[2:])
    core = lax.axis_index("cores")
    me = lax.axis_index("bx") * 2 + lax.axis_index("by")
    ids = jnp.stack([me, core]).astype(jnp.int32)
    speeds = speed_tables(speed_modes, core)
    received = []
    for chunk in range(CHUNKS):
        received.append(deal(pack(local, chunk)))
    results = []
    for chunk in range(CHUNKS):
        own = join(received[chunk])
        other = partner_2(own, "cores", 0)
        results.append(deal(levels(chunk, ids, own, other, speeds[chunk])))
    out = None
    for chunk in range(CHUNKS):
        out = unpack(results[chunk], chunk, out)
    return out.reshape(weights.shape)


def deal(pieces):
    return lax.all_to_all(pieces, ("bx", "by"), 0, 0, tiled=True)


def solution(mesh):
    sizes = dict(mesh.shape)
    spec = P(("bx", "cores"), "by", None, None, None, None)
    dealt = (sizes["bx"], sizes["by"], sizes["cores"]) == (8, 2, 2)

    def whole(weights, speed_modes):
        fits = dealt and weights.shape[2:] == (2, 16, 16, 1024)
        return jax.shard_map(
            on_device_dealt if fits else on_device,
            mesh=mesh,
            in_specs=(spec, P()),
            out_specs=spec,
            check_vma=False,
        )(weights, speed_modes)

    return whole
```

```python
from functools import partial
import math

import jax
import jax.numpy as jnp
import numpy as np
from jax import lax
from jax.experimental import pallas as pl
from jax.experimental.pallas import tpu as pltpu
from jax.sharding import PartitionSpec as P

N = 8192
TGT = 32


def partner_2(value, axis, apart):
    mask = 2**apart
    pairs = [(source, source ^ mask) for source in range(lax.axis_size(axis))]
    return lax.ppermute(value, axis, pairs)


def cheb_nodes(degree):
    return np.cos(np.pi * (2 * np.arange(degree) + 1) / (2 * degree))


def lagrange_table(degree):
    points = cheb_nodes(degree)
    result = np.ones((degree, 2 * degree))
    for child_side in range(2):
        inside = (points + 2 * child_side - 1) / 2
        for node_row in range(degree):
            for node_other in range(degree):
                if node_other != node_row:
                    result[node_row, child_side * degree : (child_side + 1) * degree] *= (
                        inside - points[node_other]
                    ) / (points[node_row] - points[node_other])
    return result


def speed_of(speed_modes, target_one, target_two):
    mode_count = speed_modes.shape[0]
    frequencies = jnp.arange(mode_count).astype(jnp.float32) * math.pi
    along_one = jnp.cos(frequencies[:, None] * target_one[None, :])
    along_two = jnp.cos(frequencies[:, None] * target_two[None, :])
    blended = jnp.dot(
        speed_modes, along_two, preferred_element_type=jnp.float32, precision=lax.Precision.HIGHEST
    )
    return 1.0 + jnp.sum(blended * along_one, axis=0)


def rotation(target_one, target_two, speed_value, wave_one, wave_two):
    phase = (
        target_one * wave_one
        + target_two * wave_two
        + speed_value * jnp.sqrt(wave_one * wave_one + wave_two * wave_two)
    )
    phase = phase - jnp.floor(phase)
    angle = 2.0 * math.pi * phase
    return (jnp.cos(angle), jnp.sin(angle))


def node_phase(layout, speed_value, center, half_width, degree):
    target_one, target_two, merge_dim, centers, child_half, other_center, other_half = layout
    points = jnp.asarray(cheb_nodes(degree), jnp.float32)
    merged = center[None, :] + half_width * points[:, None]
    across = other_center[None, :] + other_half * points[:, None]
    if merge_dim == 0:
        return rotation(target_one, target_two, speed_value, merged[:, None, :], across[None, :, :])
    return rotation(target_one, target_two, speed_value, across[:, None, :], merged[None, :, :])


def merge_children(child_low, child_high, layout, speed_modes):
    target_one, target_two, merge_dim, centers, child_half, other_center, other_half = layout
    degree = child_low.shape[1]
    speed_value = speed_of(speed_modes, target_one, target_two)
    lagrange = jnp.asarray(lagrange_table(degree), jnp.float32)
    pieces = []
    for child, center in ((child_low, centers[0]), (child_high, centers[1])):
        cosine, sine_part = node_phase(layout, speed_value, center, child_half, degree)
        real_part = child[0] * cosine + child[1] * sine_part
        imag_part = child[1] * cosine - child[0] * sine_part
        pieces.append(jnp.stack([real_part, imag_part]))
    stacked = jnp.concatenate(pieces, axis=1 + merge_dim)
    if merge_dim == 0:
        blended = jnp.einsum("ij,rjks->riks", lagrange, stacked, precision=lax.Precision.HIGHEST)
    else:
        blended = jnp.einsum("kj,rijs->riks", lagrange, stacked, precision=lax.Precision.HIGHEST)
    cosine, sine_part = node_phase(layout, speed_value, centers[2], 2.0 * child_half, degree)
    return jnp.stack(
        [blended[0] * cosine - blended[1] * sine_part, blended[0] * sine_part + blended[1] * cosine]
    )


def reversed_bits(box_code, bit_count):
    result = jnp.zeros_like(box_code)
    for bit_place in range(bit_count):
        result = result + box_code // 2**bit_place % 2 * 2 ** (bit_count - 1 - bit_place)
    return result


def x_layout(level_index, box_code, targets, y_box, geometry):
    extent, side_count, src_x, src_y = geometry
    span_size = 2 ** (level_index + 1)
    row_index = targets // side_count * span_size + reversed_bits(box_code, level_index + 1)
    target_one = (row_index.astype(jnp.float32) + 0.5) / (side_count * span_size)
    target_two = ((targets % side_count).astype(jnp.float32) + 0.5) / side_count
    parent = (box_code // span_size).astype(jnp.float32)
    child_width = extent * 2**level_index / src_x
    low_center = -extent / 2 + (2.0 * parent + 0.5) * child_width
    high_center = low_center + child_width
    parent_center = -extent / 2 + (parent + 0.5) * (2.0 * child_width)
    other_center = jnp.zeros_like(target_one) + (
        -extent / 2 + (jnp.asarray(y_box).astype(jnp.float32) + 0.5) * (extent / src_y)
    )
    return (
        target_one,
        target_two,
        0,
        (low_center, high_center, parent_center),
        child_width / 2,
        other_center,
        extent / (2 * src_y),
    )


def y_layout(level_index, box_code, targets, x_code, x_bits, geometry):
    extent, side_count, src_x, src_y = geometry
    span_size = 2 ** (level_index + 1)
    col_index = targets % side_count * span_size + reversed_bits(box_code, level_index + 1)
    target_two = (col_index.astype(jnp.float32) + 0.5) / (side_count * span_size)
    row_index = targets // side_count * src_x + reversed_bits(x_code, x_bits)
    target_one = (row_index.astype(jnp.float32) + 0.5) / (side_count * src_x)
    parent = (box_code // span_size).astype(jnp.float32)
    child_width = extent * 2**level_index / src_y
    low_center = -extent / 2 + (2.0 * parent + 0.5) * child_width
    high_center = low_center + child_width
    parent_center = -extent / 2 + (parent + 0.5) * (2.0 * child_width)
    other_center = jnp.zeros_like(target_one)
    return (
        target_one,
        target_two,
        1,
        (low_center, high_center, parent_center),
        child_width / 2,
        other_center,
        extent / 2,
    )


def pair_level(current, partner, level_index, box_code, targets, layout_fn, speed_modes):
    own_bit = box_code // 2**level_index % 2
    child_low = jnp.where(own_bit == 0, current, partner)
    child_high = jnp.where(own_bit == 0, partner, current)
    box_codes = jnp.zeros_like(targets) + box_code
    return merge_children(
        child_low, child_high, layout_fn(level_index, box_codes, targets), speed_modes
    )


def on_device(weights, speed_modes):
    current = weights.reshape(weights.shape[2:])
    pair_count = current.shape[3]
    core_count = lax.axis_size("cores")
    src_x = lax.axis_size("bx") * core_count
    src_y = lax.axis_size("by")
    x_bits = src_x.bit_length() - 1
    y_bits = src_y.bit_length() - 1
    x_code = lax.axis_index("bx") * core_count + lax.axis_index("cores")
    y_box = lax.axis_index("by")
    geometry = (float(N), TGT, src_x, src_y)
    targets = jnp.arange(pair_count, dtype=jnp.int32)
    first_layout = partial(x_layout, y_box=y_box, geometry=geometry)
    second_layout = partial(y_layout, x_code=x_code, x_bits=x_bits, geometry=geometry)
    for level_index in range(x_bits):
        if level_index == 0:
            partner = partner_2(current, "cores", 0)
        else:
            partner = partner_2(current, "bx", level_index - 1)
        current = pair_level(
            current, partner, level_index, x_code, targets, first_layout, speed_modes
        )
    for level_index in range(y_bits):
        partner = partner_2(current, "by", level_index)
        current = pair_level(
            current, partner, level_index, y_box, targets, second_layout, speed_modes
        )
    return current.reshape(weights.shape)


SIN_HALF = (4.442879586386342, -7.3078180422392816, 3.597788667381583, -0.7912380409231197)
COS_HALF = (
    1.4142134965636117,
    -6.978850988059019,
    5.739461167077472,
    -1.883562964211867,
    0.3106981455985473,
)
CHUNKS = 2
PIECES = 16
LEVEL_ROWS = (0, 256, 384, 448, 480)
VMEM_LIMIT = 48 * 2**20


def node_tables():
    points = cheb_nodes(16).astype(np.float32)
    nodes = []
    for level_index in range(5):
        width = np.float32(N * 2**level_index / 16)
        for box in range(16 >> level_index):
            center = np.float32(-N / 2 + (box + 0.5) * width)
            nodes.append(center + (width / 2) * points)
    nodes = np.concatenate(nodes).astype(np.float32)
    sub = np.arange(8)
    lane = np.arange(128)
    half = (sub // 4)[:, None] + 0 * lane[None, :]
    second = (lane // 32 * 4)[None, :] + (sub % 4)[:, None]
    wave_two = (-N / 2 + (half + 0.5) * (N / 2)).astype(np.float32) + np.float32(N / 4) * points[second]
    wave_two = wave_two.astype(np.float32)
    lengths = np.sqrt(nodes[:, None, None] * nodes[:, None, None] + wave_two * wave_two)
    return nodes, wave_two, lengths.astype(np.float32)


def final_tables():
    points = cheb_nodes(16).astype(np.float32) * np.float32(N / 2)
    lane = np.arange(128)
    one = np.broadcast_to(points.reshape(2, 8, 1), (2, 8, 128)).astype(np.float32)
    two = np.stack([np.broadcast_to(points[lane // 32 * 4 + a], (8, 128)) for a in range(4)])
    two = two.astype(np.float32)
    lengths = np.sqrt((one * one)[:, None] + (two * two)[None, :]).astype(np.float32)
    return np.array(one), two, lengths


def second_weights():
    table = lagrange_table(16)
    result = np.zeros((8, 4, 32, 4, 4, 32), np.float32)
    same = np.eye(32, dtype=np.float32)
    for half in range(2):
        for a in range(4):
            for b in range(4):
                for out_a in range(4):
                    for out_b in range(4):
                        weight = table[4 * out_b + out_a, half * 16 + 4 * b + a]
                        result[half * 4 + a, b, :, out_a, out_b, :] = np.float32(weight) * same
    return result.reshape(8, 128, 512)


def folded_table():
    table = lagrange_table(16)[:, :16]
    even = (table[:8] + table[::-1][:8]) / 2
    odd = (table[:8] - table[::-1][:8]) / 2
    return even, odd


def turn(phase):
    part = phase - jnp.round(phase)
    square = part * part
    sine = SIN_HALF[3]
    for coefficient in SIN_HALF[2::-1]:
        sine = sine * square + coefficient
    sine = sine * part
    cosine = COS_HALF[4]
    for coefficient in COS_HALF[3::-1]:
        cosine = cosine * square + coefficient
    return 1.0 - sine * sine, sine * cosine


def swap_lanes(values):
    lane = lax.broadcasted_iota(jnp.int32, (8, 128), 1)
    low = lane < 64
    even = lane // 32 % 2 == 0
    half = [None] * 4
    for b in range(2):
        half[b] = jnp.where(low, values[b], pltpu.roll(values[b + 2], 64, 1))
        half[b + 2] = jnp.where(low, pltpu.roll(values[b], 64, 1), values[b + 2])
    full = [None] * 4
    for j in (0, 2):
        full[j] = jnp.where(even, half[j], pltpu.roll(half[j + 1], 32, 1))
        full[j + 1] = jnp.where(even, pltpu.roll(half[j], 96, 1), half[j + 1])
    return full


def pack_kernel(chunk, ids, in_ref, *refs):
    outs, tiles = refs[:PIECES], refs[-1]
    me = ids[0]
    upper = lax.broadcasted_iota(jnp.int32, (8, 128), 0) < 4
    for turn_of in range(4):
        group = turn_of ^ (me // 4)
        lanes = pl.ds(pl.multiple_of(group * 128, 128), 128)

        def step(t1, carry):
            groups = [None] * 4
            for high in range(2):
                real = in_ref[0, t1, 8 * high : 8 * high + 8, lanes]
                imag = in_ref[1, t1, 8 * high : 8 * high + 8, lanes]
                groups[2 * high] = jnp.where(upper, real, pltpu.roll(imag, 4, 0))
                groups[2 * high + 1] = jnp.where(upper, pltpu.roll(real, 4, 0), imag)
            for j, tile in enumerate(swap_lanes(groups)):
                tiles[j, t1] = tile
            return carry

        lax.fori_loop(0, 16, step, 0, unroll=True)
        for j in range(4):
            outs[4 * turn_of + j][...] = tiles[j ^ (me % 4)]


def pack(weights, ids, chunk):
    piece = jax.ShapeDtypeStruct((16, 8, 128), jnp.float32)
    return pl.pallas_call(
        partial(pack_kernel, chunk),
        grid=(1,),
        in_specs=[
            pl.BlockSpec(memory_space=pltpu.SMEM),
            pl.BlockSpec((2, 16, 16, 512), lambda i: (0, 0, 0, chunk)),
        ],
        out_specs=[pl.BlockSpec((16, 8, 128), lambda i: (0, 0, 0))] * PIECES,
        out_shape=[piece] * PIECES,
        scratch_shapes=[pltpu.VMEM((4, 16, 8, 128), jnp.float32)],
        compiler_params=pltpu.CompilerParams(vmem_limit_bytes=VMEM_LIMIT),
        cost_estimate=pl.CostEstimate(flops=10**6, bytes_accessed=2**21, transcendentals=0),
        name="pack",
    )(ids, weights)


def join_kernel(ids, *refs):
    pieces, out_ref = refs[:PIECES], refs[-1]
    me = ids[0]
    upper = lax.broadcasted_iota(jnp.int32, (8, 128), 0) < 4
    by = me % 2
    is_low = jnp.broadcast_to(by, (8, 128)) == 0
    for pair in range(8):
        box = pair ^ (me // 2)
        for t1 in range(16):
            mine = pieces[2 * pair][t1]
            partner = pieces[2 * pair + 1][t1]
            low = jnp.where(is_low, mine, partner)
            high = jnp.where(is_low, partner, mine)
            out_ref[box, 0, t1] = jnp.where(upper, low, pltpu.roll(high, 4, 0))
            out_ref[box, 1, t1] = jnp.where(upper, pltpu.roll(low, 4, 0), high)


def join(ids, received):
    return pl.pallas_call(
        join_kernel,
        in_specs=[pl.BlockSpec(memory_space=pltpu.SMEM)]
        + [pl.BlockSpec(memory_space=pltpu.VMEM)] * PIECES,
        out_specs=pl.BlockSpec(memory_space=pltpu.VMEM),
        out_shape=jax.ShapeDtypeStruct((8, 2, 16, 8, 128), jnp.float32),
        compiler_params=pltpu.CompilerParams(vmem_limit_bytes=VMEM_LIMIT),
        cost_estimate=pl.CostEstimate(flops=10**6, bytes_accessed=2**21, transcendentals=0),
        name="join",
    )(ids, *received)


def levels_kernel(
    chunk, ids, nodes, own, other, speeds, waves, lengths, last_one, last_two, last_lengths,
    weights, *refs,
):
    outs, (boxes_a, boxes_b, sums, turned, mixed, last_phase) = refs[:PIECES], refs[PIECES:]
    even, odd = folded_table()
    row = (chunk * PIECES + ids[0]).astype(jnp.float32)
    core = ids[1]
    core_float = core.astype(jnp.float32)
    wave_two = waves[...]
    lane = lax.broadcasted_iota(jnp.int32, (8, 128), 1)
    along_two = ((lane % 32).astype(jnp.float32) + 0.5) * (1.0 / 32)
    second_phase = along_two * wave_two

    def first_point(level_index, low_code):
        span = 2.0 ** (level_index + 1)
        code = core_float * 2.0**level_index + low_code
        return (row * span + code + 0.5) * (1.0 / (32 * span))

    def speed_row(level_index, low_code):
        return jnp.broadcast_to(speeds[pl.ds(2**level_index - 1 + low_code, 1), :], (8, 128))

    def blend(copies, target, boxes):
        for i_half in range(2):
            totals = {}
            for parity, table in ((0, even), (1, odd)):
                for j in range(16):
                    piece = sums[parity, j, :copies]
                    for i in range(4 * i_half, 4 * i_half + 4):
                        term = piece * float(table[i, j])
                        key = (parity, i)
                        totals[key] = term if j == 0 else totals[key] + term
            for i in range(4 * i_half, 4 * i_half + 4):
                plus = totals[0, i] + totals[1, i]
                minus = totals[0, i] - totals[1, i]
                for n, box in enumerate(boxes):
                    for part in range(2):
                        target[box, part, i] = plus[2 * n + part]
                        target[box, part, 15 - i] = minus[2 * n + part]

    sign = 1.0 - 2.0 * core_float

    def first_level(box, carry):
        point = first_point(0, 0.0)
        speed = speed_row(0, 0)
        for j in range(16):
            own_node = jnp.where(core == 0, j, 15 - j)
            pieces = []
            for source, node, box_code in (
                (own, own_node, 2 * box + core),
                (other, 15 - own_node, 2 * box + 1 - core),
            ):
                entry = box_code * 16 + node
                phase = (point * nodes[entry] + second_phase) + speed * lengths[entry]
                cosine, sine = turn(phase)
                real = source[box, 0, node]
                imag = source[box, 1, node]
                pieces.append((real * cosine + imag * sine, imag * cosine - real * sine))
            for part in range(2):
                sums[0, j, part] = pieces[0][part] + pieces[1][part]
                sums[1, j, part] = (pieces[0][part] - pieces[1][part]) * sign
        blend(2, boxes_a, [box])
        return carry

    lax.fori_loop(0, 8, first_level, 0)

    def later_level(level_index, source, target):
        low_bits = level_index - 1
        stride = 2**low_bits

        def group(index, carry):
            parent = index // stride
            low = index % stride
            code = 0
            for bit in range(low_bits):
                code = code + low // 2**bit % 2 * 2 ** (low_bits - 1 - bit)
            code = jnp.int32(0) + code
            before = first_point(level_index - 1, code.astype(jnp.float32))
            before_speed = speed_row(level_index - 1, code)
            points = [first_point(level_index, (2 * code + b).astype(jnp.float32)) for b in range(2)]
            point_speeds = [speed_row(level_index, 2 * code + b) for b in range(2)]
            first_box = parent * (2 * stride) + low
            for j in range(16):
                pieces = []
                for child in range(2):
                    node = j if child == 0 else 15 - j
                    entry = LEVEL_ROWS[level_index] + (2 * parent + child) * 16 + node
                    length = lengths[entry]
                    wave = nodes[entry]
                    real = source[first_box + child * stride, 0, node]
                    imag = source[first_box + child * stride, 1, node]
                    old = (before * wave + second_phase) + before_speed * length
                    for b in range(2):
                        new = (points[b] * wave + second_phase) + point_speeds[b] * length
                        cosine, sine = turn(new - old)
                        pieces.append((real * cosine + imag * sine, imag * cosine - real * sine))
                for b in range(2):
                    for part in range(2):
                        sums[0, j, 2 * b + part] = pieces[b][part] + pieces[2 + b][part]
                        sums[1, j, 2 * b + part] = pieces[b][part] - pieces[2 + b][part]
            blend(4, target, [first_box, first_box + stride])
            return carry

        lax.fori_loop(0, 4, group, 0)

    later_level(1, boxes_a, boxes_b)
    later_level(2, boxes_b, boxes_a)
    later_level(3, boxes_a, boxes_b)

    fine_two = [((lane % 32).astype(jnp.float32) * 2.0 + (e + 0.5)) * (1.0 / 64) for e in range(2)]
    fine_phase = [fine_two[e] * wave_two for e in range(2)]

    def reversed_code(box):
        return box % 2 * 4 + box // 2 % 2 * 2 + box // 4

    def fine_speed(code, e):
        return jnp.broadcast_to(speeds[pl.ds(15 + 2 * code + e, 1), :], (8, 128))

    def rotate_box(box, carry):
        code = reversed_code(box)
        point = first_point(3, code.astype(jnp.float32))
        old_speed = speed_row(3, code)
        new_speeds = [fine_speed(code, e) for e in range(2)]
        for t1 in range(16):
            entry = LEVEL_ROWS[4] + t1
            length = lengths[entry]
            across = point * nodes[entry]
            real = boxes_b[box, 0, t1]
            imag = boxes_b[box, 1, t1]
            old = (across + second_phase) + old_speed * length
            for e in range(2):
                new = (across + fine_phase[e]) + new_speeds[e] * length
                cosine, sine = turn(new - old)
                first = pl.multiple_of((box * 32 + t1) * 8, 8)
                turned[e, pl.ds(first, 8), :] = real * cosine + imag * sine
                turned[e, pl.ds(first + 128, 8), :] = imag * cosine - real * sine
        return carry

    lax.fori_loop(0, 8, rotate_box, 0)

    for e in range(2):
        total = None
        for j in range(8):
            rows = turned[e, pl.ds(j, 256, stride=8), :]
            term = jnp.dot(
                rows, weights[j], preferred_element_type=jnp.float32, precision=lax.Precision.HIGHEST
            )
            total = term if total is None else total + term
        mixed[e] = total

    for e in range(2):
        for a in range(4):
            last_phase[e, a] = fine_two[e] * last_two[a]

    def finish_box(mask):
        target = mask ^ ids[0]
        box, e = target // 2, target % 2
        out = outs[mask]
        code = reversed_code(box)
        point = first_point(3, code.astype(jnp.float32))
        speed = fine_speed(code, e)
        for high in range(2):
            across = point * last_one[high]
            first = pl.multiple_of(box * 32 + high * 8, 8)
            for a in range(4):
                phase = (across + last_phase[e, a]) + speed * last_lengths[high, a]
                cosine, sine = turn(phase)
                real = mixed[e, pl.ds(first, 8), 128 * a : 128 * a + 128]
                imag = mixed[e, pl.ds(first + 16, 8), 128 * a : 128 * a + 128]
                out[high * 4 + a] = real * cosine - imag * sine
                out[8 + high * 4 + a] = real * sine + imag * cosine

    for mask in range(PIECES):
        finish_box(mask)


def levels(chunk, ids, own, other, speeds):
    nodes, waves, lengths = node_tables()
    last_one, last_two, last_lengths = final_tables()
    in_vmem = pl.BlockSpec(memory_space=pltpu.VMEM)
    in_smem = pl.BlockSpec(memory_space=pltpu.SMEM)
    return pl.pallas_call(
        partial(levels_kernel, chunk),
        in_specs=[in_smem, in_smem] + [in_vmem] * 9,
        out_specs=[in_vmem] * PIECES,
        out_shape=[jax.ShapeDtypeStruct((16, 8, 128), jnp.float32)] * PIECES,
        scratch_shapes=[
            pltpu.VMEM((8, 2, 16, 8, 128), jnp.float32),
            pltpu.VMEM((8, 2, 16, 8, 128), jnp.float32),
            pltpu.VMEM((2, 16, 4, 8, 128), jnp.float32),
            pltpu.VMEM((2, 2048, 128), jnp.float32),
            pltpu.VMEM((2, 256, 512), jnp.float32),
            pltpu.VMEM((2, 4, 8, 128), jnp.float32),
        ],
        compiler_params=pltpu.CompilerParams(vmem_limit_bytes=VMEM_LIMIT),
        cost_estimate=pl.CostEstimate(flops=10**8, bytes_accessed=2**23, transcendentals=0),
        name="levels",
    )(
        ids, jnp.asarray(nodes), own, other, speeds, jnp.asarray(waves), jnp.asarray(lengths),
        jnp.asarray(last_one), jnp.asarray(last_two), jnp.asarray(last_lengths),
        jnp.asarray(second_weights()),
    )


def unpack_kernel(ids, *refs):
    pieces, out_ref, tiles, rows = refs[:PIECES], refs[-3], refs[-2], refs[-1]
    me = ids[0]
    for turn_of in range(4):
        group = turn_of ^ (me // 4)
        lanes = pl.ds(pl.multiple_of(group * 128, 128), 128)
        for j in range(4):
            tiles[j ^ (me % 4)] = pieces[4 * turn_of + j][...]
        for part in range(2):
            for high in range(2):
                block = part * 2 + high
                for a in range(4):
                    values = [tiles[j, part * 8 + high * 4 + a] for j in range(4)]
                    for b, tile in enumerate(swap_lanes(values)):
                        t2 = 4 * b + a
                        rows[block, 8 * t2 : 8 * t2 + 8, :] = tile
                for t1 in range(8):
                    out_ref[part, high * 8 + t1, :, lanes] = rows[block, pl.ds(t1, 16, stride=8), :]


def unpack(ids, received, chunk, earlier):
    operands = [ids, *received]
    in_specs = [pl.BlockSpec(memory_space=pltpu.SMEM)]
    in_specs += [pl.BlockSpec((16, 8, 128), lambda i: (0, 0, 0))] * PIECES
    aliases = {}
    if earlier is not None:
        operands.append(earlier)
        in_specs.append(pl.BlockSpec(memory_space=pl.ANY))
        aliases = {len(operands) - 1: 0}
    return pl.pallas_call(
        unpack_kernel,
        grid=(1,),
        in_specs=in_specs,
        out_specs=pl.BlockSpec((2, 16, 16, 512), lambda i: (0, 0, 0, chunk)),
        out_shape=jax.ShapeDtypeStruct((2, 16, 16, 1024), jnp.float32),
        scratch_shapes=[
            pltpu.VMEM((4, 16, 8, 128), jnp.float32),
            pltpu.VMEM((4, 128, 128), jnp.float32),
        ],
        input_output_aliases=aliases,
        compiler_params=pltpu.CompilerParams(vmem_limit_bytes=VMEM_LIMIT),
        cost_estimate=pl.CostEstimate(flops=10**6, bytes_accessed=2**21, transcendentals=0),
        name="unpack",
    )(*operands)


def speed_tables(speed_modes, core):
    numerators, spans = [], []
    for level_index in range(4):
        for code in range(2**level_index):
            numerators.append(core * 2**level_index + code)
            spans.append(2 ** (level_index + 1))
    for code in range(8):
        for e in range(2):
            numerators.append(core * 8 + code)
            spans.append(16)
    codes = jnp.stack(numerators).astype(jnp.float32)
    spans = jnp.asarray(np.array(spans), jnp.float32)
    me = lax.axis_index("bx") * 2 + lax.axis_index("by")
    rows = (jnp.arange(CHUNKS) * PIECES + me).astype(jnp.float32)
    target_one = (rows[:, None] * spans + codes + 0.5) / (TGT * spans)
    columns = jnp.arange(32).astype(jnp.float32)
    coarse = jnp.broadcast_to((columns + 0.5) / TGT, (15, 32))
    fine = jnp.stack([(2 * columns + e + 0.5) / (2 * TGT) for e in range(2)])
    target_two = jnp.concatenate([coarse, jnp.tile(fine, (8, 1))])
    target_one = jnp.broadcast_to(target_one[:, :, None], (CHUNKS, 31, 32))
    target_two = jnp.broadcast_to(target_two[None], (CHUNKS, 31, 32))
    speed = speed_of(speed_modes, target_one.reshape(-1), target_two.reshape(-1))
    return jnp.tile(speed.reshape(CHUNKS, 31, 32), (1, 1, 4))


def on_device_dealt(weights, speed_modes):
    local = weights.reshape(weights.shape[2:])
    core = lax.axis_index("cores")
    me = lax.axis_index("bx") * 2 + lax.axis_index("by")
    ids = jnp.stack([me, core]).astype(jnp.int32)
    speeds = speed_tables(speed_modes, core)
    received = []
    for chunk in range(CHUNKS):
        received.append(deal(pack(local, ids, chunk)))
    results = []
    for chunk in range(CHUNKS):
        own = join(ids, received[chunk])
        other = partner_2(own, "cores", 0)
        results.append(deal(levels(chunk, ids, own, other, speeds[chunk])))
    out = None
    for chunk in range(CHUNKS):
        out = unpack(ids, results[chunk], chunk, out)
    return out.reshape(weights.shape)


def deal(pieces):
    moved = [pieces[0]]
    for mask in range(1, PIECES):
        pairs = [(source, source ^ mask) for source in range(PIECES)]
        moved.append(lax.ppermute(pieces[mask], ("bx", "by"), pairs))
    return moved


def solution(mesh):
    sizes = dict(mesh.shape)
    spec = P(("bx", "cores"), "by", None, None, None, None)
    dealt = (sizes["bx"], sizes["by"], sizes["cores"]) == (8, 2, 2)

    def whole(weights, speed_modes):
        fits = dealt and weights.shape[2:] == (2, 16, 16, 1024)
        return jax.shard_map(
            on_device_dealt if fits else on_device,
            mesh=mesh,
            in_specs=(spec, P()),
            out_specs=spec,
            check_vma=False,
        )(weights, speed_modes)

    return whole
```

```python
from functools import partial
import math

import jax
import jax.numpy as jnp
import ml_dtypes
import numpy as np
from jax import lax
from jax.experimental import pallas as pl
from jax.experimental.pallas import tpu as pltpu
from jax.sharding import PartitionSpec as P

N = 8192
TGT = 32


def partner_2(value, axis, apart):
    mask = 2**apart
    pairs = [(source, source ^ mask) for source in range(lax.axis_size(axis))]
    return lax.ppermute(value, axis, pairs)


def cheb_nodes(degree):
    return np.cos(np.pi * (2 * np.arange(degree) + 1) / (2 * degree))


def lagrange_table(degree):
    points = cheb_nodes(degree)
    result = np.ones((degree, 2 * degree))
    for child_side in range(2):
        inside = (points + 2 * child_side - 1) / 2
        for node_row in range(degree):
            for node_other in range(degree):
                if node_other != node_row:
                    result[node_row, child_side * degree : (child_side + 1) * degree] *= (
                        inside - points[node_other]
                    ) / (points[node_row] - points[node_other])
    return result


def speed_of(speed_modes, target_one, target_two):
    mode_count = speed_modes.shape[0]
    frequencies = jnp.arange(mode_count).astype(jnp.float32) * math.pi
    along_one = jnp.cos(frequencies[:, None] * target_one[None, :])
    along_two = jnp.cos(frequencies[:, None] * target_two[None, :])
    blended = jnp.dot(
        speed_modes, along_two, preferred_element_type=jnp.float32, precision=lax.Precision.HIGHEST
    )
    return 1.0 + jnp.sum(blended * along_one, axis=0)


def rotation(target_one, target_two, speed_value, wave_one, wave_two):
    phase = (
        target_one * wave_one
        + target_two * wave_two
        + speed_value * jnp.sqrt(wave_one * wave_one + wave_two * wave_two)
    )
    phase = phase - jnp.floor(phase)
    angle = 2.0 * math.pi * phase
    return (jnp.cos(angle), jnp.sin(angle))


def node_phase(layout, speed_value, center, half_width, degree):
    target_one, target_two, merge_dim, centers, child_half, other_center, other_half = layout
    points = jnp.asarray(cheb_nodes(degree), jnp.float32)
    merged = center[None, :] + half_width * points[:, None]
    across = other_center[None, :] + other_half * points[:, None]
    if merge_dim == 0:
        return rotation(target_one, target_two, speed_value, merged[:, None, :], across[None, :, :])
    return rotation(target_one, target_two, speed_value, across[:, None, :], merged[None, :, :])


def merge_children(child_low, child_high, layout, speed_modes):
    target_one, target_two, merge_dim, centers, child_half, other_center, other_half = layout
    degree = child_low.shape[1]
    speed_value = speed_of(speed_modes, target_one, target_two)
    lagrange = jnp.asarray(lagrange_table(degree), jnp.float32)
    pieces = []
    for child, center in ((child_low, centers[0]), (child_high, centers[1])):
        cosine, sine_part = node_phase(layout, speed_value, center, child_half, degree)
        real_part = child[0] * cosine + child[1] * sine_part
        imag_part = child[1] * cosine - child[0] * sine_part
        pieces.append(jnp.stack([real_part, imag_part]))
    stacked = jnp.concatenate(pieces, axis=1 + merge_dim)
    if merge_dim == 0:
        blended = jnp.einsum("ij,rjks->riks", lagrange, stacked, precision=lax.Precision.HIGHEST)
    else:
        blended = jnp.einsum("kj,rijs->riks", lagrange, stacked, precision=lax.Precision.HIGHEST)
    cosine, sine_part = node_phase(layout, speed_value, centers[2], 2.0 * child_half, degree)
    return jnp.stack(
        [blended[0] * cosine - blended[1] * sine_part, blended[0] * sine_part + blended[1] * cosine]
    )


def reversed_bits(box_code, bit_count):
    result = jnp.zeros_like(box_code)
    for bit_place in range(bit_count):
        result = result + box_code // 2**bit_place % 2 * 2 ** (bit_count - 1 - bit_place)
    return result


def x_layout(level_index, box_code, targets, y_box, geometry):
    extent, side_count, src_x, src_y = geometry
    span_size = 2 ** (level_index + 1)
    row_index = targets // side_count * span_size + reversed_bits(box_code, level_index + 1)
    target_one = (row_index.astype(jnp.float32) + 0.5) / (side_count * span_size)
    target_two = ((targets % side_count).astype(jnp.float32) + 0.5) / side_count
    parent = (box_code // span_size).astype(jnp.float32)
    child_width = extent * 2**level_index / src_x
    low_center = -extent / 2 + (2.0 * parent + 0.5) * child_width
    high_center = low_center + child_width
    parent_center = -extent / 2 + (parent + 0.5) * (2.0 * child_width)
    other_center = jnp.zeros_like(target_one) + (
        -extent / 2 + (jnp.asarray(y_box).astype(jnp.float32) + 0.5) * (extent / src_y)
    )
    return (
        target_one,
        target_two,
        0,
        (low_center, high_center, parent_center),
        child_width / 2,
        other_center,
        extent / (2 * src_y),
    )


def y_layout(level_index, box_code, targets, x_code, x_bits, geometry):
    extent, side_count, src_x, src_y = geometry
    span_size = 2 ** (level_index + 1)
    col_index = targets % side_count * span_size + reversed_bits(box_code, level_index + 1)
    target_two = (col_index.astype(jnp.float32) + 0.5) / (side_count * span_size)
    row_index = targets // side_count * src_x + reversed_bits(x_code, x_bits)
    target_one = (row_index.astype(jnp.float32) + 0.5) / (side_count * src_x)
    parent = (box_code // span_size).astype(jnp.float32)
    child_width = extent * 2**level_index / src_y
    low_center = -extent / 2 + (2.0 * parent + 0.5) * child_width
    high_center = low_center + child_width
    parent_center = -extent / 2 + (parent + 0.5) * (2.0 * child_width)
    other_center = jnp.zeros_like(target_one)
    return (
        target_one,
        target_two,
        1,
        (low_center, high_center, parent_center),
        child_width / 2,
        other_center,
        extent / 2,
    )


def pair_level(current, partner, level_index, box_code, targets, layout_fn, speed_modes):
    own_bit = box_code // 2**level_index % 2
    child_low = jnp.where(own_bit == 0, current, partner)
    child_high = jnp.where(own_bit == 0, partner, current)
    box_codes = jnp.zeros_like(targets) + box_code
    return merge_children(
        child_low, child_high, layout_fn(level_index, box_codes, targets), speed_modes
    )


def on_device(weights, speed_modes):
    current = weights.reshape(weights.shape[2:])
    pair_count = current.shape[3]
    core_count = lax.axis_size("cores")
    src_x = lax.axis_size("bx") * core_count
    src_y = lax.axis_size("by")
    x_bits = src_x.bit_length() - 1
    y_bits = src_y.bit_length() - 1
    x_code = lax.axis_index("bx") * core_count + lax.axis_index("cores")
    y_box = lax.axis_index("by")
    geometry = (float(N), TGT, src_x, src_y)
    targets = jnp.arange(pair_count, dtype=jnp.int32)
    first_layout = partial(x_layout, y_box=y_box, geometry=geometry)
    second_layout = partial(y_layout, x_code=x_code, x_bits=x_bits, geometry=geometry)
    for level_index in range(x_bits):
        if level_index == 0:
            partner = partner_2(current, "cores", 0)
        else:
            partner = partner_2(current, "bx", level_index - 1)
        current = pair_level(
            current, partner, level_index, x_code, targets, first_layout, speed_modes
        )
    for level_index in range(y_bits):
        partner = partner_2(current, "by", level_index)
        current = pair_level(
            current, partner, level_index, y_box, targets, second_layout, speed_modes
        )
    return current.reshape(weights.shape)


SIN_HALF = (4.442879586386342, -7.3078180422392816, 3.597788667381583, -0.7912380409231197)
COS_HALF = (
    1.4142134965636117,
    -6.978850988059019,
    5.739461167077472,
    -1.883562964211867,
    0.3106981455985473,
)
CHUNKS = 2
PIECES = 16
LEVEL_ROWS = (0, 256, 384, 448, 480)
VMEM_LIMIT = 48 * 2**20


def node_tables():
    points = cheb_nodes(16).astype(np.float32)
    nodes = []
    for level_index in range(5):
        width = np.float32(N * 2**level_index / 16)
        for box in range(16 >> level_index):
            center = np.float32(-N / 2 + (box + 0.5) * width)
            nodes.append(center + (width / 2) * points)
    nodes = np.concatenate(nodes).astype(np.float32)
    sub = np.arange(8)
    lane = np.arange(128)
    half = (sub // 4)[:, None] + 0 * lane[None, :]
    second = (lane // 32 * 4)[None, :] + (sub % 4)[:, None]
    wave_two = (-N / 2 + (half + 0.5) * (N / 2)).astype(np.float32) + np.float32(N / 4) * points[second]
    wave_two = wave_two.astype(np.float32)
    lengths = np.sqrt(nodes[:, None, None] * nodes[:, None, None] + wave_two * wave_two)
    return nodes, wave_two, lengths.astype(np.float32)


def final_tables():
    points = cheb_nodes(16).astype(np.float32) * np.float32(N / 2)
    lane = np.arange(128)
    one = np.broadcast_to(points.reshape(2, 8, 1), (2, 8, 128)).astype(np.float32)
    two = np.stack([np.broadcast_to(points[lane // 32 * 4 + a], (8, 128)) for a in range(4)])
    two = two.astype(np.float32)
    lengths = np.sqrt((one * one)[:, None] + (two * two)[None, :]).astype(np.float32)
    return np.array(one), two, lengths


def in_two_parts(table):
    high = table.astype(ml_dtypes.bfloat16)
    low = (table - high.astype(np.float32)).astype(ml_dtypes.bfloat16)
    return high, low


def first_weights():
    table = lagrange_table(16).astype(np.float32)
    high, low = in_two_parts(np.kron(table, np.eye(8, dtype=np.float32)))
    return np.concatenate([high, low])


def second_weights():
    table = lagrange_table(16)
    result = np.zeros((8, 4, 32, 4, 4, 32), np.float32)
    same = np.eye(32, dtype=np.float32)
    for half in range(2):
        for a in range(4):
            for b in range(4):
                for out_a in range(4):
                    for out_b in range(4):
                        weight = table[4 * out_b + out_a, half * 16 + 4 * b + a]
                        result[half * 4 + a, b, :, out_a, out_b, :] = np.float32(weight) * same
    return np.stack(in_two_parts(result.reshape(4, 256, 512)))


def turn(phase):
    part = phase - jnp.round(phase)
    square = part * part
    sine = SIN_HALF[3]
    for coefficient in SIN_HALF[2::-1]:
        sine = sine * square + coefficient
    sine = sine * part
    cosine = COS_HALF[4]
    for coefficient in COS_HALF[3::-1]:
        cosine = cosine * square + coefficient
    return 1.0 - sine * sine, sine * cosine


def swap_lanes(values):
    lane = lax.broadcasted_iota(jnp.int32, (8, 128), 1)
    low = lane < 64
    even = lane // 32 % 2 == 0
    half = [None] * 4
    for b in range(2):
        half[b] = jnp.where(low, values[b], pltpu.roll(values[b + 2], 64, 1))
        half[b + 2] = jnp.where(low, pltpu.roll(values[b], 64, 1), values[b + 2])
    full = [None] * 4
    for j in (0, 2):
        full[j] = jnp.where(even, half[j], pltpu.roll(half[j + 1], 32, 1))
        full[j + 1] = jnp.where(even, pltpu.roll(half[j], 96, 1), half[j + 1])
    return full


def pack_rows(in_ref, lanes, tiles):
    upper = lax.broadcasted_iota(jnp.int32, (8, 128), 0) < 4
    for t1 in range(16):
        groups = [None] * 4
        for high in range(2):
            real = in_ref[0, t1, 8 * high : 8 * high + 8, lanes]
            imag = in_ref[1, t1, 8 * high : 8 * high + 8, lanes]
            groups[2 * high] = jnp.where(upper, real, pltpu.roll(imag, 4, 0))
            groups[2 * high + 1] = jnp.where(upper, pltpu.roll(real, 4, 0), imag)
        for j, tile in enumerate(swap_lanes(groups)):
            tiles[j, t1] = tile


def pack_kernel(in_ref, out_ref):
    pack_rows(in_ref, slice(None), out_ref)


def pack(weights, chunk):
    return pl.pallas_call(
        pack_kernel,
        grid=(4,),
        in_specs=[pl.BlockSpec((2, 16, 16, 128), lambda i: (0, 0, 0, 4 * chunk + i))],
        out_specs=pl.BlockSpec((4, 16, 8, 128), lambda i: (i, 0, 0, 0)),
        out_shape=jax.ShapeDtypeStruct((PIECES, 16, 8, 128), jnp.float32),
        cost_estimate=pl.CostEstimate(flops=10**6, bytes_accessed=2**21, transcendentals=0),
        name="pack",
    )(weights)


def pack_masks_kernel(ids, in_ref, *refs):
    outs, tiles = refs[:4], refs[4]
    me = ids[0]

    def step(mz, carry):
        group = mz ^ (me // 4)
        pack_rows(in_ref, pl.ds(pl.multiple_of(group * 128, 128), 128), tiles)
        for mxy in range(4):
            outs[mxy][mz] = tiles[mxy ^ (me % 4)]
        return carry

    lax.fori_loop(0, 4, step, 0)


BUNDLE = (4, 16, 8, 128)


def pack_masks(weights, ids, chunk):
    return pl.pallas_call(
        pack_masks_kernel,
        grid=(1,),
        in_specs=[
            pl.BlockSpec(memory_space=pltpu.SMEM),
            pl.BlockSpec((2, 16, 16, 512), lambda i: (0, 0, 0, chunk)),
        ],
        out_specs=[pl.BlockSpec(BUNDLE, lambda i: (0, 0, 0, 0))] * 4,
        out_shape=[jax.ShapeDtypeStruct(BUNDLE, jnp.float32)] * 4,
        scratch_shapes=[pltpu.VMEM(BUNDLE, jnp.float32)],
        compiler_params=pltpu.CompilerParams(vmem_limit_bytes=VMEM_LIMIT),
        cost_estimate=pl.CostEstimate(flops=10**6, bytes_accessed=2**21, transcendentals=0),
        name="pack_masks",
    )(ids, weights)


def regroup_kernel(*refs):
    for first in range(4):
        for second in range(4):
            refs[4 + second][first] = refs[first][second]


def regroup(bundles):
    in_vmem = pl.BlockSpec(memory_space=pltpu.VMEM)
    return pl.pallas_call(
        regroup_kernel,
        in_specs=[in_vmem] * 4,
        out_specs=[in_vmem] * 4,
        out_shape=[jax.ShapeDtypeStruct(BUNDLE, jnp.float32)] * 4,
        compiler_params=pltpu.CompilerParams(vmem_limit_bytes=VMEM_LIMIT),
        cost_estimate=pl.CostEstimate(flops=10**5, bytes_accessed=2**21, transcendentals=0),
        name="regroup",
    )(*bundles)


def exchange(bundles, unit):
    moved = [bundles[0]]
    for mask in range(1, 4):
        pairs = [(source, source ^ (mask * unit)) for source in range(PIECES)]
        moved.append(lax.ppermute(bundles[mask], ("bx", "by"), pairs))
    return moved


def merge_halves(out_ref, box, t1, low, high):
    upper = lax.broadcasted_iota(jnp.int32, (8, 128), 0) < 4
    out_ref[box, 0, t1] = jnp.where(upper, low, pltpu.roll(high, 4, 0))
    out_ref[box, 1, t1] = jnp.where(upper, pltpu.roll(low, 4, 0), high)


def join_kernel(in_ref, out_ref):
    def step(box, carry):
        for t1 in range(16):
            merge_halves(out_ref, box, t1, in_ref[2 * box, t1], in_ref[2 * box + 1, t1])
        return carry

    lax.fori_loop(0, 8, step, 0)


def join_masks_kernel(ids, *refs):
    bundles, out_ref = refs[:4], refs[4]
    me = ids[0]
    is_low = jnp.broadcast_to(me % 2, (8, 128)) == 0
    for mz in range(4):
        for mx in range(2):
            box = (2 * mz + mx) ^ (me // 2)
            for t1 in range(16):
                mine = bundles[mz][2 * mx, t1]
                partner = bundles[mz][2 * mx + 1, t1]
                low = jnp.where(is_low, mine, partner)
                high = jnp.where(is_low, partner, mine)
                merge_halves(out_ref, box, t1, low, high)


def join(received, ids=None):
    in_vmem = pl.BlockSpec(memory_space=pltpu.VMEM)
    if ids is None:
        kernel, operands, in_specs = join_kernel, [received], [in_vmem]
    else:
        kernel, operands = join_masks_kernel, [ids, *received]
        in_specs = [pl.BlockSpec(memory_space=pltpu.SMEM)] + [in_vmem] * 4
    return pl.pallas_call(
        kernel,
        in_specs=in_specs,
        out_specs=in_vmem,
        out_shape=jax.ShapeDtypeStruct((8, 2, 16, 8, 128), jnp.float32),
        compiler_params=pltpu.CompilerParams(vmem_limit_bytes=VMEM_LIMIT),
        cost_estimate=pl.CostEstimate(flops=10**6, bytes_accessed=2**21, transcendentals=0),
        name="join",
    )(*operands)


def levels_kernel(
    chunk, by_masks, ids, nodes, own, other, speeds, waves, lengths, last_one, last_two,
    last_lengths, first_table, second_table, *refs,
):
    outs = refs[:4] if by_masks else refs[0]
    boxes_a, boxes_b, sums, turned, mixed, last_phase = refs[-6:]
    row = (chunk * PIECES + ids[0]).astype(jnp.float32)
    core = ids[1]
    core_float = core.astype(jnp.float32)
    wave_two = waves[...]
    lane = lax.broadcasted_iota(jnp.int32, (8, 128), 1)
    along_two = ((lane % 32).astype(jnp.float32) + 0.5) * (1.0 / 32)
    second_phase = along_two * wave_two

    def first_point(level_index, low_code):
        span = 2.0 ** (level_index + 1)
        code = core_float * 2.0**level_index + low_code
        return (row * span + code + 0.5) * (1.0 / (32 * span))

    def speed_row(level_index, low_code):
        return jnp.broadcast_to(speeds[pl.ds(2**level_index - 1 + low_code, 1), :], (8, 128))

    def blend(slot, target, boxes):
        rows = sums[slot].astype(jnp.bfloat16)
        both = jnp.dot(first_table[...], rows, preferred_element_type=jnp.float32)
        total = both[:128] + both[128:]
        for n, box in enumerate(boxes):
            for part in range(2):
                column = 128 * (2 * n + part)
                target[box, part] = total[:, column : column + 128].reshape(16, 8, 128)

    def put(slot, first_row, column, real, imag):
        sums[slot, pl.ds(first_row, 8), 256 * column : 256 * column + 128] = real
        sums[slot, pl.ds(first_row, 8), 256 * column + 128 : 256 * column + 256] = imag

    def first_level(pair, slot):
        point = first_point(0, 0.0)
        speed = speed_row(0, 0)
        for n in range(2):
            box = 2 * pair + n
            for source, child in ((own, core), (other, 1 - core)):
                for t1 in range(16):
                    entry = (2 * box + child) * 16 + t1
                    phase = (point * nodes[entry] + second_phase) + speed * lengths[entry]
                    cosine, sine = turn(phase)
                    real = source[box, 0, t1]
                    imag = source[box, 1, t1]
                    first_row = pl.multiple_of(child * 128 + 8 * t1, 8)
                    put(slot, first_row, n, real * cosine + imag * sine, imag * cosine - real * sine)
        blend(slot, boxes_a, [2 * pair, 2 * pair + 1])

    def later_level(level_index, source, target, index, slot):
        low_bits = level_index - 1
        stride = 2**low_bits
        parent = index // stride
        low = index % stride
        code = jnp.int32(0)
        for bit in range(low_bits):
            code = code + low // 2**bit % 2 * 2 ** (low_bits - 1 - bit)
        before = first_point(level_index - 1, code.astype(jnp.float32))
        before_speed = speed_row(level_index - 1, code)
        points = [first_point(level_index, (2 * code + b).astype(jnp.float32)) for b in range(2)]
        point_speeds = [speed_row(level_index, 2 * code + b) for b in range(2)]
        first_box = parent * (2 * stride) + low
        for child in range(2):
            for t1 in range(16):
                entry = LEVEL_ROWS[level_index] + (2 * parent + child) * 16 + t1
                length = lengths[entry]
                wave = nodes[entry]
                real = source[first_box + child * stride, 0, t1]
                imag = source[first_box + child * stride, 1, t1]
                old = (before * wave + second_phase) + before_speed * length
                for b in range(2):
                    new = (points[b] * wave + second_phase) + point_speeds[b] * length
                    cosine, sine = turn(new - old)
                    first_row = child * 128 + 8 * t1
                    put(slot, first_row, b, real * cosine + imag * sine, imag * cosine - real * sine)
        blend(slot, target, [first_box, first_box + stride])

    def in_pairs(one):
        def step(half, carry):
            for slot in range(2):
                one(2 * half + slot, slot)
            return carry

        lax.fori_loop(0, 2, step, 0)

    in_pairs(first_level)
    in_pairs(partial(later_level, 1, boxes_a, boxes_b))
    in_pairs(partial(later_level, 2, boxes_b, boxes_a))
    in_pairs(partial(later_level, 3, boxes_a, boxes_b))

    fine_two = [((lane % 32).astype(jnp.float32) * 2.0 + (e + 0.5)) * (1.0 / 64) for e in range(2)]
    fine_phase = [fine_two[e] * wave_two for e in range(2)]

    def reversed_code(box):
        return box % 2 * 4 + box // 2 % 2 * 2 + box // 4

    def fine_speed(code, e):
        return jnp.broadcast_to(speeds[pl.ds(15 + 2 * code + e, 1), :], (8, 128))

    def rotate_box(box, carry):
        code = reversed_code(box)
        point = first_point(3, code.astype(jnp.float32))
        old_speed = speed_row(3, code)
        new_speeds = [fine_speed(code, e) for e in range(2)]
        for t1 in range(16):
            entry = LEVEL_ROWS[4] + t1
            length = lengths[entry]
            across = point * nodes[entry]
            real = boxes_b[box, 0, t1]
            imag = boxes_b[box, 1, t1]
            old = (across + second_phase) + old_speed * length
            for e in range(2):
                new = (across + fine_phase[e]) + new_speeds[e] * length
                cosine, sine = turn(new - old)
                first = pl.multiple_of((e * 256 + box * 32 + t1) * 8, 8)
                turned[pl.ds(first, 8), :] = real * cosine + imag * sine
                turned[pl.ds(first + 128, 8), :] = imag * cosine - real * sine
        return carry

    lax.fori_loop(0, 8, rotate_box, 0)

    for e in range(2):
        for a in range(4):
            last_phase[e, a] = fine_two[e] * last_two[a]

    total = None
    for j in range(4):
        rows = jnp.concatenate(
            [turned[pl.ds(2 * j + k, 512, stride=8), :] for k in range(2)], axis=1
        ).astype(jnp.bfloat16)
        for part in range(2):
            term = jnp.dot(rows, second_table[part, j], preferred_element_type=jnp.float32)
            total = term if total is None else total + term
    mixed[...] = total

    def finish_box(target, out):
        box, e = target // 2, target % 2
        code = reversed_code(box)
        point = first_point(3, code.astype(jnp.float32))
        speed = fine_speed(code, e)
        for high in range(2):
            across = point * last_one[high]
            first = pl.multiple_of(e * 256 + box * 32 + high * 8, 8)
            for a in range(4):
                phase = (across + last_phase[e, a]) + speed * last_lengths[high, a]
                cosine, sine = turn(phase)
                real = mixed[pl.ds(first, 8), 128 * a : 128 * a + 128]
                imag = mixed[pl.ds(first + 16, 8), 128 * a : 128 * a + 128]
                out[high * 4 + a] = real * cosine - imag * sine
                out[8 + high * 4 + a] = real * sine + imag * cosine

    def finish_row(major, carry):
        for minor in range(4):
            if by_masks:
                finish_box((4 * minor + major) ^ ids[0], outs[minor].at[major])
            else:
                finish_box(4 * major + minor, outs.at[4 * major + minor])
        return carry

    lax.fori_loop(0, 4, finish_row, 0)


def levels(chunk, by_masks, ids, own, other, speeds):
    nodes, waves, lengths = node_tables()
    last_one, last_two, last_lengths = final_tables()
    tables = (waves, lengths, last_one, last_two, last_lengths, first_weights(), second_weights())
    in_vmem = pl.BlockSpec(memory_space=pltpu.VMEM)
    in_smem = pl.BlockSpec(memory_space=pltpu.SMEM)
    if by_masks:
        out_shape = [jax.ShapeDtypeStruct(BUNDLE, jnp.float32)] * 4
        out_specs = [in_vmem] * 4
    else:
        out_shape = jax.ShapeDtypeStruct((PIECES, 16, 8, 128), jnp.float32)
        out_specs = in_vmem
    return pl.pallas_call(
        partial(levels_kernel, chunk, by_masks),
        in_specs=[in_smem, in_smem] + [in_vmem] * 10,
        out_specs=out_specs,
        out_shape=out_shape,
        scratch_shapes=[
            pltpu.VMEM((8, 2, 16, 8, 128), jnp.float32),
            pltpu.VMEM((8, 2, 16, 8, 128), jnp.float32),
            pltpu.VMEM((2, 256, 512), jnp.float32),
            pltpu.VMEM((4096, 128), jnp.float32),
            pltpu.VMEM((512, 512), jnp.float32),
            pltpu.VMEM((2, 4, 8, 128), jnp.float32),
        ],
        compiler_params=pltpu.CompilerParams(vmem_limit_bytes=VMEM_LIMIT),
        cost_estimate=pl.CostEstimate(flops=10**8, bytes_accessed=2**23, transcendentals=0),
        name="levels",
    )(ids, jnp.asarray(nodes), own, other, speeds, *[jnp.asarray(table) for table in tables])


def unpack_rows(tiles, rows, out_ref, lanes):
    for part in range(2):
        for high in range(2):
            block = part * 2 + high
            for a in range(4):
                values = [tiles[j, part * 8 + high * 4 + a] for j in range(4)]
                for b, tile in enumerate(swap_lanes(values)):
                    t2 = 4 * b + a
                    rows[block, 8 * t2 : 8 * t2 + 8, :] = tile
            for t1 in range(8):
                out_ref[part, high * 8 + t1, :, lanes] = rows[block, pl.ds(t1, 16, stride=8), :]


def unpack_kernel(*refs):
    unpack_rows(refs[0], refs[-1], refs[-2], slice(None))


def unpack_masks_kernel(ids, *refs):
    bundles, out_ref, tiles, rows = refs[:4], refs[-3], refs[-2], refs[-1]
    me = ids[0]

    def step(mz, carry):
        group = mz ^ (me // 4)
        for mxy in range(4):
            tiles[mxy ^ (me % 4)] = bundles[mxy][mz]
        unpack_rows(tiles, rows, out_ref, pl.ds(pl.multiple_of(group * 128, 128), 128))
        return carry

    lax.fori_loop(0, 4, step, 0)


def unpack(received, chunk, earlier, ids=None):
    rows = pltpu.VMEM((4, 128, 128), jnp.float32)
    if ids is None:
        kernel, operands, grid = unpack_kernel, [received], (4,)
        in_specs = [pl.BlockSpec((4, 16, 8, 128), lambda i: (i, 0, 0, 0))]
        out_spec = pl.BlockSpec((2, 16, 16, 128), lambda i: (0, 0, 0, 4 * chunk + i))
        scratch = [rows]
    else:
        kernel, operands, grid = unpack_masks_kernel, [ids, *received], (1,)
        in_specs = [pl.BlockSpec(memory_space=pltpu.SMEM)]
        in_specs += [pl.BlockSpec(BUNDLE, lambda i: (0, 0, 0, 0))] * 4
        out_spec = pl.BlockSpec((2, 16, 16, 512), lambda i: (0, 0, 0, chunk))
        scratch = [pltpu.VMEM(BUNDLE, jnp.float32), rows]
    aliases = {}
    if earlier is not None:
        aliases = {len(operands): 0}
        operands.append(earlier)
        in_specs.append(pl.BlockSpec(memory_space=pl.ANY))
    return pl.pallas_call(
        kernel,
        grid=grid,
        in_specs=in_specs,
        out_specs=out_spec,
        out_shape=jax.ShapeDtypeStruct((2, 16, 16, 1024), jnp.float32),
        scratch_shapes=scratch,
        input_output_aliases=aliases,
        compiler_params=pltpu.CompilerParams(vmem_limit_bytes=VMEM_LIMIT),
        cost_estimate=pl.CostEstimate(flops=10**6, bytes_accessed=2**21, transcendentals=0),
        name="unpack",
    )(*operands)


def speed_tables(speed_modes, core):
    numerators, spans = [], []
    for level_index in range(4):
        for code in range(2**level_index):
            numerators.append(core * 2**level_index + code)
            spans.append(2 ** (level_index + 1))
    for code in range(8):
        for e in range(2):
            numerators.append(core * 8 + code)
            spans.append(16)
    codes = jnp.stack(numerators).astype(jnp.float32)
    spans = jnp.asarray(np.array(spans), jnp.float32)
    me = lax.axis_index("bx") * 2 + lax.axis_index("by")
    rows = (jnp.arange(CHUNKS) * PIECES + me).astype(jnp.float32)
    target_one = (rows[:, None] * spans + codes + 0.5) / (TGT * spans)
    columns = jnp.arange(32).astype(jnp.float32)
    coarse = jnp.broadcast_to((columns + 0.5) / TGT, (15, 32))
    fine = jnp.stack([(2 * columns + e + 0.5) / (2 * TGT) for e in range(2)])
    target_two = jnp.concatenate([coarse, jnp.tile(fine, (8, 1))])
    target_one = jnp.broadcast_to(target_one[:, :, None], (CHUNKS, 31, 32))
    target_two = jnp.broadcast_to(target_two[None], (CHUNKS, 31, 32))
    speed = speed_of(speed_modes, target_one.reshape(-1), target_two.reshape(-1))
    return jnp.tile(speed.reshape(CHUNKS, 31, 32), (1, 1, 4))


def on_device_dealt(weights, speed_modes):
    local = weights.reshape(weights.shape[2:])
    core = lax.axis_index("cores")
    me = lax.axis_index("bx") * 2 + lax.axis_index("by")
    ids = jnp.stack([me, core]).astype(jnp.int32)
    speeds = speed_tables(speed_modes, core)

    first = deal(pack(local, 0))
    near = exchange(pack_masks(local, ids, 1), 1)
    second = exchange(regroup(near), 4)

    own = join(first)
    result = levels(0, True, ids, own, partner_2(own, "cores", 0), speeds[0])
    far = exchange(result, 4)
    back_first = exchange(regroup(far), 1)

    own = join(second, ids)
    result = levels(1, False, ids, own, partner_2(own, "cores", 0), speeds[1])
    back_second = deal(result)

    out = unpack(back_first, 0, None, ids)
    out = unpack(back_second, 1, out)
    return out.reshape(weights.shape)


def deal(pieces):
    return lax.all_to_all(pieces, ("bx", "by"), 0, 0, tiled=True)


def solution(mesh):
    sizes = dict(mesh.shape)
    spec = P(("bx", "cores"), "by", None, None, None, None)
    dealt = (sizes["bx"], sizes["by"], sizes["cores"]) == (8, 2, 2)

    def whole(weights, speed_modes):
        fits = dealt and weights.shape[2:] == (2, 16, 16, 1024)
        return jax.shard_map(
            on_device_dealt if fits else on_device,
            mesh=mesh,
            in_specs=(spec, P()),
            out_specs=spec,
            check_vma=False,
        )(weights, speed_modes)

    return whole
```

```python
from functools import partial
import math

import jax
import jax.numpy as jnp
import ml_dtypes
import numpy as np
from jax import lax
from jax.experimental import pallas as pl
from jax.experimental.pallas import tpu as pltpu
from jax.sharding import PartitionSpec as P

N = 8192
TGT = 32


def partner_2(value, axis, apart):
    mask = 2**apart
    pairs = [(source, source ^ mask) for source in range(lax.axis_size(axis))]
    return lax.ppermute(value, axis, pairs)


def cheb_nodes(degree):
    return np.cos(np.pi * (2 * np.arange(degree) + 1) / (2 * degree))


def lagrange_table(degree):
    points = cheb_nodes(degree)
    result = np.ones((degree, 2 * degree))
    for child_side in range(2):
        inside = (points + 2 * child_side - 1) / 2
        for node_row in range(degree):
            for node_other in range(degree):
                if node_other != node_row:
                    result[node_row, child_side * degree : (child_side + 1) * degree] *= (
                        inside - points[node_other]
                    ) / (points[node_row] - points[node_other])
    return result


def speed_of(speed_modes, target_one, target_two):
    mode_count = speed_modes.shape[0]
    frequencies = jnp.arange(mode_count).astype(jnp.float32) * math.pi
    along_one = jnp.cos(frequencies[:, None] * target_one[None, :])
    along_two = jnp.cos(frequencies[:, None] * target_two[None, :])
    blended = jnp.dot(
        speed_modes, along_two, preferred_element_type=jnp.float32, precision=lax.Precision.HIGHEST
    )
    return 1.0 + jnp.sum(blended * along_one, axis=0)


def rotation(target_one, target_two, speed_value, wave_one, wave_two):
    phase = (
        target_one * wave_one
        + target_two * wave_two
        + speed_value * jnp.sqrt(wave_one * wave_one + wave_two * wave_two)
    )
    phase = phase - jnp.floor(phase)
    angle = 2.0 * math.pi * phase
    return (jnp.cos(angle), jnp.sin(angle))


def node_phase(layout, speed_value, center, half_width, degree):
    target_one, target_two, merge_dim, centers, child_half, other_center, other_half = layout
    points = jnp.asarray(cheb_nodes(degree), jnp.float32)
    merged = center[None, :] + half_width * points[:, None]
    across = other_center[None, :] + other_half * points[:, None]
    if merge_dim == 0:
        return rotation(target_one, target_two, speed_value, merged[:, None, :], across[None, :, :])
    return rotation(target_one, target_two, speed_value, across[:, None, :], merged[None, :, :])


def merge_children(child_low, child_high, layout, speed_modes):
    target_one, target_two, merge_dim, centers, child_half, other_center, other_half = layout
    degree = child_low.shape[1]
    speed_value = speed_of(speed_modes, target_one, target_two)
    lagrange = jnp.asarray(lagrange_table(degree), jnp.float32)
    pieces = []
    for child, center in ((child_low, centers[0]), (child_high, centers[1])):
        cosine, sine_part = node_phase(layout, speed_value, center, child_half, degree)
        real_part = child[0] * cosine + child[1] * sine_part
        imag_part = child[1] * cosine - child[0] * sine_part
        pieces.append(jnp.stack([real_part, imag_part]))
    stacked = jnp.concatenate(pieces, axis=1 + merge_dim)
    if merge_dim == 0:
        blended = jnp.einsum("ij,rjks->riks", lagrange, stacked, precision=lax.Precision.HIGHEST)
    else:
        blended = jnp.einsum("kj,rijs->riks", lagrange, stacked, precision=lax.Precision.HIGHEST)
    cosine, sine_part = node_phase(layout, speed_value, centers[2], 2.0 * child_half, degree)
    return jnp.stack(
        [blended[0] * cosine - blended[1] * sine_part, blended[0] * sine_part + blended[1] * cosine]
    )


def reversed_bits(box_code, bit_count):
    result = jnp.zeros_like(box_code)
    for bit_place in range(bit_count):
        result = result + box_code // 2**bit_place % 2 * 2 ** (bit_count - 1 - bit_place)
    return result


def x_layout(level_index, box_code, targets, y_box, geometry):
    extent, side_count, src_x, src_y = geometry
    span_size = 2 ** (level_index + 1)
    row_index = targets // side_count * span_size + reversed_bits(box_code, level_index + 1)
    target_one = (row_index.astype(jnp.float32) + 0.5) / (side_count * span_size)
    target_two = ((targets % side_count).astype(jnp.float32) + 0.5) / side_count
    parent = (box_code // span_size).astype(jnp.float32)
    child_width = extent * 2**level_index / src_x
    low_center = -extent / 2 + (2.0 * parent + 0.5) * child_width
    high_center = low_center + child_width
    parent_center = -extent / 2 + (parent + 0.5) * (2.0 * child_width)
    other_center = jnp.zeros_like(target_one) + (
        -extent / 2 + (jnp.asarray(y_box).astype(jnp.float32) + 0.5) * (extent / src_y)
    )
    return (
        target_one,
        target_two,
        0,
        (low_center, high_center, parent_center),
        child_width / 2,
        other_center,
        extent / (2 * src_y),
    )


def y_layout(level_index, box_code, targets, x_code, x_bits, geometry):
    extent, side_count, src_x, src_y = geometry
    span_size = 2 ** (level_index + 1)
    col_index = targets % side_count * span_size + reversed_bits(box_code, level_index + 1)
    target_two = (col_index.astype(jnp.float32) + 0.5) / (side_count * span_size)
    row_index = targets // side_count * src_x + reversed_bits(x_code, x_bits)
    target_one = (row_index.astype(jnp.float32) + 0.5) / (side_count * src_x)
    parent = (box_code // span_size).astype(jnp.float32)
    child_width = extent * 2**level_index / src_y
    low_center = -extent / 2 + (2.0 * parent + 0.5) * child_width
    high_center = low_center + child_width
    parent_center = -extent / 2 + (parent + 0.5) * (2.0 * child_width)
    other_center = jnp.zeros_like(target_one)
    return (
        target_one,
        target_two,
        1,
        (low_center, high_center, parent_center),
        child_width / 2,
        other_center,
        extent / 2,
    )


def pair_level(current, partner, level_index, box_code, targets, layout_fn, speed_modes):
    own_bit = box_code // 2**level_index % 2
    child_low = jnp.where(own_bit == 0, current, partner)
    child_high = jnp.where(own_bit == 0, partner, current)
    box_codes = jnp.zeros_like(targets) + box_code
    return merge_children(
        child_low, child_high, layout_fn(level_index, box_codes, targets), speed_modes
    )


def on_device(weights, speed_modes):
    current = weights.reshape(weights.shape[2:])
    pair_count = current.shape[3]
    core_count = lax.axis_size("cores")
    src_x = lax.axis_size("bx") * core_count
    src_y = lax.axis_size("by")
    x_bits = src_x.bit_length() - 1
    y_bits = src_y.bit_length() - 1
    x_code = lax.axis_index("bx") * core_count + lax.axis_index("cores")
    y_box = lax.axis_index("by")
    geometry = (float(N), TGT, src_x, src_y)
    targets = jnp.arange(pair_count, dtype=jnp.int32)
    first_layout = partial(x_layout, y_box=y_box, geometry=geometry)
    second_layout = partial(y_layout, x_code=x_code, x_bits=x_bits, geometry=geometry)
    for level_index in range(x_bits):
        if level_index == 0:
            partner = partner_2(current, "cores", 0)
        else:
            partner = partner_2(current, "bx", level_index - 1)
        current = pair_level(
            current, partner, level_index, x_code, targets, first_layout, speed_modes
        )
    for level_index in range(y_bits):
        partner = partner_2(current, "by", level_index)
        current = pair_level(
            current, partner, level_index, y_box, targets, second_layout, speed_modes
        )
    return current.reshape(weights.shape)


SIN_HALF = (4.442879586386342, -7.3078180422392816, 3.597788667381583, -0.7912380409231197)
COS_HALF = (
    1.4142134965636117,
    -6.978850988059019,
    5.739461167077472,
    -1.883562964211867,
    0.3106981455985473,
)
CHUNKS = 2
PIECES = 16
LEVEL_ROWS = (0, 256, 384, 448, 480)
VMEM_LIMIT = 48 * 2**20


def node_tables():
    points = cheb_nodes(16).astype(np.float32)
    nodes = []
    for level_index in range(5):
        width = np.float32(N * 2**level_index / 16)
        for box in range(16 >> level_index):
            center = np.float32(-N / 2 + (box + 0.5) * width)
            nodes.append(center + (width / 2) * points)
    nodes = np.concatenate(nodes).astype(np.float32)
    sub = np.arange(8)
    lane = np.arange(128)
    half = (sub // 4)[:, None] + 0 * lane[None, :]
    second = (lane // 32 * 4)[None, :] + (sub % 4)[:, None]
    wave_two = (-N / 2 + (half + 0.5) * (N / 2)).astype(np.float32) + np.float32(N / 4) * points[second]
    wave_two = wave_two.astype(np.float32)
    lengths = np.sqrt(nodes[:, None, None] * nodes[:, None, None] + wave_two * wave_two)
    return nodes, wave_two, lengths.astype(np.float32)


def final_tables():
    points = cheb_nodes(16).astype(np.float32) * np.float32(N / 2)
    lane = np.arange(128)
    one = np.broadcast_to(points.reshape(2, 8, 1), (2, 8, 128)).astype(np.float32)
    two = np.stack([np.broadcast_to(points[lane // 32 * 4 + a], (8, 128)) for a in range(4)])
    two = two.astype(np.float32)
    lengths = np.sqrt((one * one)[:, None] + (two * two)[None, :]).astype(np.float32)
    return np.array(one), two, lengths


def in_two_parts(table):
    high = table.astype(ml_dtypes.bfloat16)
    low = (table - high.astype(np.float32)).astype(ml_dtypes.bfloat16)
    return high, low


def first_weights():
    table = lagrange_table(16).astype(np.float32)
    high, low = in_two_parts(np.kron(table, np.eye(8, dtype=np.float32)))
    return np.concatenate([high, low])


def second_weights():
    table = lagrange_table(16)
    result = np.zeros((8, 4, 32, 4, 4, 32), np.float32)
    same = np.eye(32, dtype=np.float32)
    for half in range(2):
        for a in range(4):
            for b in range(4):
                for out_a in range(4):
                    for out_b in range(4):
                        weight = table[4 * out_b + out_a, half * 16 + 4 * b + a]
                        result[half * 4 + a, b, :, out_a, out_b, :] = np.float32(weight) * same
    return np.stack(in_two_parts(result.reshape(4, 256, 512)))


def turn(phase):
    part = phase - jnp.round(phase)
    square = part * part
    sine = SIN_HALF[3]
    for coefficient in SIN_HALF[2::-1]:
        sine = sine * square + coefficient
    sine = sine * part
    cosine = COS_HALF[4]
    for coefficient in COS_HALF[3::-1]:
        cosine = cosine * square + coefficient
    return 1.0 - sine * sine, sine * cosine


def swap_lanes(values):
    lane = lax.broadcasted_iota(jnp.int32, (8, 128), 1)
    low = lane < 64
    even = lane // 32 % 2 == 0
    half = [None] * 4
    for b in range(2):
        half[b] = jnp.where(low, values[b], pltpu.roll(values[b + 2], 64, 1))
        half[b + 2] = jnp.where(low, pltpu.roll(values[b], 64, 1), values[b + 2])
    full = [None] * 4
    for j in (0, 2):
        full[j] = jnp.where(even, half[j], pltpu.roll(half[j + 1], 32, 1))
        full[j + 1] = jnp.where(even, pltpu.roll(half[j], 96, 1), half[j + 1])
    return full


def pack_rows(in_ref, lanes, tiles):
    upper = lax.broadcasted_iota(jnp.int32, (8, 128), 0) < 4
    for t1 in range(16):
        groups = [None] * 4
        for high in range(2):
            real = in_ref[0, t1, 8 * high : 8 * high + 8, lanes]
            imag = in_ref[1, t1, 8 * high : 8 * high + 8, lanes]
            groups[2 * high] = jnp.where(upper, real, pltpu.roll(imag, 4, 0))
            groups[2 * high + 1] = jnp.where(upper, pltpu.roll(real, 4, 0), imag)
        for j, tile in enumerate(swap_lanes(groups)):
            tiles[j, t1] = tile


def entry_of(bundles, z_first, mz, xy):
    return bundles[mz].at[xy] if z_first else bundles[0].at[xy, mz]


def in_bundles(z_first):
    shapes = [BUNDLE] * 4 if z_first else [(4,) + BUNDLE]
    return [jax.ShapeDtypeStruct(shape, jnp.float32) for shape in shapes]


def whole_blocks(shapes):
    def zeros(rank):
        return lambda i: (0,) * rank

    return [pl.BlockSpec(shape.shape, zeros(len(shape.shape))) for shape in shapes]


def pack_kernel(z_first, ids, in_ref, *refs):
    outs, tiles = refs[:-1], refs[-1]
    for mz in range(4):
        group = mz ^ (ids[0] // 4)
        pack_rows(in_ref, pl.ds(pl.multiple_of(group * 128, 128), 128), tiles)
        for xy in range(4):
            entry_of(outs, z_first, mz, xy)[...] = tiles[xy]


BUNDLE = (4, 16, 8, 128)


def pack(weights, ids, chunk, z_first):
    return pl.pallas_call(
        partial(pack_kernel, z_first),
        grid=(1,),
        in_specs=[
            pl.BlockSpec(memory_space=pltpu.SMEM),
            pl.BlockSpec((2, 16, 16, 512), lambda i: (0, 0, 0, chunk)),
        ],
        out_specs=whole_blocks(in_bundles(z_first)),
        out_shape=in_bundles(z_first),
        scratch_shapes=[pltpu.VMEM(BUNDLE, jnp.float32)],
        compiler_params=pltpu.CompilerParams(vmem_limit_bytes=VMEM_LIMIT),
        cost_estimate=pl.CostEstimate(flops=1000, bytes_accessed=1000, transcendentals=0),
        name="pack",
    )(ids, weights)


def regroup_kernel(z_first, *refs):
    count = 4 if z_first else 1
    outs = refs[-(5 - count) :]
    for mz in range(4):
        for xy in range(4):
            piece = entry_of(refs, z_first, mz, xy)[...]
            entry_of(outs, not z_first, mz, xy)[...] = piece


def regroup(bundles, z_first, after=()):
    in_vmem = pl.BlockSpec(memory_space=pltpu.VMEM)
    shapes = in_bundles(not z_first)
    return pl.pallas_call(
        partial(regroup_kernel, z_first),
        in_specs=[in_vmem] * len(bundles) + [pl.BlockSpec(memory_space=pl.ANY)] * len(after),
        out_specs=[in_vmem] * len(shapes),
        out_shape=shapes,
        compiler_params=pltpu.CompilerParams(vmem_limit_bytes=VMEM_LIMIT),
        cost_estimate=pl.CostEstimate(flops=1000, bytes_accessed=1000, transcendentals=0),
        name="regroup",
    )(*bundles, *after)


def cross_z(bundles):
    moved = [bundles[0]]
    for mask in range(1, 4):
        pairs = [(source, source ^ (4 * mask)) for source in range(PIECES)]
        moved.append(lax.ppermute(bundles[mask], ("bx", "by"), pairs))
    return moved


def cross_xy(bundles):
    groups = [[4 * z + xy for xy in range(4)] for z in range(4)]
    return [
        lax.all_to_all(bundles[0], ("bx", "by"), 0, 0, axis_index_groups=groups, tiled=True)
    ]


def merge_halves(out_ref, box, t1, low, high):
    upper = lax.broadcasted_iota(jnp.int32, (8, 128), 0) < 4
    out_ref[box, 0, t1] = jnp.where(upper, low, pltpu.roll(high, 4, 0))
    out_ref[box, 1, t1] = jnp.where(upper, pltpu.roll(low, 4, 0), high)


def join_kernel(z_first, ids, *refs):
    bundles, out_ref = refs[:4], refs[-1]
    for mz in range(4):
        for x in range(2):
            box = 2 * (mz ^ (ids[0] // 4)) + x
            for t1 in range(16):
                low = entry_of(bundles, z_first, mz, 2 * x)[t1]
                high = entry_of(bundles, z_first, mz, 2 * x + 1)[t1]
                merge_halves(out_ref, box, t1, low, high)


def join(received, ids, z_first, after=()):
    in_vmem = pl.BlockSpec(memory_space=pltpu.VMEM)
    return pl.pallas_call(
        partial(join_kernel, z_first),
        in_specs=[pl.BlockSpec(memory_space=pltpu.SMEM)]
        + [in_vmem] * len(received)
        + [pl.BlockSpec(memory_space=pl.ANY)] * len(after),
        out_specs=in_vmem,
        out_shape=jax.ShapeDtypeStruct((8, 2, 16, 8, 128), jnp.float32),
        compiler_params=pltpu.CompilerParams(vmem_limit_bytes=VMEM_LIMIT),
        cost_estimate=pl.CostEstimate(flops=1000, bytes_accessed=1000, transcendentals=0),
        name="join",
    )(ids, *received, *after)


def levels_kernel(
    chunk, z_first, ids, nodes, own, other, speeds, waves, lengths, last_one, last_two,
    last_lengths, first_table, second_table, *refs,
):
    outs = refs[:-6]
    boxes_a, boxes_b, sums, turned, mixed, last_phase = refs[-6:]
    row = (chunk * PIECES + ids[0]).astype(jnp.float32)
    core = ids[1]
    core_float = core.astype(jnp.float32)
    wave_two = waves[...]
    lane = lax.broadcasted_iota(jnp.int32, (8, 128), 1)
    along_two = ((lane % 32).astype(jnp.float32) + 0.5) * (1.0 / 32)
    second_phase = along_two * wave_two

    def first_point(level_index, low_code):
        span = 2.0 ** (level_index + 1)
        code = core_float * 2.0**level_index + low_code
        return (row * span + code + 0.5) * (1.0 / (32 * span))

    def speed_row(level_index, low_code):
        return jnp.broadcast_to(speeds[pl.ds(2**level_index - 1 + low_code, 1), :], (8, 128))

    def blend(slot, target, boxes):
        rows = sums[slot].astype(jnp.bfloat16)
        both = jnp.dot(first_table[...], rows, preferred_element_type=jnp.float32)
        total = both[:128] + both[128:]
        for n, box in enumerate(boxes):
            for part in range(2):
                column = 128 * (2 * n + part)
                target[box, part] = total[:, column : column + 128].reshape(16, 8, 128)

    def put(slot, first_row, column, real, imag):
        sums[slot, pl.ds(first_row, 8), 256 * column : 256 * column + 128] = real
        sums[slot, pl.ds(first_row, 8), 256 * column + 128 : 256 * column + 256] = imag

    def first_level(pair, slot):
        point = first_point(0, 0.0)
        speed = speed_row(0, 0)
        for n in range(2):
            box = 2 * pair + n
            for source, child in ((own, core), (other, 1 - core)):
                for t1 in range(16):
                    entry = (2 * box + child) * 16 + t1
                    phase = (point * nodes[entry] + second_phase) + speed * lengths[entry]
                    cosine, sine = turn(phase)
                    real = source[box, 0, t1]
                    imag = source[box, 1, t1]
                    first_row = pl.multiple_of(child * 128 + 8 * t1, 8)
                    put(slot, first_row, n, real * cosine + imag * sine, imag * cosine - real * sine)
        blend(slot, boxes_a, [2 * pair, 2 * pair + 1])

    def later_level(level_index, source, target, index, slot):
        low_bits = level_index - 1
        stride = 2**low_bits
        parent = index // stride
        low = index % stride
        code = jnp.int32(0)
        for bit in range(low_bits):
            code = code + low // 2**bit % 2 * 2 ** (low_bits - 1 - bit)
        before = first_point(level_index - 1, code.astype(jnp.float32))
        before_speed = speed_row(level_index - 1, code)
        points = [first_point(level_index, (2 * code + b).astype(jnp.float32)) for b in range(2)]
        point_speeds = [speed_row(level_index, 2 * code + b) for b in range(2)]
        first_box = parent * (2 * stride) + low
        for child in range(2):
            for t1 in range(16):
                entry = LEVEL_ROWS[level_index] + (2 * parent + child) * 16 + t1
                length = lengths[entry]
                wave = nodes[entry]
                real = source[first_box + child * stride, 0, t1]
                imag = source[first_box + child * stride, 1, t1]
                old = (before * wave + second_phase) + before_speed * length
                for b in range(2):
                    new = (points[b] * wave + second_phase) + point_speeds[b] * length
                    cosine, sine = turn(new - old)
                    first_row = child * 128 + 8 * t1
                    put(slot, first_row, b, real * cosine + imag * sine, imag * cosine - real * sine)
        blend(slot, target, [first_box, first_box + stride])

    def in_pairs(one):
        def step(half, carry):
            for slot in range(2):
                one(2 * half + slot, slot)
            return carry

        lax.fori_loop(0, 2, step, 0)

    in_pairs(first_level)
    in_pairs(partial(later_level, 1, boxes_a, boxes_b))
    in_pairs(partial(later_level, 2, boxes_b, boxes_a))
    in_pairs(partial(later_level, 3, boxes_a, boxes_b))

    fine_two = [((lane % 32).astype(jnp.float32) * 2.0 + (e + 0.5)) * (1.0 / 64) for e in range(2)]
    fine_phase = [fine_two[e] * wave_two for e in range(2)]

    def reversed_code(box):
        return box % 2 * 4 + box // 2 % 2 * 2 + box // 4

    def fine_speed(code, e):
        return jnp.broadcast_to(speeds[pl.ds(15 + 2 * code + e, 1), :], (8, 128))

    def rotate_box(box, carry):
        code = reversed_code(box)
        point = first_point(3, code.astype(jnp.float32))
        old_speed = speed_row(3, code)
        new_speeds = [fine_speed(code, e) for e in range(2)]
        for t1 in range(16):
            entry = LEVEL_ROWS[4] + t1
            length = lengths[entry]
            across = point * nodes[entry]
            real = boxes_b[box, 0, t1]
            imag = boxes_b[box, 1, t1]
            old = (across + second_phase) + old_speed * length
            for e in range(2):
                new = (across + fine_phase[e]) + new_speeds[e] * length
                cosine, sine = turn(new - old)
                first = pl.multiple_of((e * 256 + box * 32 + t1) * 8, 8)
                turned[pl.ds(first, 8), :] = real * cosine + imag * sine
                turned[pl.ds(first + 128, 8), :] = imag * cosine - real * sine
        return carry

    lax.fori_loop(0, 8, rotate_box, 0)

    for e in range(2):
        for a in range(4):
            last_phase[e, a] = fine_two[e] * last_two[a]

    total = None
    for j in range(4):
        rows = jnp.concatenate(
            [turned[pl.ds(2 * j + k, 512, stride=8), :] for k in range(2)], axis=1
        ).astype(jnp.bfloat16)
        for part in range(2):
            term = jnp.dot(rows, second_table[part, j], preferred_element_type=jnp.float32)
            total = term if total is None else total + term
    mixed[...] = total

    def finish_box(target, out):
        box, e = target // 2, target % 2
        code = reversed_code(box)
        point = first_point(3, code.astype(jnp.float32))
        speed = fine_speed(code, e)
        for high in range(2):
            across = point * last_one[high]
            first = pl.multiple_of(e * 256 + box * 32 + high * 8, 8)
            for a in range(4):
                phase = (across + last_phase[e, a]) + speed * last_lengths[high, a]
                cosine, sine = turn(phase)
                real = mixed[pl.ds(first, 8), 128 * a : 128 * a + 128]
                imag = mixed[pl.ds(first + 16, 8), 128 * a : 128 * a + 128]
                out[high * 4 + a] = real * cosine - imag * sine
                out[8 + high * 4 + a] = real * sine + imag * cosine

    def finish_row(xy, carry):
        for mz in range(4):
            target = 4 * (mz ^ (ids[0] // 4)) + xy
            finish_box(target, entry_of(outs, z_first, mz, xy))
        return carry

    lax.fori_loop(0, 4, finish_row, 0)


def levels(chunk, z_first, ids, own, other, speeds):
    nodes, waves, lengths = node_tables()
    last_one, last_two, last_lengths = final_tables()
    tables = (waves, lengths, last_one, last_two, last_lengths, first_weights(), second_weights())
    in_vmem = pl.BlockSpec(memory_space=pltpu.VMEM)
    in_smem = pl.BlockSpec(memory_space=pltpu.SMEM)
    return pl.pallas_call(
        partial(levels_kernel, chunk, z_first),
        in_specs=[in_smem, in_smem] + [in_vmem] * 10,
        out_specs=[in_vmem] * len(in_bundles(z_first)),
        out_shape=in_bundles(z_first),
        scratch_shapes=[
            pltpu.VMEM((8, 2, 16, 8, 128), jnp.float32),
            pltpu.VMEM((8, 2, 16, 8, 128), jnp.float32),
            pltpu.VMEM((2, 256, 512), jnp.float32),
            pltpu.VMEM((4096, 128), jnp.float32),
            pltpu.VMEM((512, 512), jnp.float32),
            pltpu.VMEM((2, 4, 8, 128), jnp.float32),
        ],
        compiler_params=pltpu.CompilerParams(vmem_limit_bytes=VMEM_LIMIT),
        cost_estimate=pl.CostEstimate(flops=1000, bytes_accessed=1000, transcendentals=0),
        name="levels",
    )(ids, jnp.asarray(nodes), own, other, speeds, *[jnp.asarray(table) for table in tables])


def unpack_rows(tiles, rows, out_ref, lanes):
    for part in range(2):
        for high in range(2):
            block = part * 2 + high
            for a in range(4):
                values = [tiles[j, part * 8 + high * 4 + a] for j in range(4)]
                for b, tile in enumerate(swap_lanes(values)):
                    t2 = 4 * b + a
                    rows[block, 8 * t2 : 8 * t2 + 8, :] = tile
            for t1 in range(8):
                out_ref[part, high * 8 + t1, :, lanes] = rows[block, pl.ds(t1, 16, stride=8), :]


def unpack_kernel(z_first, ids, *refs):
    bundles, out_ref, tiles, rows = refs[:4], refs[-3], refs[-2], refs[-1]
    me = ids[0]
    for mz in range(4):
        group = mz ^ (me // 4)
        for xy in range(4):
            tiles[xy] = entry_of(bundles, z_first, mz, xy)[...]
        unpack_rows(tiles, rows, out_ref, pl.ds(pl.multiple_of(group * 128, 128), 128))


def unpack(received, ids, chunk, z_first, earlier):
    operands = [ids, *received]
    in_specs = [pl.BlockSpec(memory_space=pltpu.SMEM)]
    in_specs += whole_blocks(in_bundles(z_first))
    aliases = {}
    if earlier is not None:
        aliases = {len(operands): 0}
        operands.append(earlier)
        in_specs.append(pl.BlockSpec(memory_space=pl.ANY))
    return pl.pallas_call(
        partial(unpack_kernel, z_first),
        grid=(1,),
        in_specs=in_specs,
        out_specs=pl.BlockSpec((2, 16, 16, 512), lambda i: (0, 0, 0, chunk)),
        out_shape=jax.ShapeDtypeStruct((2, 16, 16, 1024), jnp.float32),
        scratch_shapes=[pltpu.VMEM(BUNDLE, jnp.float32), pltpu.VMEM((4, 128, 128), jnp.float32)],
        input_output_aliases=aliases,
        compiler_params=pltpu.CompilerParams(vmem_limit_bytes=VMEM_LIMIT),
        cost_estimate=pl.CostEstimate(flops=1000, bytes_accessed=1000, transcendentals=0),
        name="unpack",
    )(*operands)


def speed_tables(speed_modes, core):
    numerators, spans = [], []
    for level_index in range(4):
        for code in range(2**level_index):
            numerators.append(core * 2**level_index + code)
            spans.append(2 ** (level_index + 1))
    for code in range(8):
        for e in range(2):
            numerators.append(core * 8 + code)
            spans.append(16)
    codes = jnp.stack(numerators).astype(jnp.float32)
    spans = jnp.asarray(np.array(spans), jnp.float32)
    me = lax.axis_index("bx") * 2 + lax.axis_index("by")
    rows = (jnp.arange(CHUNKS) * PIECES + me).astype(jnp.float32)
    target_one = (rows[:, None] * spans + codes + 0.5) / (TGT * spans)
    columns = jnp.arange(32).astype(jnp.float32)
    coarse = jnp.broadcast_to((columns + 0.5) / TGT, (15, 32))
    fine = jnp.stack([(2 * columns + e + 0.5) / (2 * TGT) for e in range(2)])
    target_two = jnp.concatenate([coarse, jnp.tile(fine, (8, 1))])
    target_one = jnp.broadcast_to(target_one[:, :, None], (CHUNKS, 31, 32))
    target_two = jnp.broadcast_to(target_two[None], (CHUNKS, 31, 32))
    speed = speed_of(speed_modes, target_one.reshape(-1), target_two.reshape(-1))
    return jnp.tile(speed.reshape(CHUNKS, 31, 32), (1, 1, 4))


def on_device_dealt(weights, speed_modes):
    local = weights.reshape(weights.shape[2:])
    core = lax.axis_index("cores")
    me = lax.axis_index("bx") * 2 + lax.axis_index("by")
    ids = jnp.stack([me, core]).astype(jnp.int32)
    speeds = speed_tables(speed_modes, core)

    z_crossed = cross_z(pack(local, ids, 0, True))
    xy_crossed = cross_xy(pack(local, ids, 1, False))
    grouped = regroup(xy_crossed, False, z_crossed[1:])
    first = cross_xy(regroup(z_crossed, True, grouped[:1]))
    second = cross_z(grouped)

    own = join(first, ids, False)
    result = levels(0, True, ids, own, partner_2(own, "cores", 0), speeds[0])
    z_crossed = cross_z(result)

    own = join(second, ids, True, result[:1])
    result = levels(1, False, ids, own, partner_2(own, "cores", 0), speeds[1])
    xy_crossed = cross_xy(result)

    grouped = regroup(xy_crossed, False, z_crossed[1:])
    first = cross_xy(regroup(z_crossed, True, grouped[:1]))
    second = cross_z(grouped)
    out = unpack(first, ids, 0, False, None)
    out = unpack(second, ids, 1, True, out)
    return out.reshape(weights.shape)


def solution(mesh):
    sizes = dict(mesh.shape)
    spec = P(("bx", "cores"), "by", None, None, None, None)
    dealt = (sizes["bx"], sizes["by"], sizes["cores"]) == (8, 2, 2)

    def whole(weights, speed_modes):
        fits = dealt and weights.shape[2:] == (2, 16, 16, 1024)
        return jax.shard_map(
            on_device_dealt if fits else on_device,
            mesh=mesh,
            in_specs=(spec, P()),
            out_specs=spec,
            check_vma=False,
        )(weights, speed_modes)

    return whole
```

```python
from functools import partial
import math

import jax
import jax.numpy as jnp
import ml_dtypes
import numpy as np
from jax import lax
from jax.experimental import pallas as pl
from jax.experimental.pallas import tpu as pltpu
from jax.sharding import PartitionSpec as P

N = 8192
TGT = 32


def partner_2(value, axis, apart):
    mask = 2**apart
    pairs = [(source, source ^ mask) for source in range(lax.axis_size(axis))]
    return lax.ppermute(value, axis, pairs)


def cheb_nodes(degree):
    return np.cos(np.pi * (2 * np.arange(degree) + 1) / (2 * degree))


def lagrange_table(degree):
    points = cheb_nodes(degree)
    result = np.ones((degree, 2 * degree))
    for child_side in range(2):
        inside = (points + 2 * child_side - 1) / 2
        for node_row in range(degree):
            for node_other in range(degree):
                if node_other != node_row:
                    result[node_row, child_side * degree : (child_side + 1) * degree] *= (
                        inside - points[node_other]
                    ) / (points[node_row] - points[node_other])
    return result


def speed_of(speed_modes, target_one, target_two):
    mode_count = speed_modes.shape[0]
    frequencies = jnp.arange(mode_count).astype(jnp.float32) * math.pi
    along_one = jnp.cos(frequencies[:, None] * target_one[None, :])
    along_two = jnp.cos(frequencies[:, None] * target_two[None, :])
    blended = jnp.dot(
        speed_modes, along_two, preferred_element_type=jnp.float32, precision=lax.Precision.HIGHEST
    )
    return 1.0 + jnp.sum(blended * along_one, axis=0)


def rotation(target_one, target_two, speed_value, wave_one, wave_two):
    phase = (
        target_one * wave_one
        + target_two * wave_two
        + speed_value * jnp.sqrt(wave_one * wave_one + wave_two * wave_two)
    )
    phase = phase - jnp.floor(phase)
    angle = 2.0 * math.pi * phase
    return (jnp.cos(angle), jnp.sin(angle))


def node_phase(layout, speed_value, center, half_width, degree):
    target_one, target_two, merge_dim, centers, child_half, other_center, other_half = layout
    points = jnp.asarray(cheb_nodes(degree), jnp.float32)
    merged = center[None, :] + half_width * points[:, None]
    across = other_center[None, :] + other_half * points[:, None]
    if merge_dim == 0:
        return rotation(target_one, target_two, speed_value, merged[:, None, :], across[None, :, :])
    return rotation(target_one, target_two, speed_value, across[:, None, :], merged[None, :, :])


def merge_children(child_low, child_high, layout, speed_modes):
    target_one, target_two, merge_dim, centers, child_half, other_center, other_half = layout
    degree = child_low.shape[1]
    speed_value = speed_of(speed_modes, target_one, target_two)
    lagrange = jnp.asarray(lagrange_table(degree), jnp.float32)
    pieces = []
    for child, center in ((child_low, centers[0]), (child_high, centers[1])):
        cosine, sine_part = node_phase(layout, speed_value, center, child_half, degree)
        real_part = child[0] * cosine + child[1] * sine_part
        imag_part = child[1] * cosine - child[0] * sine_part
        pieces.append(jnp.stack([real_part, imag_part]))
    stacked = jnp.concatenate(pieces, axis=1 + merge_dim)
    if merge_dim == 0:
        blended = jnp.einsum("ij,rjks->riks", lagrange, stacked, precision=lax.Precision.HIGHEST)
    else:
        blended = jnp.einsum("kj,rijs->riks", lagrange, stacked, precision=lax.Precision.HIGHEST)
    cosine, sine_part = node_phase(layout, speed_value, centers[2], 2.0 * child_half, degree)
    return jnp.stack(
        [blended[0] * cosine - blended[1] * sine_part, blended[0] * sine_part + blended[1] * cosine]
    )


def reversed_bits(box_code, bit_count):
    result = jnp.zeros_like(box_code)
    for bit_place in range(bit_count):
        result = result + box_code // 2**bit_place % 2 * 2 ** (bit_count - 1 - bit_place)
    return result


def x_layout(level_index, box_code, targets, y_box, geometry):
    extent, side_count, src_x, src_y = geometry
    span_size = 2 ** (level_index + 1)
    row_index = targets // side_count * span_size + reversed_bits(box_code, level_index + 1)
    target_one = (row_index.astype(jnp.float32) + 0.5) / (side_count * span_size)
    target_two = ((targets % side_count).astype(jnp.float32) + 0.5) / side_count
    parent = (box_code // span_size).astype(jnp.float32)
    child_width = extent * 2**level_index / src_x
    low_center = -extent / 2 + (2.0 * parent + 0.5) * child_width
    high_center = low_center + child_width
    parent_center = -extent / 2 + (parent + 0.5) * (2.0 * child_width)
    other_center = jnp.zeros_like(target_one) + (
        -extent / 2 + (jnp.asarray(y_box).astype(jnp.float32) + 0.5) * (extent / src_y)
    )
    return (
        target_one,
        target_two,
        0,
        (low_center, high_center, parent_center),
        child_width / 2,
        other_center,
        extent / (2 * src_y),
    )


def y_layout(level_index, box_code, targets, x_code, x_bits, geometry):
    extent, side_count, src_x, src_y = geometry
    span_size = 2 ** (level_index + 1)
    col_index = targets % side_count * span_size + reversed_bits(box_code, level_index + 1)
    target_two = (col_index.astype(jnp.float32) + 0.5) / (side_count * span_size)
    row_index = targets // side_count * src_x + reversed_bits(x_code, x_bits)
    target_one = (row_index.astype(jnp.float32) + 0.5) / (side_count * src_x)
    parent = (box_code // span_size).astype(jnp.float32)
    child_width = extent * 2**level_index / src_y
    low_center = -extent / 2 + (2.0 * parent + 0.5) * child_width
    high_center = low_center + child_width
    parent_center = -extent / 2 + (parent + 0.5) * (2.0 * child_width)
    other_center = jnp.zeros_like(target_one)
    return (
        target_one,
        target_two,
        1,
        (low_center, high_center, parent_center),
        child_width / 2,
        other_center,
        extent / 2,
    )


def pair_level(current, partner, level_index, box_code, targets, layout_fn, speed_modes):
    own_bit = box_code // 2**level_index % 2
    child_low = jnp.where(own_bit == 0, current, partner)
    child_high = jnp.where(own_bit == 0, partner, current)
    box_codes = jnp.zeros_like(targets) + box_code
    return merge_children(
        child_low, child_high, layout_fn(level_index, box_codes, targets), speed_modes
    )


def on_device(weights, speed_modes):
    current = weights.reshape(weights.shape[2:])
    pair_count = current.shape[3]
    core_count = lax.axis_size("cores")
    src_x = lax.axis_size("bx") * core_count
    src_y = lax.axis_size("by")
    x_bits = src_x.bit_length() - 1
    y_bits = src_y.bit_length() - 1
    x_code = lax.axis_index("bx") * core_count + lax.axis_index("cores")
    y_box = lax.axis_index("by")
    geometry = (float(N), TGT, src_x, src_y)
    targets = jnp.arange(pair_count, dtype=jnp.int32)
    first_layout = partial(x_layout, y_box=y_box, geometry=geometry)
    second_layout = partial(y_layout, x_code=x_code, x_bits=x_bits, geometry=geometry)
    for level_index in range(x_bits):
        if level_index == 0:
            partner = partner_2(current, "cores", 0)
        else:
            partner = partner_2(current, "bx", level_index - 1)
        current = pair_level(
            current, partner, level_index, x_code, targets, first_layout, speed_modes
        )
    for level_index in range(y_bits):
        partner = partner_2(current, "by", level_index)
        current = pair_level(
            current, partner, level_index, y_box, targets, second_layout, speed_modes
        )
    return current.reshape(weights.shape)


SIN_HALF = (4.442879586386342, -7.3078180422392816, 3.597788667381583, -0.7912380409231197)
COS_HALF = (
    1.4142134965636117,
    -6.978850988059019,
    5.739461167077472,
    -1.883562964211867,
    0.3106981455985473,
)
CHUNKS = 2
PIECES = 16
LEVEL_ROWS = (0, 256, 384, 448, 480)
VMEM_LIMIT = 48 * 2**20


def node_tables():
    points = cheb_nodes(16).astype(np.float32)
    nodes = []
    for level_index in range(5):
        width = np.float32(N * 2**level_index / 16)
        for box in range(16 >> level_index):
            center = np.float32(-N / 2 + (box + 0.5) * width)
            nodes.append(center + (width / 2) * points)
    nodes = np.concatenate(nodes).astype(np.float32)
    sub = np.arange(8)
    lane = np.arange(128)
    half = (sub // 4)[:, None] + 0 * lane[None, :]
    second = (lane // 32 * 4)[None, :] + (sub % 4)[:, None]
    wave_two = (-N / 2 + (half + 0.5) * (N / 2)).astype(np.float32) + np.float32(N / 4) * points[second]
    wave_two = wave_two.astype(np.float32)
    lengths = np.sqrt(nodes[:, None, None] * nodes[:, None, None] + wave_two * wave_two)
    return nodes, wave_two, lengths.astype(np.float32)


def final_tables():
    points = cheb_nodes(16).astype(np.float32) * np.float32(N / 2)
    lane = np.arange(128)
    one = np.broadcast_to(points.reshape(2, 8, 1), (2, 8, 128)).astype(np.float32)
    two = np.stack([np.broadcast_to(points[lane // 32 * 4 + a], (8, 128)) for a in range(4)])
    two = two.astype(np.float32)
    lengths = np.sqrt((one * one)[:, None] + (two * two)[None, :]).astype(np.float32)
    return np.array(one), two, lengths


def in_two_parts(table):
    high = table.astype(ml_dtypes.bfloat16)
    low = (table - high.astype(np.float32)).astype(ml_dtypes.bfloat16)
    return high, low


def first_weights():
    table = lagrange_table(16).astype(np.float32)
    high, low = in_two_parts(np.kron(table, np.eye(8, dtype=np.float32)))
    return np.concatenate([high, low])


def second_weights():
    table = lagrange_table(16)
    result = np.zeros((8, 4, 32, 4, 4, 32), np.float32)
    same = np.eye(32, dtype=np.float32)
    for half in range(2):
        for a in range(4):
            for b in range(4):
                for out_a in range(4):
                    for out_b in range(4):
                        weight = table[4 * out_b + out_a, half * 16 + 4 * b + a]
                        result[half * 4 + a, b, :, out_a, out_b, :] = np.float32(weight) * same
    return np.stack(in_two_parts(result.reshape(4, 256, 512)))


def turn(phase):
    part = phase - jnp.round(phase)
    square = part * part
    sine = SIN_HALF[3]
    for coefficient in SIN_HALF[2::-1]:
        sine = sine * square + coefficient
    sine = sine * part
    cosine = COS_HALF[4]
    for coefficient in COS_HALF[3::-1]:
        cosine = cosine * square + coefficient
    return 1.0 - sine * sine, sine * cosine


def swap_lanes(values):
    lane = lax.broadcasted_iota(jnp.int32, (8, 128), 1)
    low = lane < 64
    even = lane // 32 % 2 == 0
    half = [None] * 4
    for b in range(2):
        half[b] = jnp.where(low, values[b], pltpu.roll(values[b + 2], 64, 1))
        half[b + 2] = jnp.where(low, pltpu.roll(values[b], 64, 1), values[b + 2])
    full = [None] * 4
    for j in (0, 2):
        full[j] = jnp.where(even, half[j], pltpu.roll(half[j + 1], 32, 1))
        full[j + 1] = jnp.where(even, pltpu.roll(half[j], 96, 1), half[j + 1])
    return full


def pack_rows(in_ref, lanes, tiles):
    upper = lax.broadcasted_iota(jnp.int32, (8, 128), 0) < 4
    for t1 in range(16):
        groups = [None] * 4
        for high in range(2):
            real = in_ref[0, t1, 8 * high : 8 * high + 8, lanes]
            imag = in_ref[1, t1, 8 * high : 8 * high + 8, lanes]
            groups[2 * high] = jnp.where(upper, real, pltpu.roll(imag, 4, 0))
            groups[2 * high + 1] = jnp.where(upper, pltpu.roll(real, 4, 0), imag)
        for j, tile in enumerate(swap_lanes(groups)):
            tiles[j, t1] = tile


def pack_kernel(in_ref, out_ref):
    def step(group, carry):
        lanes = pl.ds(pl.multiple_of(group * 128, 128), 128)
        pack_rows(in_ref, lanes, out_ref.at[pl.ds(4 * group, 4)])
        return carry

    lax.fori_loop(0, 4, step, 0)


def pack(weights, chunk):
    return pl.pallas_call(
        pack_kernel,
        grid=(1,),
        in_specs=[pl.BlockSpec((2, 16, 16, 512), lambda i: (0, 0, 0, chunk))],
        out_specs=pl.BlockSpec((PIECES, 16, 8, 128), lambda i: (0, 0, 0, 0)),
        out_shape=jax.ShapeDtypeStruct((PIECES, 16, 8, 128), jnp.float32),
        compiler_params=pltpu.CompilerParams(vmem_limit_bytes=VMEM_LIMIT),
        cost_estimate=pl.CostEstimate(flops=10**6, bytes_accessed=2**21, transcendentals=0),
        name="pack",
    )(weights)


def pack_masks_kernel(ids, in_ref, *refs):
    outs, tiles = refs[:4], refs[4]
    me = ids[0]

    def step(mz, carry):
        group = mz ^ (me // 4)
        pack_rows(in_ref, pl.ds(pl.multiple_of(group * 128, 128), 128), tiles)
        for mxy in range(4):
            outs[mxy][mz] = tiles[mxy ^ (me % 4)]
        return carry

    lax.fori_loop(0, 4, step, 0)


BUNDLE = (4, 16, 8, 128)


def pack_masks(weights, ids, chunk):
    return pl.pallas_call(
        pack_masks_kernel,
        grid=(1,),
        in_specs=[
            pl.BlockSpec(memory_space=pltpu.SMEM),
            pl.BlockSpec((2, 16, 16, 512), lambda i: (0, 0, 0, chunk)),
        ],
        out_specs=[pl.BlockSpec(BUNDLE, lambda i: (0, 0, 0, 0))] * 4,
        out_shape=[jax.ShapeDtypeStruct(BUNDLE, jnp.float32)] * 4,
        scratch_shapes=[pltpu.VMEM(BUNDLE, jnp.float32)],
        compiler_params=pltpu.CompilerParams(vmem_limit_bytes=VMEM_LIMIT),
        cost_estimate=pl.CostEstimate(flops=10**6, bytes_accessed=2**21, transcendentals=0),
        name="pack_masks",
    )(ids, weights)


def regroup_kernel(*refs):
    for first in range(4):
        for second in range(4):
            refs[4 + second][first] = refs[first][second]


def regroup(bundles):
    in_vmem = pl.BlockSpec(memory_space=pltpu.VMEM)
    return pl.pallas_call(
        regroup_kernel,
        in_specs=[in_vmem] * 4,
        out_specs=[in_vmem] * 4,
        out_shape=[jax.ShapeDtypeStruct(BUNDLE, jnp.float32)] * 4,
        compiler_params=pltpu.CompilerParams(vmem_limit_bytes=VMEM_LIMIT),
        cost_estimate=pl.CostEstimate(flops=10**5, bytes_accessed=2**21, transcendentals=0),
        name="regroup",
    )(*bundles)


def exchange(bundles, unit):
    moved = [bundles[0]]
    for mask in range(1, 4):
        pairs = [(source, source ^ (mask * unit)) for source in range(PIECES)]
        moved.append(lax.ppermute(bundles[mask], ("bx", "by"), pairs))
    return moved


def merge_halves(out_ref, box, t1, low, high):
    upper = lax.broadcasted_iota(jnp.int32, (8, 128), 0) < 4
    out_ref[box, 0, t1] = jnp.where(upper, low, pltpu.roll(high, 4, 0))
    out_ref[box, 1, t1] = jnp.where(upper, pltpu.roll(low, 4, 0), high)


def join_kernel(in_ref, *refs):
    out_ref = refs[-1]

    def step(box, carry):
        for t1 in range(16):
            merge_halves(out_ref, box, t1, in_ref[2 * box, t1], in_ref[2 * box + 1, t1])
        return carry

    lax.fori_loop(0, 8, step, 0)


def join_masks_kernel(ids, *refs):
    bundles, out_ref = refs[:4], refs[-1]
    me = ids[0]
    is_low = jnp.broadcast_to(me % 2, (8, 128)) == 0
    for mz in range(4):
        for mx in range(2):
            box = (2 * mz + mx) ^ (me // 2)
            for t1 in range(16):
                mine = bundles[mz][2 * mx, t1]
                partner = bundles[mz][2 * mx + 1, t1]
                low = jnp.where(is_low, mine, partner)
                high = jnp.where(is_low, partner, mine)
                merge_halves(out_ref, box, t1, low, high)


def join(received, ids=None, after=()):
    in_vmem = pl.BlockSpec(memory_space=pltpu.VMEM)
    if ids is None:
        kernel, operands, in_specs = join_kernel, [received], [in_vmem]
    else:
        kernel, operands = join_masks_kernel, [ids, *received]
        in_specs = [pl.BlockSpec(memory_space=pltpu.SMEM)] + [in_vmem] * 4
    return pl.pallas_call(
        kernel,
        in_specs=in_specs + [pl.BlockSpec(memory_space=pl.ANY)] * len(after),
        out_specs=in_vmem,
        out_shape=jax.ShapeDtypeStruct((8, 2, 16, 8, 128), jnp.float32),
        compiler_params=pltpu.CompilerParams(vmem_limit_bytes=VMEM_LIMIT),
        cost_estimate=pl.CostEstimate(flops=1000, bytes_accessed=1000, transcendentals=0),
        name="join",
    )(*operands, *after)


def levels_kernel(
    chunk, ids, nodes, own, other, speeds, waves, lengths, last_one, last_two,
    last_lengths, first_table, second_table, *refs,
):
    outs = refs[0]
    boxes_a, boxes_b, sums, turned, mixed, last_phase = refs[-6:]
    row = (chunk * PIECES + ids[0]).astype(jnp.float32)
    core = ids[1]
    core_float = core.astype(jnp.float32)
    wave_two = waves[...]
    lane = lax.broadcasted_iota(jnp.int32, (8, 128), 1)
    along_two = ((lane % 32).astype(jnp.float32) + 0.5) * (1.0 / 32)
    second_phase = along_two * wave_two

    def first_point(level_index, low_code):
        span = 2.0 ** (level_index + 1)
        code = core_float * 2.0**level_index + low_code
        return (row * span + code + 0.5) * (1.0 / (32 * span))

    def speed_row(level_index, low_code):
        return jnp.broadcast_to(speeds[pl.ds(2**level_index - 1 + low_code, 1), :], (8, 128))

    def blend(slot, target, boxes):
        rows = sums[slot].astype(jnp.bfloat16)
        both = jnp.dot(first_table[...], rows, preferred_element_type=jnp.float32)
        total = both[:128] + both[128:]
        for n, box in enumerate(boxes):
            for part in range(2):
                column = 128 * (2 * n + part)
                target[box, part] = total[:, column : column + 128].reshape(16, 8, 128)

    def put(slot, first_row, column, real, imag):
        sums[slot, pl.ds(first_row, 8), 256 * column : 256 * column + 128] = real
        sums[slot, pl.ds(first_row, 8), 256 * column + 128 : 256 * column + 256] = imag

    def first_level(pair, slot):
        point = first_point(0, 0.0)
        speed = speed_row(0, 0)
        for n in range(2):
            box = 2 * pair + n
            for source, child in ((own, core), (other, 1 - core)):
                for t1 in range(16):
                    entry = (2 * box + child) * 16 + t1
                    phase = (point * nodes[entry] + second_phase) + speed * lengths[entry]
                    cosine, sine = turn(phase)
                    real = source[box, 0, t1]
                    imag = source[box, 1, t1]
                    first_row = pl.multiple_of(child * 128 + 8 * t1, 8)
                    put(slot, first_row, n, real * cosine + imag * sine, imag * cosine - real * sine)
        blend(slot, boxes_a, [2 * pair, 2 * pair + 1])

    def later_level(level_index, source, target, index, slot):
        low_bits = level_index - 1
        stride = 2**low_bits
        parent = index // stride
        low = index % stride
        code = jnp.int32(0)
        for bit in range(low_bits):
            code = code + low // 2**bit % 2 * 2 ** (low_bits - 1 - bit)
        before = first_point(level_index - 1, code.astype(jnp.float32))
        before_speed = speed_row(level_index - 1, code)
        points = [first_point(level_index, (2 * code + b).astype(jnp.float32)) for b in range(2)]
        point_speeds = [speed_row(level_index, 2 * code + b) for b in range(2)]
        first_box = parent * (2 * stride) + low
        for child in range(2):
            for t1 in range(16):
                entry = LEVEL_ROWS[level_index] + (2 * parent + child) * 16 + t1
                length = lengths[entry]
                wave = nodes[entry]
                real = source[first_box + child * stride, 0, t1]
                imag = source[first_box + child * stride, 1, t1]
                old = (before * wave + second_phase) + before_speed * length
                for b in range(2):
                    new = (points[b] * wave + second_phase) + point_speeds[b] * length
                    cosine, sine = turn(new - old)
                    first_row = child * 128 + 8 * t1
                    put(slot, first_row, b, real * cosine + imag * sine, imag * cosine - real * sine)
        blend(slot, target, [first_box, first_box + stride])

    def in_pairs(one):
        def step(half, carry):
            for slot in range(2):
                one(2 * half + slot, slot)
            return carry

        lax.fori_loop(0, 2, step, 0)

    in_pairs(first_level)
    in_pairs(partial(later_level, 1, boxes_a, boxes_b))
    in_pairs(partial(later_level, 2, boxes_b, boxes_a))
    in_pairs(partial(later_level, 3, boxes_a, boxes_b))

    fine_two = [((lane % 32).astype(jnp.float32) * 2.0 + (e + 0.5)) * (1.0 / 64) for e in range(2)]
    fine_phase = [fine_two[e] * wave_two for e in range(2)]

    def reversed_code(box):
        return box % 2 * 4 + box // 2 % 2 * 2 + box // 4

    def fine_speed(code, e):
        return jnp.broadcast_to(speeds[pl.ds(15 + 2 * code + e, 1), :], (8, 128))

    def rotate_box(box, carry):
        code = reversed_code(box)
        point = first_point(3, code.astype(jnp.float32))
        old_speed = speed_row(3, code)
        new_speeds = [fine_speed(code, e) for e in range(2)]
        for t1 in range(16):
            entry = LEVEL_ROWS[4] + t1
            length = lengths[entry]
            across = point * nodes[entry]
            real = boxes_b[box, 0, t1]
            imag = boxes_b[box, 1, t1]
            old = (across + second_phase) + old_speed * length
            for e in range(2):
                new = (across + fine_phase[e]) + new_speeds[e] * length
                cosine, sine = turn(new - old)
                first = pl.multiple_of((e * 256 + box * 32 + t1) * 8, 8)
                turned[pl.ds(first, 8), :] = real * cosine + imag * sine
                turned[pl.ds(first + 128, 8), :] = imag * cosine - real * sine
        return carry

    lax.fori_loop(0, 8, rotate_box, 0)

    for e in range(2):
        for a in range(4):
            last_phase[e, a] = fine_two[e] * last_two[a]

    total = None
    for j in range(4):
        rows = jnp.concatenate(
            [turned[pl.ds(2 * j + k, 512, stride=8), :] for k in range(2)], axis=1
        ).astype(jnp.bfloat16)
        for part in range(2):
            term = jnp.dot(rows, second_table[part, j], preferred_element_type=jnp.float32)
            total = term if total is None else total + term
    mixed[...] = total

    def finish_box(target, out):
        box, e = target // 2, target % 2
        code = reversed_code(box)
        point = first_point(3, code.astype(jnp.float32))
        speed = fine_speed(code, e)
        for high in range(2):
            across = point * last_one[high]
            first = pl.multiple_of(e * 256 + box * 32 + high * 8, 8)
            for a in range(4):
                phase = (across + last_phase[e, a]) + speed * last_lengths[high, a]
                cosine, sine = turn(phase)
                real = mixed[pl.ds(first, 8), 128 * a : 128 * a + 128]
                imag = mixed[pl.ds(first + 16, 8), 128 * a : 128 * a + 128]
                out[high * 4 + a] = real * cosine - imag * sine
                out[8 + high * 4 + a] = real * sine + imag * cosine

    def finish_row(major, carry):
        for minor in range(4):
            finish_box(4 * major + minor, outs.at[4 * major + minor])
        return carry

    lax.fori_loop(0, 4, finish_row, 0)


def levels(chunk, ids, own, other, speeds):
    nodes, waves, lengths = node_tables()
    last_one, last_two, last_lengths = final_tables()
    tables = (waves, lengths, last_one, last_two, last_lengths, first_weights(), second_weights())
    in_vmem = pl.BlockSpec(memory_space=pltpu.VMEM)
    in_smem = pl.BlockSpec(memory_space=pltpu.SMEM)
    return pl.pallas_call(
        partial(levels_kernel, chunk),
        in_specs=[in_smem, in_smem] + [in_vmem] * 10,
        out_specs=in_vmem,
        out_shape=jax.ShapeDtypeStruct((PIECES, 16, 8, 128), jnp.float32),
        scratch_shapes=[
            pltpu.VMEM((8, 2, 16, 8, 128), jnp.float32),
            pltpu.VMEM((8, 2, 16, 8, 128), jnp.float32),
            pltpu.VMEM((2, 256, 512), jnp.float32),
            pltpu.VMEM((4096, 128), jnp.float32),
            pltpu.VMEM((512, 512), jnp.float32),
            pltpu.VMEM((2, 4, 8, 128), jnp.float32),
        ],
        compiler_params=pltpu.CompilerParams(vmem_limit_bytes=VMEM_LIMIT),
        cost_estimate=pl.CostEstimate(
            flops=1000, bytes_accessed=4 * 10**8 if chunk else 1000, transcendentals=0
        ),
        name="levels",
    )(ids, jnp.asarray(nodes), own, other, speeds, *[jnp.asarray(table) for table in tables])


def unpack_rows(tiles, rows, out_ref, lanes):
    for part in range(2):
        for high in range(2):
            block = part * 2 + high
            for a in range(4):
                values = [tiles[j, part * 8 + high * 4 + a] for j in range(4)]
                for b, tile in enumerate(swap_lanes(values)):
                    t2 = 4 * b + a
                    rows[block, 8 * t2 : 8 * t2 + 8, :] = tile
            for t1 in range(8):
                out_ref[part, high * 8 + t1, :, lanes] = rows[block, pl.ds(t1, 16, stride=8), :]


def unpack_kernel(*refs):
    unpack_rows(refs[0], refs[-1], refs[-2], slice(None))


def unpack(received, chunk, earlier):
    operands = [received]
    in_specs = [pl.BlockSpec((4, 16, 8, 128), lambda i: (i, 0, 0, 0))]
    aliases = {}
    if earlier is not None:
        aliases = {1: 0}
        operands.append(earlier)
        in_specs.append(pl.BlockSpec(memory_space=pl.ANY))
    return pl.pallas_call(
        unpack_kernel,
        grid=(4,),
        in_specs=in_specs,
        out_specs=pl.BlockSpec((2, 16, 16, 128), lambda i: (0, 0, 0, 4 * chunk + i)),
        out_shape=jax.ShapeDtypeStruct((2, 16, 16, 1024), jnp.float32),
        scratch_shapes=[pltpu.VMEM((4, 128, 128), jnp.float32)],
        input_output_aliases=aliases,
        compiler_params=pltpu.CompilerParams(vmem_limit_bytes=VMEM_LIMIT),
        cost_estimate=pl.CostEstimate(flops=10**6, bytes_accessed=2**21, transcendentals=0),
        name="unpack",
    )(*operands)


def speed_tables(speed_modes, core):
    numerators, spans = [], []
    for level_index in range(4):
        for code in range(2**level_index):
            numerators.append(core * 2**level_index + code)
            spans.append(2 ** (level_index + 1))
    for code in range(8):
        for e in range(2):
            numerators.append(core * 8 + code)
            spans.append(16)
    codes = jnp.stack(numerators).astype(jnp.float32)
    spans = jnp.asarray(np.array(spans), jnp.float32)
    me = lax.axis_index("bx") * 2 + lax.axis_index("by")
    rows = (jnp.arange(CHUNKS) * PIECES + me).astype(jnp.float32)
    target_one = (rows[:, None] * spans + codes + 0.5) / (TGT * spans)
    columns = jnp.arange(32).astype(jnp.float32)
    coarse = jnp.broadcast_to((columns + 0.5) / TGT, (15, 32))
    fine = jnp.stack([(2 * columns + e + 0.5) / (2 * TGT) for e in range(2)])
    target_two = jnp.concatenate([coarse, jnp.tile(fine, (8, 1))])
    target_one = jnp.broadcast_to(target_one[:, :, None], (CHUNKS, 31, 32))
    target_two = jnp.broadcast_to(target_two[None], (CHUNKS, 31, 32))
    speed = speed_of(speed_modes, target_one.reshape(-1), target_two.reshape(-1))
    return jnp.tile(speed.reshape(CHUNKS, 31, 32), (1, 1, 4))


def on_device_dealt(weights, speed_modes):
    local = weights.reshape(weights.shape[2:])
    core = lax.axis_index("cores")
    me = lax.axis_index("bx") * 2 + lax.axis_index("by")
    ids = jnp.stack([me, core]).astype(jnp.int32)
    speeds = speed_tables(speed_modes, core)

    first = deal(pack(local, 0))
    near = exchange(pack_masks(local, ids, 1), 1)
    second = exchange(regroup(near), 4)

    own = join(first)
    first = levels(0, ids, own, partner_2(own, "cores", 0), speeds[0])
    back_first = deal(first)

    own = join(second, ids, [first])
    back_second = deal(levels(1, ids, own, partner_2(own, "cores", 0), speeds[1]))

    out = unpack(back_first, 0, None)
    out = unpack(back_second, 1, out)
    return out.reshape(weights.shape)


def deal(pieces):
    return lax.all_to_all(pieces, ("bx", "by"), 0, 0, tiled=True)


def solution(mesh):
    sizes = dict(mesh.shape)
    spec = P(("bx", "cores"), "by", None, None, None, None)
    dealt = (sizes["bx"], sizes["by"], sizes["cores"]) == (8, 2, 2)

    def whole(weights, speed_modes):
        fits = dealt and weights.shape[2:] == (2, 16, 16, 1024)
        return jax.shard_map(
            on_device_dealt if fits else on_device,
            mesh=mesh,
            in_specs=(spec, P()),
            out_specs=spec,
            check_vma=False,
        )(weights, speed_modes)

    return whole
```

```python
from functools import partial
import math

import jax
import jax.numpy as jnp
import ml_dtypes
import numpy as np
from jax import lax
from jax.experimental import pallas as pl
from jax.experimental.pallas import tpu as pltpu
from jax.sharding import PartitionSpec as P

N = 8192
TGT = 32


def partner_2(value, axis, apart):
    mask = 2**apart
    pairs = [(source, source ^ mask) for source in range(lax.axis_size(axis))]
    return lax.ppermute(value, axis, pairs)


def cheb_nodes(degree):
    return np.cos(np.pi * (2 * np.arange(degree) + 1) / (2 * degree))


def lagrange_table(degree):
    points = cheb_nodes(degree)
    result = np.ones((degree, 2 * degree))
    for child_side in range(2):
        inside = (points + 2 * child_side - 1) / 2
        for node_row in range(degree):
            for node_other in range(degree):
                if node_other != node_row:
                    result[node_row, child_side * degree : (child_side + 1) * degree] *= (
                        inside - points[node_other]
                    ) / (points[node_row] - points[node_other])
    return result


def speed_of(speed_modes, target_one, target_two):
    mode_count = speed_modes.shape[0]
    frequencies = jnp.arange(mode_count).astype(jnp.float32) * math.pi
    along_one = jnp.cos(frequencies[:, None] * target_one[None, :])
    along_two = jnp.cos(frequencies[:, None] * target_two[None, :])
    blended = jnp.dot(
        speed_modes, along_two, preferred_element_type=jnp.float32, precision=lax.Precision.HIGHEST
    )
    return 1.0 + jnp.sum(blended * along_one, axis=0)


def rotation(target_one, target_two, speed_value, wave_one, wave_two):
    phase = (
        target_one * wave_one
        + target_two * wave_two
        + speed_value * jnp.sqrt(wave_one * wave_one + wave_two * wave_two)
    )
    phase = phase - jnp.floor(phase)
    angle = 2.0 * math.pi * phase
    return (jnp.cos(angle), jnp.sin(angle))


def node_phase(layout, speed_value, center, half_width, degree):
    target_one, target_two, merge_dim, centers, child_half, other_center, other_half = layout
    points = jnp.asarray(cheb_nodes(degree), jnp.float32)
    merged = center[None, :] + half_width * points[:, None]
    across = other_center[None, :] + other_half * points[:, None]
    if merge_dim == 0:
        return rotation(target_one, target_two, speed_value, merged[:, None, :], across[None, :, :])
    return rotation(target_one, target_two, speed_value, across[:, None, :], merged[None, :, :])


def merge_children(child_low, child_high, layout, speed_modes):
    target_one, target_two, merge_dim, centers, child_half, other_center, other_half = layout
    degree = child_low.shape[1]
    speed_value = speed_of(speed_modes, target_one, target_two)
    lagrange = jnp.asarray(lagrange_table(degree), jnp.float32)
    pieces = []
    for child, center in ((child_low, centers[0]), (child_high, centers[1])):
        cosine, sine_part = node_phase(layout, speed_value, center, child_half, degree)
        real_part = child[0] * cosine + child[1] * sine_part
        imag_part = child[1] * cosine - child[0] * sine_part
        pieces.append(jnp.stack([real_part, imag_part]))
    stacked = jnp.concatenate(pieces, axis=1 + merge_dim)
    if merge_dim == 0:
        blended = jnp.einsum("ij,rjks->riks", lagrange, stacked, precision=lax.Precision.HIGHEST)
    else:
        blended = jnp.einsum("kj,rijs->riks", lagrange, stacked, precision=lax.Precision.HIGHEST)
    cosine, sine_part = node_phase(layout, speed_value, centers[2], 2.0 * child_half, degree)
    return jnp.stack(
        [blended[0] * cosine - blended[1] * sine_part, blended[0] * sine_part + blended[1] * cosine]
    )


def reversed_bits(box_code, bit_count):
    result = jnp.zeros_like(box_code)
    for bit_place in range(bit_count):
        result = result + box_code // 2**bit_place % 2 * 2 ** (bit_count - 1 - bit_place)
    return result


def x_layout(level_index, box_code, targets, y_box, geometry):
    extent, side_count, src_x, src_y = geometry
    span_size = 2 ** (level_index + 1)
    row_index = targets // side_count * span_size + reversed_bits(box_code, level_index + 1)
    target_one = (row_index.astype(jnp.float32) + 0.5) / (side_count * span_size)
    target_two = ((targets % side_count).astype(jnp.float32) + 0.5) / side_count
    parent = (box_code // span_size).astype(jnp.float32)
    child_width = extent * 2**level_index / src_x
    low_center = -extent / 2 + (2.0 * parent + 0.5) * child_width
    high_center = low_center + child_width
    parent_center = -extent / 2 + (parent + 0.5) * (2.0 * child_width)
    other_center = jnp.zeros_like(target_one) + (
        -extent / 2 + (jnp.asarray(y_box).astype(jnp.float32) + 0.5) * (extent / src_y)
    )
    return (
        target_one,
        target_two,
        0,
        (low_center, high_center, parent_center),
        child_width / 2,
        other_center,
        extent / (2 * src_y),
    )


def y_layout(level_index, box_code, targets, x_code, x_bits, geometry):
    extent, side_count, src_x, src_y = geometry
    span_size = 2 ** (level_index + 1)
    col_index = targets % side_count * span_size + reversed_bits(box_code, level_index + 1)
    target_two = (col_index.astype(jnp.float32) + 0.5) / (side_count * span_size)
    row_index = targets // side_count * src_x + reversed_bits(x_code, x_bits)
    target_one = (row_index.astype(jnp.float32) + 0.5) / (side_count * src_x)
    parent = (box_code // span_size).astype(jnp.float32)
    child_width = extent * 2**level_index / src_y
    low_center = -extent / 2 + (2.0 * parent + 0.5) * child_width
    high_center = low_center + child_width
    parent_center = -extent / 2 + (parent + 0.5) * (2.0 * child_width)
    other_center = jnp.zeros_like(target_one)
    return (
        target_one,
        target_two,
        1,
        (low_center, high_center, parent_center),
        child_width / 2,
        other_center,
        extent / 2,
    )


def pair_level(current, partner, level_index, box_code, targets, layout_fn, speed_modes):
    own_bit = box_code // 2**level_index % 2
    child_low = jnp.where(own_bit == 0, current, partner)
    child_high = jnp.where(own_bit == 0, partner, current)
    box_codes = jnp.zeros_like(targets) + box_code
    return merge_children(
        child_low, child_high, layout_fn(level_index, box_codes, targets), speed_modes
    )


def on_device(weights, speed_modes):
    current = weights.reshape(weights.shape[2:])
    pair_count = current.shape[3]
    core_count = lax.axis_size("cores")
    src_x = lax.axis_size("bx") * core_count
    src_y = lax.axis_size("by")
    x_bits = src_x.bit_length() - 1
    y_bits = src_y.bit_length() - 1
    x_code = lax.axis_index("bx") * core_count + lax.axis_index("cores")
    y_box = lax.axis_index("by")
    geometry = (float(N), TGT, src_x, src_y)
    targets = jnp.arange(pair_count, dtype=jnp.int32)
    first_layout = partial(x_layout, y_box=y_box, geometry=geometry)
    second_layout = partial(y_layout, x_code=x_code, x_bits=x_bits, geometry=geometry)
    for level_index in range(x_bits):
        if level_index == 0:
            partner = partner_2(current, "cores", 0)
        else:
            partner = partner_2(current, "bx", level_index - 1)
        current = pair_level(
            current, partner, level_index, x_code, targets, first_layout, speed_modes
        )
    for level_index in range(y_bits):
        partner = partner_2(current, "by", level_index)
        current = pair_level(
            current, partner, level_index, y_box, targets, second_layout, speed_modes
        )
    return current.reshape(weights.shape)


SIN_HALF = (4.442879586386342, -7.3078180422392816, 3.597788667381583, -0.7912380409231197)
COS_HALF = (
    1.4142134965636117,
    -6.978850988059019,
    5.739461167077472,
    -1.883562964211867,
    0.3106981455985473,
)
CHUNKS = 2
PIECES = 16
LEVEL_ROWS = (0, 256, 384, 448, 480)
VMEM_LIMIT = 48 * 2**20


def node_tables():
    points = cheb_nodes(16).astype(np.float32)
    nodes = []
    for level_index in range(5):
        width = np.float32(N * 2**level_index / 16)
        for box in range(16 >> level_index):
            center = np.float32(-N / 2 + (box + 0.5) * width)
            nodes.append(center + (width / 2) * points)
    nodes = np.concatenate(nodes).astype(np.float32)
    sub = np.arange(8)
    lane = np.arange(128)
    half = (sub // 4)[:, None] + 0 * lane[None, :]
    second = (lane // 32 * 4)[None, :] + (sub % 4)[:, None]
    wave_two = (-N / 2 + (half + 0.5) * (N / 2)).astype(np.float32) + np.float32(N / 4) * points[second]
    wave_two = wave_two.astype(np.float32)
    lengths = np.sqrt(nodes[:, None, None] * nodes[:, None, None] + wave_two * wave_two)
    return nodes, wave_two, lengths.astype(np.float32)


def final_tables():
    points = cheb_nodes(16).astype(np.float32) * np.float32(N / 2)
    lane = np.arange(128)
    one = np.broadcast_to(points.reshape(2, 8, 1), (2, 8, 128)).astype(np.float32)
    two = np.stack([np.broadcast_to(points[lane // 32 * 4 + a], (8, 128)) for a in range(4)])
    two = two.astype(np.float32)
    lengths = np.sqrt((one * one)[:, None] + (two * two)[None, :]).astype(np.float32)
    return np.array(one), two, lengths


def in_two_parts(table):
    high = table.astype(ml_dtypes.bfloat16)
    low = (table - high.astype(np.float32)).astype(ml_dtypes.bfloat16)
    return high, low


def first_weights():
    table = lagrange_table(16).astype(np.float32)
    high, low = in_two_parts(np.kron(table, np.eye(8, dtype=np.float32)))
    return np.concatenate([high, low])


def second_weights():
    table = lagrange_table(16)
    result = np.zeros((8, 4, 32, 4, 4, 32), np.float32)
    same = np.eye(32, dtype=np.float32)
    for half in range(2):
        for a in range(4):
            for b in range(4):
                for out_a in range(4):
                    for out_b in range(4):
                        weight = table[4 * out_b + out_a, half * 16 + 4 * b + a]
                        result[half * 4 + a, b, :, out_a, out_b, :] = np.float32(weight) * same
    return np.stack(in_two_parts(result.reshape(4, 256, 512)))


def turn(phase):
    part = phase - jnp.round(phase)
    square = part * part
    sine = SIN_HALF[3]
    for coefficient in SIN_HALF[2::-1]:
        sine = sine * square + coefficient
    sine = sine * part
    cosine = COS_HALF[4]
    for coefficient in COS_HALF[3::-1]:
        cosine = cosine * square + coefficient
    return 1.0 - sine * sine, sine * cosine


def swap_lanes(values):
    lane = lax.broadcasted_iota(jnp.int32, (8, 128), 1)
    low = lane < 64
    even = lane // 32 % 2 == 0
    half = [None] * 4
    for b in range(2):
        half[b] = jnp.where(low, values[b], pltpu.roll(values[b + 2], 64, 1))
        half[b + 2] = jnp.where(low, pltpu.roll(values[b], 64, 1), values[b + 2])
    full = [None] * 4
    for j in (0, 2):
        full[j] = jnp.where(even, half[j], pltpu.roll(half[j + 1], 32, 1))
        full[j + 1] = jnp.where(even, pltpu.roll(half[j], 96, 1), half[j + 1])
    return full


def pack_rows(in_ref, lanes, tiles):
    upper = lax.broadcasted_iota(jnp.int32, (8, 128), 0) < 4
    for t1 in range(16):
        groups = [None] * 4
        for high in range(2):
            real = in_ref[0, t1, 8 * high : 8 * high + 8, lanes]
            imag = in_ref[1, t1, 8 * high : 8 * high + 8, lanes]
            groups[2 * high] = jnp.where(upper, real, pltpu.roll(imag, 4, 0))
            groups[2 * high + 1] = jnp.where(upper, pltpu.roll(real, 4, 0), imag)
        for j, tile in enumerate(swap_lanes(groups)):
            tiles[j, t1] = tile


def pack_kernel(in_ref, out_ref):
    def step(group, carry):
        lanes = pl.ds(pl.multiple_of(group * 128, 128), 128)
        pack_rows(in_ref, lanes, out_ref.at[pl.ds(4 * group, 4)])
        return carry

    lax.fori_loop(0, 4, step, 0)


def pack(weights, chunk):
    return pl.pallas_call(
        pack_kernel,
        grid=(1,),
        in_specs=[pl.BlockSpec((2, 16, 16, 512), lambda i: (0, 0, 0, chunk))],
        out_specs=pl.BlockSpec((PIECES, 16, 8, 128), lambda i: (0, 0, 0, 0)),
        out_shape=jax.ShapeDtypeStruct((PIECES, 16, 8, 128), jnp.float32),
        compiler_params=pltpu.CompilerParams(vmem_limit_bytes=VMEM_LIMIT),
        cost_estimate=pl.CostEstimate(flops=10**6, bytes_accessed=2**21, transcendentals=0),
        name="pack",
    )(weights)


BUNDLE = (4, 16, 8, 128)


def bundles_of(by_z):
    shapes = [(4,) + BUNDLE] if by_z else [BUNDLE] * 4
    return [jax.ShapeDtypeStruct(shape, jnp.float32) for shape in shapes]


def entry_of(bundles, by_z, z, mask):
    return bundles[0].at[z, mask] if by_z else bundles[mask].at[z]


def pack_masks_kernel(ids, in_ref, *refs):
    outs, tiles = refs[:4], refs[4]

    def step(z, carry):
        pack_rows(in_ref, pl.ds(pl.multiple_of(z * 128, 128), 128), tiles)
        for mask in range(4):
            outs[mask][z] = tiles[mask ^ (ids[0] % 4)]
        return carry

    lax.fori_loop(0, 4, step, 0)


def pack_masks(weights, ids, chunk):
    return pl.pallas_call(
        pack_masks_kernel,
        grid=(1,),
        in_specs=[
            pl.BlockSpec(memory_space=pltpu.SMEM),
            pl.BlockSpec((2, 16, 16, 512), lambda i: (0, 0, 0, chunk)),
        ],
        out_specs=[pl.BlockSpec(BUNDLE, lambda i: (0, 0, 0, 0))] * 4,
        out_shape=bundles_of(False),
        scratch_shapes=[pltpu.VMEM(BUNDLE, jnp.float32)],
        compiler_params=pltpu.CompilerParams(vmem_limit_bytes=VMEM_LIMIT),
        cost_estimate=pl.CostEstimate(flops=10**6, bytes_accessed=2**21, transcendentals=0),
        name="pack_masks",
    )(ids, weights)


def regroup_kernel(by_z, *refs):
    outs = refs[-4:] if by_z else refs[-1:]

    def step(z, carry):
        for mask in range(4):
            entry_of(outs, not by_z, z, mask)[...] = entry_of(refs, by_z, z, mask)[...]
        return carry

    lax.fori_loop(0, 4, step, 0)


def regroup(bundles, by_z, after=()):
    in_vmem = pl.BlockSpec(memory_space=pltpu.VMEM)
    shapes = bundles_of(not by_z)
    return pl.pallas_call(
        partial(regroup_kernel, by_z),
        in_specs=[in_vmem] * len(bundles) + [pl.BlockSpec(memory_space=pl.ANY)] * len(after),
        out_specs=[in_vmem] * len(shapes),
        out_shape=shapes,
        compiler_params=pltpu.CompilerParams(vmem_limit_bytes=VMEM_LIMIT),
        cost_estimate=pl.CostEstimate(flops=10**5, bytes_accessed=2**21, transcendentals=0),
        name="regroup",
    )(*bundles, *after)


def cross_xy(bundles):
    moved = [bundles[0]]
    for mask in range(1, 4):
        pairs = [(source, source ^ mask) for source in range(PIECES)]
        moved.append(lax.ppermute(bundles[mask], ("bx", "by"), pairs))
    return moved


def deal_z(bundles):
    groups = [[4 * z + xy for z in range(4)] for xy in range(4)]
    return [
        lax.all_to_all(bundles[0], ("bx", "by"), 0, 0, axis_index_groups=groups, tiled=True)
    ]


def merge_halves(out_ref, box, t1, low, high):
    upper = lax.broadcasted_iota(jnp.int32, (8, 128), 0) < 4
    out_ref[box, 0, t1] = jnp.where(upper, low, pltpu.roll(high, 4, 0))
    out_ref[box, 1, t1] = jnp.where(upper, pltpu.roll(low, 4, 0), high)


def join_kernel(in_ref, *refs):
    out_ref = refs[-1]

    def step(box, carry):
        for t1 in range(16):
            merge_halves(out_ref, box, t1, in_ref[2 * box, t1], in_ref[2 * box + 1, t1])
        return carry

    lax.fori_loop(0, 8, step, 0)


def join_masks_kernel(ids, *refs):
    bundles, out_ref = refs[:1], refs[-1]
    me = ids[0]
    is_low = jnp.broadcast_to(me % 2, (8, 128)) == 0

    def step(z, carry):
        for mx in range(2):
            box = 2 * z + (mx ^ (me // 2 % 2))
            for t1 in range(16):
                mine = entry_of(bundles, True, z, 2 * mx)[t1]
                partner = entry_of(bundles, True, z, 2 * mx + 1)[t1]
                low = jnp.where(is_low, mine, partner)
                high = jnp.where(is_low, partner, mine)
                merge_halves(out_ref, box, t1, low, high)
        return carry

    lax.fori_loop(0, 4, step, 0)


def join(received, ids=None, after=()):
    in_vmem = pl.BlockSpec(memory_space=pltpu.VMEM)
    if ids is None:
        kernel, operands, in_specs = join_kernel, received, [in_vmem]
    else:
        kernel, operands = join_masks_kernel, [ids, *received]
        in_specs = [pl.BlockSpec(memory_space=pltpu.SMEM), in_vmem]
    return pl.pallas_call(
        kernel,
        in_specs=in_specs + [pl.BlockSpec(memory_space=pl.ANY)] * len(after),
        out_specs=in_vmem,
        out_shape=jax.ShapeDtypeStruct((8, 2, 16, 8, 128), jnp.float32),
        compiler_params=pltpu.CompilerParams(vmem_limit_bytes=VMEM_LIMIT),
        cost_estimate=pl.CostEstimate(flops=10**6, bytes_accessed=2**21, transcendentals=0),
        name="join",
    )(*operands, *after)


def levels_kernel(
    chunk, by_z, ids, nodes, own, other, speeds, waves, lengths, last_one, last_two,
    last_lengths, first_table, second_table, *refs,
):
    outs = refs[:-6]
    boxes_a, boxes_b, sums, turned, mixed, last_phase = refs[-6:]
    row = (chunk * PIECES + ids[0]).astype(jnp.float32)
    core = ids[1]
    core_float = core.astype(jnp.float32)
    wave_two = waves[...]
    lane = lax.broadcasted_iota(jnp.int32, (8, 128), 1)
    along_two = ((lane % 32).astype(jnp.float32) + 0.5) * (1.0 / 32)
    second_phase = along_two * wave_two

    def first_point(level_index, low_code):
        span = 2.0 ** (level_index + 1)
        code = core_float * 2.0**level_index + low_code
        return (row * span + code + 0.5) * (1.0 / (32 * span))

    def speed_row(level_index, low_code):
        return jnp.broadcast_to(speeds[pl.ds(2**level_index - 1 + low_code, 1), :], (8, 128))

    def blend(slot, target, boxes):
        rows = sums[slot].astype(jnp.bfloat16)
        both = jnp.dot(first_table[...], rows, preferred_element_type=jnp.float32)
        total = both[:128] + both[128:]
        for n, box in enumerate(boxes):
            for part in range(2):
                column = 128 * (2 * n + part)
                target[box, part] = total[:, column : column + 128].reshape(16, 8, 128)

    def put(slot, first_row, column, real, imag):
        sums[slot, pl.ds(first_row, 8), 256 * column : 256 * column + 128] = real
        sums[slot, pl.ds(first_row, 8), 256 * column + 128 : 256 * column + 256] = imag

    def first_level(pair, slot):
        point = first_point(0, 0.0)
        speed = speed_row(0, 0)
        for n in range(2):
            box = 2 * pair + n
            for source, child in ((own, core), (other, 1 - core)):
                for t1 in range(16):
                    entry = (2 * box + child) * 16 + t1
                    phase = (point * nodes[entry] + second_phase) + speed * lengths[entry]
                    cosine, sine = turn(phase)
                    real = source[box, 0, t1]
                    imag = source[box, 1, t1]
                    first_row = pl.multiple_of(child * 128 + 8 * t1, 8)
                    put(slot, first_row, n, real * cosine + imag * sine, imag * cosine - real * sine)
        blend(slot, boxes_a, [2 * pair, 2 * pair + 1])

    def later_level(level_index, source, target, index, slot):
        low_bits = level_index - 1
        stride = 2**low_bits
        parent = index // stride
        low = index % stride
        code = jnp.int32(0)
        for bit in range(low_bits):
            code = code + low // 2**bit % 2 * 2 ** (low_bits - 1 - bit)
        before = first_point(level_index - 1, code.astype(jnp.float32))
        before_speed = speed_row(level_index - 1, code)
        points = [first_point(level_index, (2 * code + b).astype(jnp.float32)) for b in range(2)]
        point_speeds = [speed_row(level_index, 2 * code + b) for b in range(2)]
        first_box = parent * (2 * stride) + low
        for child in range(2):
            for t1 in range(16):
                entry = LEVEL_ROWS[level_index] + (2 * parent + child) * 16 + t1
                length = lengths[entry]
                wave = nodes[entry]
                real = source[first_box + child * stride, 0, t1]
                imag = source[first_box + child * stride, 1, t1]
                old = (before * wave + second_phase) + before_speed * length
                for b in range(2):
                    new = (points[b] * wave + second_phase) + point_speeds[b] * length
                    cosine, sine = turn(new - old)
                    first_row = child * 128 + 8 * t1
                    put(slot, first_row, b, real * cosine + imag * sine, imag * cosine - real * sine)
        blend(slot, target, [first_box, first_box + stride])

    def in_pairs(one):
        def step(half, carry):
            for slot in range(2):
                one(2 * half + slot, slot)
            return carry

        lax.fori_loop(0, 2, step, 0)

    in_pairs(first_level)
    in_pairs(partial(later_level, 1, boxes_a, boxes_b))
    in_pairs(partial(later_level, 2, boxes_b, boxes_a))
    in_pairs(partial(later_level, 3, boxes_a, boxes_b))

    fine_two = [((lane % 32).astype(jnp.float32) * 2.0 + (e + 0.5)) * (1.0 / 64) for e in range(2)]
    fine_phase = [fine_two[e] * wave_two for e in range(2)]

    def reversed_code(box):
        return box % 2 * 4 + box // 2 % 2 * 2 + box // 4

    def fine_speed(code, e):
        return jnp.broadcast_to(speeds[pl.ds(15 + 2 * code + e, 1), :], (8, 128))

    def rotate_box(box, carry):
        code = reversed_code(box)
        point = first_point(3, code.astype(jnp.float32))
        old_speed = speed_row(3, code)
        new_speeds = [fine_speed(code, e) for e in range(2)]
        for t1 in range(16):
            entry = LEVEL_ROWS[4] + t1
            length = lengths[entry]
            across = point * nodes[entry]
            real = boxes_b[box, 0, t1]
            imag = boxes_b[box, 1, t1]
            old = (across + second_phase) + old_speed * length
            for e in range(2):
                new = (across + fine_phase[e]) + new_speeds[e] * length
                cosine, sine = turn(new - old)
                first = pl.multiple_of((e * 256 + box * 32 + t1) * 8, 8)
                turned[pl.ds(first, 8), :] = real * cosine + imag * sine
                turned[pl.ds(first + 128, 8), :] = imag * cosine - real * sine
        return carry

    lax.fori_loop(0, 8, rotate_box, 0)

    for e in range(2):
        for a in range(4):
            last_phase[e, a] = fine_two[e] * last_two[a]

    total = None
    for j in range(4):
        rows = jnp.concatenate(
            [turned[pl.ds(2 * j + k, 512, stride=8), :] for k in range(2)], axis=1
        ).astype(jnp.bfloat16)
        for part in range(2):
            term = jnp.dot(rows, second_table[part, j], preferred_element_type=jnp.float32)
            total = term if total is None else total + term
    mixed[...] = total

    def finish_box(target, out):
        box, e = target // 2, target % 2
        code = reversed_code(box)
        point = first_point(3, code.astype(jnp.float32))
        speed = fine_speed(code, e)
        for high in range(2):
            across = point * last_one[high]
            first = pl.multiple_of(e * 256 + box * 32 + high * 8, 8)
            for a in range(4):
                phase = (across + last_phase[e, a]) + speed * last_lengths[high, a]
                cosine, sine = turn(phase)
                real = mixed[pl.ds(first, 8), 128 * a : 128 * a + 128]
                imag = mixed[pl.ds(first + 16, 8), 128 * a : 128 * a + 128]
                out[high * 4 + a] = real * cosine - imag * sine
                out[8 + high * 4 + a] = real * sine + imag * cosine

    def finish_row(z, carry):
        for mask in range(4):
            finish_box(4 * z + (mask ^ (ids[0] % 4)), entry_of(outs, by_z, z, mask))
        return carry

    lax.fori_loop(0, 4, finish_row, 0)


def levels(chunk, by_z, ids, own, other, speeds):
    nodes, waves, lengths = node_tables()
    last_one, last_two, last_lengths = final_tables()
    tables = (waves, lengths, last_one, last_two, last_lengths, first_weights(), second_weights())
    in_vmem = pl.BlockSpec(memory_space=pltpu.VMEM)
    in_smem = pl.BlockSpec(memory_space=pltpu.SMEM)
    return pl.pallas_call(
        partial(levels_kernel, chunk, by_z),
        in_specs=[in_smem, in_smem] + [in_vmem] * 10,
        out_specs=[in_vmem] * len(bundles_of(by_z)),
        out_shape=bundles_of(by_z),
        scratch_shapes=[
            pltpu.VMEM((8, 2, 16, 8, 128), jnp.float32),
            pltpu.VMEM((8, 2, 16, 8, 128), jnp.float32),
            pltpu.VMEM((2, 256, 512), jnp.float32),
            pltpu.VMEM((4096, 128), jnp.float32),
            pltpu.VMEM((512, 512), jnp.float32),
            pltpu.VMEM((2, 4, 8, 128), jnp.float32),
        ],
        compiler_params=pltpu.CompilerParams(vmem_limit_bytes=VMEM_LIMIT),
        cost_estimate=pl.CostEstimate(flops=10**8, bytes_accessed=2**23, transcendentals=0),
        name="levels",
    )(ids, jnp.asarray(nodes), own, other, speeds, *[jnp.asarray(table) for table in tables])


def unpack_rows(tiles, rows, out_ref, lanes):
    for part in range(2):
        for high in range(2):
            block = part * 2 + high
            for a in range(4):
                values = [tiles[j, part * 8 + high * 4 + a] for j in range(4)]
                for b, tile in enumerate(swap_lanes(values)):
                    t2 = 4 * b + a
                    rows[block, 8 * t2 : 8 * t2 + 8, :] = tile
            for t1 in range(8):
                out_ref[part, high * 8 + t1, :, lanes] = rows[block, pl.ds(t1, 16, stride=8), :]


def unpack_kernel(by_z, ids, *refs):
    bundles, out_ref, tiles, rows = refs[:-3], refs[-3], refs[-2], refs[-1]
    for mask in range(4):
        tiles[mask ^ (ids[0] % 4)] = entry_of(bundles, by_z, 0, mask)[...]
    unpack_rows(tiles, rows, out_ref, slice(None))


def unpack(received, ids, chunk, by_z, earlier):
    operands = [ids, *received]
    in_specs = [pl.BlockSpec(memory_space=pltpu.SMEM)]
    if by_z:
        in_specs.append(pl.BlockSpec((1,) + BUNDLE, lambda z: (z, 0, 0, 0, 0)))
    else:
        in_specs += [pl.BlockSpec((1,) + BUNDLE[1:], lambda z: (z, 0, 0, 0))] * 4
    aliases = {}
    if earlier is not None:
        aliases = {len(operands): 0}
        operands.append(earlier)
        in_specs.append(pl.BlockSpec(memory_space=pl.ANY))
    return pl.pallas_call(
        partial(unpack_kernel, by_z),
        grid=(4,),
        in_specs=in_specs,
        out_specs=pl.BlockSpec((2, 16, 16, 128), lambda z: (0, 0, 0, 4 * chunk + z)),
        out_shape=jax.ShapeDtypeStruct((2, 16, 16, 1024), jnp.float32),
        scratch_shapes=[pltpu.VMEM(BUNDLE, jnp.float32), pltpu.VMEM((4, 128, 128), jnp.float32)],
        input_output_aliases=aliases,
        compiler_params=pltpu.CompilerParams(vmem_limit_bytes=VMEM_LIMIT),
        cost_estimate=pl.CostEstimate(flops=10**6, bytes_accessed=2**21, transcendentals=0),
        name="unpack",
    )(*operands)


def speed_tables(speed_modes, core):
    numerators, spans = [], []
    for level_index in range(4):
        for code in range(2**level_index):
            numerators.append(core * 2**level_index + code)
            spans.append(2 ** (level_index + 1))
    for code in range(8):
        for e in range(2):
            numerators.append(core * 8 + code)
            spans.append(16)
    codes = jnp.stack(numerators).astype(jnp.float32)
    spans = jnp.asarray(np.array(spans), jnp.float32)
    me = lax.axis_index("bx") * 2 + lax.axis_index("by")
    rows = (jnp.arange(CHUNKS) * PIECES + me).astype(jnp.float32)
    target_one = (rows[:, None] * spans + codes + 0.5) / (TGT * spans)
    columns = jnp.arange(32).astype(jnp.float32)
    coarse = jnp.broadcast_to((columns + 0.5) / TGT, (15, 32))
    fine = jnp.stack([(2 * columns + e + 0.5) / (2 * TGT) for e in range(2)])
    target_two = jnp.concatenate([coarse, jnp.tile(fine, (8, 1))])
    target_one = jnp.broadcast_to(target_one[:, :, None], (CHUNKS, 31, 32))
    target_two = jnp.broadcast_to(target_two[None], (CHUNKS, 31, 32))
    speed = speed_of(speed_modes, target_one.reshape(-1), target_two.reshape(-1))
    return jnp.tile(speed.reshape(CHUNKS, 31, 32), (1, 1, 4))


def on_device_dealt(weights, speed_modes):
    local = weights.reshape(weights.shape[2:])
    core = lax.axis_index("cores")
    me = lax.axis_index("bx") * 2 + lax.axis_index("by")
    ids = jnp.stack([me, core]).astype(jnp.int32)
    speeds = speed_tables(speed_modes, core)

    first = deal(pack(local, 0))
    grouped = regroup(cross_xy(pack_masks(local, ids, 1)), False)
    second = deal_z(grouped)

    own = join([first], None, grouped)
    first = levels(0, True, ids, own, partner_2(own, "cores", 0), speeds[0])
    back_first = deal_z(first)

    own = join(second, ids, first)
    second = levels(1, False, ids, own, partner_2(own, "cores", 0), speeds[1])
    grouped = regroup(cross_xy(second), False)
    back_second = deal_z(grouped)

    back_first = cross_xy(regroup(back_first, True, grouped))
    out = unpack(back_first, ids, 0, False, None)
    out = unpack(back_second, ids, 1, True, out)
    return out.reshape(weights.shape)


def deal(pieces):
    return lax.all_to_all(pieces, ("bx", "by"), 0, 0, tiled=True)


def solution(mesh):
    sizes = dict(mesh.shape)
    spec = P(("bx", "cores"), "by", None, None, None, None)
    dealt = (sizes["bx"], sizes["by"], sizes["cores"]) == (8, 2, 2)

    def whole(weights, speed_modes):
        fits = dealt and weights.shape[2:] == (2, 16, 16, 1024)
        return jax.shard_map(
            on_device_dealt if fits else on_device,
            mesh=mesh,
            in_specs=(spec, P()),
            out_specs=spec,
            check_vma=False,
        )(weights, speed_modes)

    return whole
```

```python
from functools import partial
import math

import jax
import jax.numpy as jnp
import ml_dtypes
import numpy as np
from jax import lax
from jax.experimental import pallas as pl
from jax.experimental.pallas import tpu as pltpu
from jax.sharding import PartitionSpec as P

N = 8192
TGT = 32


def partner_2(value, axis, apart):
    mask = 2**apart
    pairs = [(source, source ^ mask) for source in range(lax.axis_size(axis))]
    return lax.ppermute(value, axis, pairs)


def cheb_nodes(degree):
    return np.cos(np.pi * (2 * np.arange(degree) + 1) / (2 * degree))


def lagrange_table(degree):
    points = cheb_nodes(degree)
    result = np.ones((degree, 2 * degree))
    for child_side in range(2):
        inside = (points + 2 * child_side - 1) / 2
        for node_row in range(degree):
            for node_other in range(degree):
                if node_other != node_row:
                    result[node_row, child_side * degree : (child_side + 1) * degree] *= (
                        inside - points[node_other]
                    ) / (points[node_row] - points[node_other])
    return result


def speed_of(speed_modes, target_one, target_two):
    mode_count = speed_modes.shape[0]
    frequencies = jnp.arange(mode_count).astype(jnp.float32) * math.pi
    along_one = jnp.cos(frequencies[:, None] * target_one[None, :])
    along_two = jnp.cos(frequencies[:, None] * target_two[None, :])
    blended = jnp.dot(
        speed_modes, along_two, preferred_element_type=jnp.float32, precision=lax.Precision.HIGHEST
    )
    return 1.0 + jnp.sum(blended * along_one, axis=0)


def rotation(target_one, target_two, speed_value, wave_one, wave_two):
    phase = (
        target_one * wave_one
        + target_two * wave_two
        + speed_value * jnp.sqrt(wave_one * wave_one + wave_two * wave_two)
    )
    phase = phase - jnp.floor(phase)
    angle = 2.0 * math.pi * phase
    return (jnp.cos(angle), jnp.sin(angle))


def node_phase(layout, speed_value, center, half_width, degree):
    target_one, target_two, merge_dim, centers, child_half, other_center, other_half = layout
    points = jnp.asarray(cheb_nodes(degree), jnp.float32)
    merged = center[None, :] + half_width * points[:, None]
    across = other_center[None, :] + other_half * points[:, None]
    if merge_dim == 0:
        return rotation(target_one, target_two, speed_value, merged[:, None, :], across[None, :, :])
    return rotation(target_one, target_two, speed_value, across[:, None, :], merged[None, :, :])


def merge_children(child_low, child_high, layout, speed_modes):
    target_one, target_two, merge_dim, centers, child_half, other_center, other_half = layout
    degree = child_low.shape[1]
    speed_value = speed_of(speed_modes, target_one, target_two)
    lagrange = jnp.asarray(lagrange_table(degree), jnp.float32)
    pieces = []
    for child, center in ((child_low, centers[0]), (child_high, centers[1])):
        cosine, sine_part = node_phase(layout, speed_value, center, child_half, degree)
        real_part = child[0] * cosine + child[1] * sine_part
        imag_part = child[1] * cosine - child[0] * sine_part
        pieces.append(jnp.stack([real_part, imag_part]))
    stacked = jnp.concatenate(pieces, axis=1 + merge_dim)
    if merge_dim == 0:
        blended = jnp.einsum("ij,rjks->riks", lagrange, stacked, precision=lax.Precision.HIGHEST)
    else:
        blended = jnp.einsum("kj,rijs->riks", lagrange, stacked, precision=lax.Precision.HIGHEST)
    cosine, sine_part = node_phase(layout, speed_value, centers[2], 2.0 * child_half, degree)
    return jnp.stack(
        [blended[0] * cosine - blended[1] * sine_part, blended[0] * sine_part + blended[1] * cosine]
    )


def reversed_bits(box_code, bit_count):
    result = jnp.zeros_like(box_code)
    for bit_place in range(bit_count):
        result = result + box_code // 2**bit_place % 2 * 2 ** (bit_count - 1 - bit_place)
    return result


def x_layout(level_index, box_code, targets, y_box, geometry):
    extent, side_count, src_x, src_y = geometry
    span_size = 2 ** (level_index + 1)
    row_index = targets // side_count * span_size + reversed_bits(box_code, level_index + 1)
    target_one = (row_index.astype(jnp.float32) + 0.5) / (side_count * span_size)
    target_two = ((targets % side_count).astype(jnp.float32) + 0.5) / side_count
    parent = (box_code // span_size).astype(jnp.float32)
    child_width = extent * 2**level_index / src_x
    low_center = -extent / 2 + (2.0 * parent + 0.5) * child_width
    high_center = low_center + child_width
    parent_center = -extent / 2 + (parent + 0.5) * (2.0 * child_width)
    other_center = jnp.zeros_like(target_one) + (
        -extent / 2 + (jnp.asarray(y_box).astype(jnp.float32) + 0.5) * (extent / src_y)
    )
    return (
        target_one,
        target_two,
        0,
        (low_center, high_center, parent_center),
        child_width / 2,
        other_center,
        extent / (2 * src_y),
    )


def y_layout(level_index, box_code, targets, x_code, x_bits, geometry):
    extent, side_count, src_x, src_y = geometry
    span_size = 2 ** (level_index + 1)
    col_index = targets % side_count * span_size + reversed_bits(box_code, level_index + 1)
    target_two = (col_index.astype(jnp.float32) + 0.5) / (side_count * span_size)
    row_index = targets // side_count * src_x + reversed_bits(x_code, x_bits)
    target_one = (row_index.astype(jnp.float32) + 0.5) / (side_count * src_x)
    parent = (box_code // span_size).astype(jnp.float32)
    child_width = extent * 2**level_index / src_y
    low_center = -extent / 2 + (2.0 * parent + 0.5) * child_width
    high_center = low_center + child_width
    parent_center = -extent / 2 + (parent + 0.5) * (2.0 * child_width)
    other_center = jnp.zeros_like(target_one)
    return (
        target_one,
        target_two,
        1,
        (low_center, high_center, parent_center),
        child_width / 2,
        other_center,
        extent / 2,
    )


def pair_level(current, partner, level_index, box_code, targets, layout_fn, speed_modes):
    own_bit = box_code // 2**level_index % 2
    child_low = jnp.where(own_bit == 0, current, partner)
    child_high = jnp.where(own_bit == 0, partner, current)
    box_codes = jnp.zeros_like(targets) + box_code
    return merge_children(
        child_low, child_high, layout_fn(level_index, box_codes, targets), speed_modes
    )


def on_device(weights, speed_modes):
    current = weights.reshape(weights.shape[2:])
    pair_count = current.shape[3]
    core_count = lax.axis_size("cores")
    src_x = lax.axis_size("bx") * core_count
    src_y = lax.axis_size("by")
    x_bits = src_x.bit_length() - 1
    y_bits = src_y.bit_length() - 1
    x_code = lax.axis_index("bx") * core_count + lax.axis_index("cores")
    y_box = lax.axis_index("by")
    geometry = (float(N), TGT, src_x, src_y)
    targets = jnp.arange(pair_count, dtype=jnp.int32)
    first_layout = partial(x_layout, y_box=y_box, geometry=geometry)
    second_layout = partial(y_layout, x_code=x_code, x_bits=x_bits, geometry=geometry)
    for level_index in range(x_bits):
        if level_index == 0:
            partner = partner_2(current, "cores", 0)
        else:
            partner = partner_2(current, "bx", level_index - 1)
        current = pair_level(
            current, partner, level_index, x_code, targets, first_layout, speed_modes
        )
    for level_index in range(y_bits):
        partner = partner_2(current, "by", level_index)
        current = pair_level(
            current, partner, level_index, y_box, targets, second_layout, speed_modes
        )
    return current.reshape(weights.shape)


SIN_HALF = (4.442879586386342, -7.3078180422392816, 3.597788667381583, -0.7912380409231197)
COS_HALF = (
    1.4142134965636117,
    -6.978850988059019,
    5.739461167077472,
    -1.883562964211867,
    0.3106981455985473,
)
CHUNKS = 2
PIECES = 16
LEVEL_ROWS = (0, 256, 384, 448, 480)
VMEM_LIMIT = 48 * 2**20


def node_tables():
    points = cheb_nodes(16).astype(np.float32)
    nodes = []
    for level_index in range(5):
        width = np.float32(N * 2**level_index / 16)
        for box in range(16 >> level_index):
            center = np.float32(-N / 2 + (box + 0.5) * width)
            nodes.append(center + (width / 2) * points)
    nodes = np.concatenate(nodes).astype(np.float32)
    sub = np.arange(8)
    lane = np.arange(128)
    half = (sub // 4)[:, None] + 0 * lane[None, :]
    second = (lane // 32 * 4)[None, :] + (sub % 4)[:, None]
    wave_two = (-N / 2 + (half + 0.5) * (N / 2)).astype(np.float32) + np.float32(N / 4) * points[second]
    wave_two = wave_two.astype(np.float32)
    lengths = np.sqrt(nodes[:, None, None] * nodes[:, None, None] + wave_two * wave_two)
    return nodes, wave_two, lengths.astype(np.float32)


def final_tables():
    points = cheb_nodes(16).astype(np.float32) * np.float32(N / 2)
    lane = np.arange(128)
    one = np.broadcast_to(points.reshape(2, 8, 1), (2, 8, 128)).astype(np.float32)
    two = np.stack([np.broadcast_to(points[lane // 32 * 4 + a], (8, 128)) for a in range(4)])
    two = two.astype(np.float32)
    lengths = np.sqrt((one * one)[:, None] + (two * two)[None, :]).astype(np.float32)
    return np.array(one), two, lengths


def in_two_parts(table):
    high = table.astype(ml_dtypes.bfloat16)
    low = (table - high.astype(np.float32)).astype(ml_dtypes.bfloat16)
    return high, low


def first_weights():
    table = lagrange_table(16).astype(np.float32)
    high, low = in_two_parts(np.kron(table, np.eye(8, dtype=np.float32)))
    return np.concatenate([high, low])


def second_weights():
    table = lagrange_table(16)
    result = np.zeros((8, 4, 32, 4, 4, 32), np.float32)
    same = np.eye(32, dtype=np.float32)
    for half in range(2):
        for a in range(4):
            for b in range(4):
                for out_a in range(4):
                    for out_b in range(4):
                        weight = table[4 * out_b + out_a, half * 16 + 4 * b + a]
                        result[half * 4 + a, b, :, out_a, out_b, :] = np.float32(weight) * same
    return np.stack(in_two_parts(result.reshape(4, 256, 512)))


def turn(phase):
    part = phase - jnp.round(phase)
    square = part * part
    sine = SIN_HALF[3]
    for coefficient in SIN_HALF[2::-1]:
        sine = sine * square + coefficient
    sine = sine * part
    cosine = COS_HALF[4]
    for coefficient in COS_HALF[3::-1]:
        cosine = cosine * square + coefficient
    return 1.0 - sine * sine, sine * cosine


def swap_lanes(values):
    lane = lax.broadcasted_iota(jnp.int32, (8, 128), 1)
    low = lane < 64
    even = lane // 32 % 2 == 0
    half = [None] * 4
    for b in range(2):
        half[b] = jnp.where(low, values[b], pltpu.roll(values[b + 2], 64, 1))
        half[b + 2] = jnp.where(low, pltpu.roll(values[b], 64, 1), values[b + 2])
    full = [None] * 4
    for j in (0, 2):
        full[j] = jnp.where(even, half[j], pltpu.roll(half[j + 1], 32, 1))
        full[j + 1] = jnp.where(even, pltpu.roll(half[j], 96, 1), half[j + 1])
    return full


def pack_rows(in_ref, lanes, tiles):
    upper = lax.broadcasted_iota(jnp.int32, (8, 128), 0) < 4
    for t1 in range(16):
        groups = [None] * 4
        for high in range(2):
            real = in_ref[0, t1, 8 * high : 8 * high + 8, lanes]
            imag = in_ref[1, t1, 8 * high : 8 * high + 8, lanes]
            groups[2 * high] = jnp.where(upper, real, pltpu.roll(imag, 4, 0))
            groups[2 * high + 1] = jnp.where(upper, pltpu.roll(real, 4, 0), imag)
        for j, tile in enumerate(swap_lanes(groups)):
            tiles[j, t1] = tile


def pack_kernel(chunk, in_ref, out_ref, held, arrived):
    group = pl.program_id(0)

    def fetch(place):
        lanes = pl.ds((4 * chunk + place) * 128, 128)
        return pltpu.make_async_copy(
            in_ref.at[:, :, :, lanes], held.at[place], arrived.at[place]
        )

    @pl.when(group == 0)
    def _():
        for place in range(4):
            fetch(place).start()

    for place in range(4):

        @pl.when(group == place)
        def _(place=place):
            fetch(place).wait()

    pack_rows(held.at[group], slice(None), out_ref)


def pack(weights, chunk):
    return pl.pallas_call(
        partial(pack_kernel, chunk),
        grid=(4,),
        in_specs=[pl.BlockSpec(memory_space=pl.ANY)],
        out_specs=pl.BlockSpec((4, 16, 8, 128), lambda i: (i, 0, 0, 0)),
        out_shape=jax.ShapeDtypeStruct((PIECES, 16, 8, 128), jnp.float32),
        scratch_shapes=[pltpu.VMEM((4, 2, 16, 16, 128), jnp.float32), pltpu.SemaphoreType.DMA((4,))],
        cost_estimate=pl.CostEstimate(flops=10**6, bytes_accessed=2**21, transcendentals=0),
        name="pack",
    )(weights)


def merge_halves(out_ref, box, t1, low, high):
    upper = lax.broadcasted_iota(jnp.int32, (8, 128), 0) < 4
    out_ref[box, 0, t1] = jnp.where(upper, low, pltpu.roll(high, 4, 0))
    out_ref[box, 1, t1] = jnp.where(upper, pltpu.roll(low, 4, 0), high)


def join_kernel(in_ref, *refs):
    out_ref = refs[-1]

    def step(box, carry):
        for t1 in range(16):
            merge_halves(out_ref, box, t1, in_ref[2 * box, t1], in_ref[2 * box + 1, t1])
        return carry

    lax.fori_loop(0, 8, step, 0)


def join(received):
    in_vmem = pl.BlockSpec(memory_space=pltpu.VMEM)
    return pl.pallas_call(
        join_kernel,
        in_specs=[in_vmem],
        out_specs=in_vmem,
        out_shape=jax.ShapeDtypeStruct((8, 2, 16, 8, 128), jnp.float32),
        compiler_params=pltpu.CompilerParams(vmem_limit_bytes=VMEM_LIMIT),
        cost_estimate=pl.CostEstimate(flops=10**6, bytes_accessed=2**21, transcendentals=0),
        name="join",
    )(received)


def levels_kernel(
    chunk, ids, nodes, own, other, speeds, waves, lengths, last_one, last_two,
    last_lengths, first_table, second_table, *refs,
):
    outs = refs[0]
    boxes_a, boxes_b, sums, turned, mixed, last_phase = refs[-6:]
    row = (chunk * PIECES + ids[0]).astype(jnp.float32)
    core = ids[1]
    core_float = core.astype(jnp.float32)
    wave_two = waves[...]
    lane = lax.broadcasted_iota(jnp.int32, (8, 128), 1)
    along_two = ((lane % 32).astype(jnp.float32) + 0.5) * (1.0 / 32)
    second_phase = along_two * wave_two

    def first_point(level_index, low_code):
        span = 2.0 ** (level_index + 1)
        code = core_float * 2.0**level_index + low_code
        return (row * span + code + 0.5) * (1.0 / (32 * span))

    def speed_row(level_index, low_code):
        return jnp.broadcast_to(speeds[pl.ds(2**level_index - 1 + low_code, 1), :], (8, 128))

    def blend(slot, target, boxes):
        rows = sums[slot].astype(jnp.bfloat16)
        both = jnp.dot(first_table[...], rows, preferred_element_type=jnp.float32)
        total = both[:128] + both[128:]
        for n, box in enumerate(boxes):
            for part in range(2):
                column = 128 * (2 * n + part)
                target[box, part] = total[:, column : column + 128].reshape(16, 8, 128)

    def put(slot, first_row, column, real, imag):
        sums[slot, pl.ds(first_row, 8), 256 * column : 256 * column + 128] = real
        sums[slot, pl.ds(first_row, 8), 256 * column + 128 : 256 * column + 256] = imag

    def first_level(pair, slot):
        point = first_point(0, 0.0)
        speed = speed_row(0, 0)
        for n in range(2):
            box = 2 * pair + n
            for source, child in ((own, core), (other, 1 - core)):
                for t1 in range(16):
                    entry = (2 * box + child) * 16 + t1
                    phase = (point * nodes[entry] + second_phase) + speed * lengths[entry]
                    cosine, sine = turn(phase)
                    real = source[box, 0, t1]
                    imag = source[box, 1, t1]
                    first_row = pl.multiple_of(child * 128 + 8 * t1, 8)
                    put(slot, first_row, n, real * cosine + imag * sine, imag * cosine - real * sine)
        blend(slot, boxes_a, [2 * pair, 2 * pair + 1])

    def later_level(level_index, source, target, index, slot):
        low_bits = level_index - 1
        stride = 2**low_bits
        parent = index // stride
        low = index % stride
        code = jnp.int32(0)
        for bit in range(low_bits):
            code = code + low // 2**bit % 2 * 2 ** (low_bits - 1 - bit)
        before = first_point(level_index - 1, code.astype(jnp.float32))
        before_speed = speed_row(level_index - 1, code)
        points = [first_point(level_index, (2 * code + b).astype(jnp.float32)) for b in range(2)]
        point_speeds = [speed_row(level_index, 2 * code + b) for b in range(2)]
        first_box = parent * (2 * stride) + low
        for child in range(2):
            for t1 in range(16):
                entry = LEVEL_ROWS[level_index] + (2 * parent + child) * 16 + t1
                length = lengths[entry]
                wave = nodes[entry]
                real = source[first_box + child * stride, 0, t1]
                imag = source[first_box + child * stride, 1, t1]
                old = (before * wave + second_phase) + before_speed * length
                for b in range(2):
                    new = (points[b] * wave + second_phase) + point_speeds[b] * length
                    cosine, sine = turn(new - old)
                    first_row = child * 128 + 8 * t1
                    put(slot, first_row, b, real * cosine + imag * sine, imag * cosine - real * sine)
        blend(slot, target, [first_box, first_box + stride])

    def in_pairs(one):
        def step(half, carry):
            for slot in range(2):
                one(2 * half + slot, slot)
            return carry

        lax.fori_loop(0, 2, step, 0)

    in_pairs(first_level)
    in_pairs(partial(later_level, 1, boxes_a, boxes_b))
    in_pairs(partial(later_level, 2, boxes_b, boxes_a))
    in_pairs(partial(later_level, 3, boxes_a, boxes_b))

    fine_two = [((lane % 32).astype(jnp.float32) * 2.0 + (e + 0.5)) * (1.0 / 64) for e in range(2)]
    fine_phase = [fine_two[e] * wave_two for e in range(2)]

    def reversed_code(box):
        return box % 2 * 4 + box // 2 % 2 * 2 + box // 4

    def fine_speed(code, e):
        return jnp.broadcast_to(speeds[pl.ds(15 + 2 * code + e, 1), :], (8, 128))

    def rotate_box(box, carry):
        code = reversed_code(box)
        point = first_point(3, code.astype(jnp.float32))
        old_speed = speed_row(3, code)
        new_speeds = [fine_speed(code, e) for e in range(2)]
        for t1 in range(16):
            entry = LEVEL_ROWS[4] + t1
            length = lengths[entry]
            across = point * nodes[entry]
            real = boxes_b[box, 0, t1]
            imag = boxes_b[box, 1, t1]
            old = (across + second_phase) + old_speed * length
            for e in range(2):
                new = (across + fine_phase[e]) + new_speeds[e] * length
                cosine, sine = turn(new - old)
                first = pl.multiple_of((e * 256 + box * 32 + t1) * 8, 8)
                turned[pl.ds(first, 8), :] = real * cosine + imag * sine
                turned[pl.ds(first + 128, 8), :] = imag * cosine - real * sine
        return carry

    lax.fori_loop(0, 8, rotate_box, 0)

    for e in range(2):
        for a in range(4):
            last_phase[e, a] = fine_two[e] * last_two[a]

    total = None
    for j in range(4):
        rows = jnp.concatenate(
            [turned[pl.ds(2 * j + k, 512, stride=8), :] for k in range(2)], axis=1
        ).astype(jnp.bfloat16)
        for part in range(2):
            term = jnp.dot(rows, second_table[part, j], preferred_element_type=jnp.float32)
            total = term if total is None else total + term
    mixed[...] = total

    def finish_box(target, out):
        box, e = target // 2, target % 2
        code = reversed_code(box)
        point = first_point(3, code.astype(jnp.float32))
        speed = fine_speed(code, e)
        for high in range(2):
            across = point * last_one[high]
            first = pl.multiple_of(e * 256 + box * 32 + high * 8, 8)
            for a in range(4):
                phase = (across + last_phase[e, a]) + speed * last_lengths[high, a]
                cosine, sine = turn(phase)
                real = mixed[pl.ds(first, 8), 128 * a : 128 * a + 128]
                imag = mixed[pl.ds(first + 16, 8), 128 * a : 128 * a + 128]
                out[high * 4 + a] = real * cosine - imag * sine
                out[8 + high * 4 + a] = real * sine + imag * cosine

    def finish_row(major, carry):
        for minor in range(4):
            finish_box(4 * major + minor, outs.at[4 * major + minor])
        return carry

    lax.fori_loop(0, 4, finish_row, 0)


def levels(chunk, ids, own, other, speeds):
    nodes, waves, lengths = node_tables()
    last_one, last_two, last_lengths = final_tables()
    tables = (waves, lengths, last_one, last_two, last_lengths, first_weights(), second_weights())
    in_vmem = pl.BlockSpec(memory_space=pltpu.VMEM)
    in_smem = pl.BlockSpec(memory_space=pltpu.SMEM)
    return pl.pallas_call(
        partial(levels_kernel, chunk),
        in_specs=[in_smem, in_smem] + [in_vmem] * 10,
        out_specs=in_vmem,
        out_shape=jax.ShapeDtypeStruct((PIECES, 16, 8, 128), jnp.float32),
        scratch_shapes=[
            pltpu.VMEM((8, 2, 16, 8, 128), jnp.float32),
            pltpu.VMEM((8, 2, 16, 8, 128), jnp.float32),
            pltpu.VMEM((2, 256, 512), jnp.float32),
            pltpu.VMEM((4096, 128), jnp.float32),
            pltpu.VMEM((512, 512), jnp.float32),
            pltpu.VMEM((2, 4, 8, 128), jnp.float32),
        ],
        compiler_params=pltpu.CompilerParams(vmem_limit_bytes=VMEM_LIMIT),
        cost_estimate=pl.CostEstimate(flops=10**8, bytes_accessed=2**23, transcendentals=0),
        name="levels",
    )(ids, jnp.asarray(nodes), own, other, speeds, *[jnp.asarray(table) for table in tables])


def unpack_rows(tiles, rows, out_ref, lanes):
    for part in range(2):
        for high in range(2):
            block = part * 2 + high
            for a in range(4):
                values = [tiles[j, part * 8 + high * 4 + a] for j in range(4)]
                for b, tile in enumerate(swap_lanes(values)):
                    t2 = 4 * b + a
                    rows[block, 8 * t2 : 8 * t2 + 8, :] = tile
            for t1 in range(8):
                out_ref[part, high * 8 + t1, :, lanes] = rows[block, pl.ds(t1, 16, stride=8), :]


def unpack_kernel(*refs):
    unpack_rows(refs[0], refs[-1], refs[-2], slice(None))


def unpack(received, chunk, earlier):
    operands = [received]
    in_specs = [pl.BlockSpec((4, 16, 8, 128), lambda i: (i, 0, 0, 0))]
    aliases = {}
    if earlier is not None:
        aliases = {1: 0}
        operands.append(earlier)
        in_specs.append(pl.BlockSpec(memory_space=pl.ANY))
    return pl.pallas_call(
        unpack_kernel,
        grid=(4,),
        in_specs=in_specs,
        out_specs=pl.BlockSpec((2, 16, 16, 128), lambda i: (0, 0, 0, 4 * chunk + i)),
        out_shape=jax.ShapeDtypeStruct((2, 16, 16, 1024), jnp.float32),
        scratch_shapes=[pltpu.VMEM((4, 128, 128), jnp.float32)],
        input_output_aliases=aliases,
        cost_estimate=pl.CostEstimate(flops=10**6, bytes_accessed=2**21, transcendentals=0),
        name="unpack",
    )(*operands)


def speed_tables(speed_modes, core):
    numerators, spans = [], []
    for level_index in range(4):
        for code in range(2**level_index):
            numerators.append(core * 2**level_index + code)
            spans.append(2 ** (level_index + 1))
    for code in range(8):
        for e in range(2):
            numerators.append(core * 8 + code)
            spans.append(16)
    codes = jnp.stack(numerators).astype(jnp.float32)
    spans = jnp.asarray(np.array(spans), jnp.float32)
    me = lax.axis_index("bx") * 2 + lax.axis_index("by")
    rows = (jnp.arange(CHUNKS) * PIECES + me).astype(jnp.float32)
    target_one = (rows[:, None] * spans + codes + 0.5) / (TGT * spans)
    columns = jnp.arange(32).astype(jnp.float32)
    coarse = jnp.broadcast_to((columns + 0.5) / TGT, (15, 32))
    fine = jnp.stack([(2 * columns + e + 0.5) / (2 * TGT) for e in range(2)])
    target_two = jnp.concatenate([coarse, jnp.tile(fine, (8, 1))])
    target_one = jnp.broadcast_to(target_one[:, :, None], (CHUNKS, 31, 32))
    target_two = jnp.broadcast_to(target_two[None], (CHUNKS, 31, 32))
    speed = speed_of(speed_modes, target_one.reshape(-1), target_two.reshape(-1))
    return jnp.tile(speed.reshape(CHUNKS, 31, 32), (1, 1, 4))


def on_device_dealt(weights, speed_modes):
    local = weights.reshape(weights.shape[2:])
    core = lax.axis_index("cores")
    me = lax.axis_index("bx") * 2 + lax.axis_index("by")
    ids = jnp.stack([me, core]).astype(jnp.int32)
    speeds = speed_tables(speed_modes, core)

    received = [deal(pack(local, chunk)) for chunk in range(CHUNKS)]
    results = []
    for chunk in range(CHUNKS):
        own = join(received[chunk])
        other = partner_2(own, "cores", 0)
        results.append(deal(levels(chunk, ids, own, other, speeds[chunk])))
    out = None
    for chunk in range(CHUNKS):
        out = unpack(results[chunk], chunk, out)
    return out.reshape(weights.shape)


def deal(pieces):
    return lax.all_to_all(pieces, ("bx", "by"), 0, 0, tiled=True)


def solution(mesh):
    sizes = dict(mesh.shape)
    spec = P(("bx", "cores"), "by", None, None, None, None)
    dealt = (sizes["bx"], sizes["by"], sizes["cores"]) == (8, 2, 2)

    def whole(weights, speed_modes):
        fits = dealt and weights.shape[2:] == (2, 16, 16, 1024)
        return jax.shard_map(
            on_device_dealt if fits else on_device,
            mesh=mesh,
            in_specs=(spec, P()),
            out_specs=spec,
            check_vma=False,
        )(weights, speed_modes)

    return whole
```

```python
from functools import partial
import math

import jax
import jax.numpy as jnp
import ml_dtypes
import numpy as np
from jax import lax
from jax.experimental import pallas as pl
from jax.experimental.pallas import tpu as pltpu
from jax.sharding import PartitionSpec as P

N = 8192
TGT = 32


def partner_2(value, axis, apart):
    mask = 2**apart
    pairs = [(source, source ^ mask) for source in range(lax.axis_size(axis))]
    return lax.ppermute(value, axis, pairs)


def cheb_nodes(degree):
    return np.cos(np.pi * (2 * np.arange(degree) + 1) / (2 * degree))


def lagrange_table(degree):
    points = cheb_nodes(degree)
    result = np.ones((degree, 2 * degree))
    for child_side in range(2):
        inside = (points + 2 * child_side - 1) / 2
        for node_row in range(degree):
            for node_other in range(degree):
                if node_other != node_row:
                    result[node_row, child_side * degree : (child_side + 1) * degree] *= (
                        inside - points[node_other]
                    ) / (points[node_row] - points[node_other])
    return result


def speed_of(speed_modes, target_one, target_two):
    mode_count = speed_modes.shape[0]
    frequencies = jnp.arange(mode_count).astype(jnp.float32) * math.pi
    along_one = jnp.cos(frequencies[:, None] * target_one[None, :])
    along_two = jnp.cos(frequencies[:, None] * target_two[None, :])
    blended = jnp.dot(
        speed_modes, along_two, preferred_element_type=jnp.float32, precision=lax.Precision.HIGHEST
    )
    return 1.0 + jnp.sum(blended * along_one, axis=0)


def rotation(target_one, target_two, speed_value, wave_one, wave_two):
    phase = (
        target_one * wave_one
        + target_two * wave_two
        + speed_value * jnp.sqrt(wave_one * wave_one + wave_two * wave_two)
    )
    phase = phase - jnp.floor(phase)
    angle = 2.0 * math.pi * phase
    return (jnp.cos(angle), jnp.sin(angle))


def node_phase(layout, speed_value, center, half_width, degree):
    target_one, target_two, merge_dim, centers, child_half, other_center, other_half = layout
    points = jnp.asarray(cheb_nodes(degree), jnp.float32)
    merged = center[None, :] + half_width * points[:, None]
    across = other_center[None, :] + other_half * points[:, None]
    if merge_dim == 0:
        return rotation(target_one, target_two, speed_value, merged[:, None, :], across[None, :, :])
    return rotation(target_one, target_two, speed_value, across[:, None, :], merged[None, :, :])


def merge_children(child_low, child_high, layout, speed_modes):
    target_one, target_two, merge_dim, centers, child_half, other_center, other_half = layout
    degree = child_low.shape[1]
    speed_value = speed_of(speed_modes, target_one, target_two)
    lagrange = jnp.asarray(lagrange_table(degree), jnp.float32)
    pieces = []
    for child, center in ((child_low, centers[0]), (child_high, centers[1])):
        cosine, sine_part = node_phase(layout, speed_value, center, child_half, degree)
        real_part = child[0] * cosine + child[1] * sine_part
        imag_part = child[1] * cosine - child[0] * sine_part
        pieces.append(jnp.stack([real_part, imag_part]))
    stacked = jnp.concatenate(pieces, axis=1 + merge_dim)
    if merge_dim == 0:
        blended = jnp.einsum("ij,rjks->riks", lagrange, stacked, precision=lax.Precision.HIGHEST)
    else:
        blended = jnp.einsum("kj,rijs->riks", lagrange, stacked, precision=lax.Precision.HIGHEST)
    cosine, sine_part = node_phase(layout, speed_value, centers[2], 2.0 * child_half, degree)
    return jnp.stack(
        [blended[0] * cosine - blended[1] * sine_part, blended[0] * sine_part + blended[1] * cosine]
    )


def reversed_bits(box_code, bit_count):
    result = jnp.zeros_like(box_code)
    for bit_place in range(bit_count):
        result = result + box_code // 2**bit_place % 2 * 2 ** (bit_count - 1 - bit_place)
    return result


def x_layout(level_index, box_code, targets, y_box, geometry):
    extent, side_count, src_x, src_y = geometry
    span_size = 2 ** (level_index + 1)
    row_index = targets // side_count * span_size + reversed_bits(box_code, level_index + 1)
    target_one = (row_index.astype(jnp.float32) + 0.5) / (side_count * span_size)
    target_two = ((targets % side_count).astype(jnp.float32) + 0.5) / side_count
    parent = (box_code // span_size).astype(jnp.float32)
    child_width = extent * 2**level_index / src_x
    low_center = -extent / 2 + (2.0 * parent + 0.5) * child_width
    high_center = low_center + child_width
    parent_center = -extent / 2 + (parent + 0.5) * (2.0 * child_width)
    other_center = jnp.zeros_like(target_one) + (
        -extent / 2 + (jnp.asarray(y_box).astype(jnp.float32) + 0.5) * (extent / src_y)
    )
    return (
        target_one,
        target_two,
        0,
        (low_center, high_center, parent_center),
        child_width / 2,
        other_center,
        extent / (2 * src_y),
    )


def y_layout(level_index, box_code, targets, x_code, x_bits, geometry):
    extent, side_count, src_x, src_y = geometry
    span_size = 2 ** (level_index + 1)
    col_index = targets % side_count * span_size + reversed_bits(box_code, level_index + 1)
    target_two = (col_index.astype(jnp.float32) + 0.5) / (side_count * span_size)
    row_index = targets // side_count * src_x + reversed_bits(x_code, x_bits)
    target_one = (row_index.astype(jnp.float32) + 0.5) / (side_count * src_x)
    parent = (box_code // span_size).astype(jnp.float32)
    child_width = extent * 2**level_index / src_y
    low_center = -extent / 2 + (2.0 * parent + 0.5) * child_width
    high_center = low_center + child_width
    parent_center = -extent / 2 + (parent + 0.5) * (2.0 * child_width)
    other_center = jnp.zeros_like(target_one)
    return (
        target_one,
        target_two,
        1,
        (low_center, high_center, parent_center),
        child_width / 2,
        other_center,
        extent / 2,
    )


def pair_level(current, partner, level_index, box_code, targets, layout_fn, speed_modes):
    own_bit = box_code // 2**level_index % 2
    child_low = jnp.where(own_bit == 0, current, partner)
    child_high = jnp.where(own_bit == 0, partner, current)
    box_codes = jnp.zeros_like(targets) + box_code
    return merge_children(
        child_low, child_high, layout_fn(level_index, box_codes, targets), speed_modes
    )


def on_device(weights, speed_modes):
    current = weights.reshape(weights.shape[2:])
    pair_count = current.shape[3]
    core_count = lax.axis_size("cores")
    src_x = lax.axis_size("bx") * core_count
    src_y = lax.axis_size("by")
    x_bits = src_x.bit_length() - 1
    y_bits = src_y.bit_length() - 1
    x_code = lax.axis_index("bx") * core_count + lax.axis_index("cores")
    y_box = lax.axis_index("by")
    geometry = (float(N), TGT, src_x, src_y)
    targets = jnp.arange(pair_count, dtype=jnp.int32)
    first_layout = partial(x_layout, y_box=y_box, geometry=geometry)
    second_layout = partial(y_layout, x_code=x_code, x_bits=x_bits, geometry=geometry)
    for level_index in range(x_bits):
        if level_index == 0:
            partner = partner_2(current, "cores", 0)
        else:
            partner = partner_2(current, "bx", level_index - 1)
        current = pair_level(
            current, partner, level_index, x_code, targets, first_layout, speed_modes
        )
    for level_index in range(y_bits):
        partner = partner_2(current, "by", level_index)
        current = pair_level(
            current, partner, level_index, y_box, targets, second_layout, speed_modes
        )
    return current.reshape(weights.shape)


SIN_HALF = (4.442879586386342, -7.3078180422392816, 3.597788667381583, -0.7912380409231197)
COS_HALF = (
    1.4142134965636117,
    -6.978850988059019,
    5.739461167077472,
    -1.883562964211867,
    0.3106981455985473,
)
CHUNKS = 2
PIECES = 16
LEVEL_ROWS = (0, 256, 384, 448, 480)
VMEM_LIMIT = 48 * 2**20


def node_tables():
    points = cheb_nodes(16).astype(np.float32)
    nodes = []
    for level_index in range(5):
        width = np.float32(N * 2**level_index / 16)
        for box in range(16 >> level_index):
            center = np.float32(-N / 2 + (box + 0.5) * width)
            nodes.append(center + (width / 2) * points)
    nodes = np.concatenate(nodes).astype(np.float32)
    sub = np.arange(8)
    lane = np.arange(128)
    half = (sub // 4)[:, None] + 0 * lane[None, :]
    second = (lane // 32 * 4)[None, :] + (sub % 4)[:, None]
    wave_two = (-N / 2 + (half + 0.5) * (N / 2)).astype(np.float32) + np.float32(N / 4) * points[second]
    wave_two = wave_two.astype(np.float32)
    lengths = np.sqrt(nodes[:, None, None] * nodes[:, None, None] + wave_two * wave_two)
    return nodes, wave_two, lengths.astype(np.float32)


def final_tables():
    points = cheb_nodes(16).astype(np.float32) * np.float32(N / 2)
    lane = np.arange(128)
    one = np.broadcast_to(points.reshape(2, 8, 1), (2, 8, 128)).astype(np.float32)
    two = np.stack([np.broadcast_to(points[lane // 32 * 4 + a], (8, 128)) for a in range(4)])
    two = two.astype(np.float32)
    lengths = np.sqrt((one * one)[:, None] + (two * two)[None, :]).astype(np.float32)
    return np.array(one), two, lengths


def in_two_parts(table):
    high = table.astype(ml_dtypes.bfloat16)
    low = (table - high.astype(np.float32)).astype(ml_dtypes.bfloat16)
    return high, low


def first_weights():
    table = lagrange_table(16).astype(np.float32)
    high, low = in_two_parts(np.kron(table, np.eye(8, dtype=np.float32)))
    return np.concatenate([high, low])


def second_weights():
    table = lagrange_table(16)
    result = np.zeros((8, 4, 32, 4, 4, 32), np.float32)
    same = np.eye(32, dtype=np.float32)
    for half in range(2):
        for a in range(4):
            for b in range(4):
                for out_a in range(4):
                    for out_b in range(4):
                        weight = table[4 * out_b + out_a, half * 16 + 4 * b + a]
                        result[half * 4 + a, b, :, out_a, out_b, :] = np.float32(weight) * same
    return np.stack(in_two_parts(result.reshape(4, 256, 512)))


def turn(phase):
    part = phase - jnp.round(phase)
    square = part * part
    sine = SIN_HALF[3]
    for coefficient in SIN_HALF[2::-1]:
        sine = sine * square + coefficient
    sine = sine * part
    cosine = COS_HALF[4]
    for coefficient in COS_HALF[3::-1]:
        cosine = cosine * square + coefficient
    return 1.0 - sine * sine, sine * cosine


def swap_lanes(values):
    lane = lax.broadcasted_iota(jnp.int32, (8, 128), 1)
    low = lane < 64
    even = lane // 32 % 2 == 0
    half = [None] * 4
    for b in range(2):
        half[b] = jnp.where(low, values[b], pltpu.roll(values[b + 2], 64, 1))
        half[b + 2] = jnp.where(low, pltpu.roll(values[b], 64, 1), values[b + 2])
    full = [None] * 4
    for j in (0, 2):
        full[j] = jnp.where(even, half[j], pltpu.roll(half[j + 1], 32, 1))
        full[j + 1] = jnp.where(even, pltpu.roll(half[j], 96, 1), half[j + 1])
    return full


def pack_rows(in_ref, lanes, tiles):
    upper = lax.broadcasted_iota(jnp.int32, (8, 128), 0) < 4

    def step(quarter, carry):
        for place in range(4):
            t1 = 4 * quarter + place
            groups = [None] * 4
            for high in range(2):
                real = in_ref[0, t1, 8 * high : 8 * high + 8, lanes]
                imag = in_ref[1, t1, 8 * high : 8 * high + 8, lanes]
                groups[2 * high] = jnp.where(upper, real, pltpu.roll(imag, 4, 0))
                groups[2 * high + 1] = jnp.where(upper, pltpu.roll(real, 4, 0), imag)
            for j, tile in enumerate(swap_lanes(groups)):
                tiles[j, t1] = tile
        return carry

    lax.fori_loop(0, 4, step, 0)


def pack_kernel(chunk, in_ref, out_ref, held, arrived):
    group = pl.program_id(0)

    def fetch(place):
        lanes = pl.ds((4 * chunk + place) * 128, 128)
        return pltpu.make_async_copy(
            in_ref.at[:, :, :, lanes], held.at[place], arrived.at[place]
        )

    @pl.when(group == 0)
    def _():
        for place in range(4):
            fetch(place).start()

    for place in range(4):

        @pl.when(group == place)
        def _(place=place):
            fetch(place).wait()

    pack_rows(held.at[group], slice(None), out_ref)


def pack(weights, chunk):
    return pl.pallas_call(
        partial(pack_kernel, chunk),
        grid=(4,),
        in_specs=[pl.BlockSpec(memory_space=pl.ANY)],
        out_specs=pl.BlockSpec((4, 16, 8, 128), lambda i: (i, 0, 0, 0)),
        out_shape=jax.ShapeDtypeStruct((PIECES, 16, 8, 128), jnp.float32),
        scratch_shapes=[pltpu.VMEM((4, 2, 16, 16, 128), jnp.float32), pltpu.SemaphoreType.DMA((4,))],
        cost_estimate=pl.CostEstimate(flops=10**6, bytes_accessed=2**21, transcendentals=0),
        name="pack",
    )(weights)


def merge_halves(out_ref, box, t1, low, high):
    upper = lax.broadcasted_iota(jnp.int32, (8, 128), 0) < 4
    out_ref[box, 0, t1] = jnp.where(upper, low, pltpu.roll(high, 4, 0))
    out_ref[box, 1, t1] = jnp.where(upper, pltpu.roll(low, 4, 0), high)


def join_kernel(in_ref, *refs):
    out_ref = refs[-1]

    def step(box, carry):
        for t1 in range(16):
            merge_halves(out_ref, box, t1, in_ref[2 * box, t1], in_ref[2 * box + 1, t1])
        return carry

    lax.fori_loop(0, 8, step, 0)


def join(received):
    in_vmem = pl.BlockSpec(memory_space=pltpu.VMEM)
    return pl.pallas_call(
        join_kernel,
        in_specs=[in_vmem],
        out_specs=in_vmem,
        out_shape=jax.ShapeDtypeStruct((8, 2, 16, 8, 128), jnp.float32),
        compiler_params=pltpu.CompilerParams(vmem_limit_bytes=VMEM_LIMIT),
        cost_estimate=pl.CostEstimate(flops=10**6, bytes_accessed=2**21, transcendentals=0),
        name="join",
    )(received)


def levels_kernel(
    chunk, ids, nodes, own, other, speeds, waves, lengths, last_one, last_two,
    last_lengths, first_table, second_table, *refs,
):
    outs = refs[0]
    boxes_a, boxes_b, sums, turned, mixed, last_phase = refs[-6:]
    row = (chunk * PIECES + ids[0]).astype(jnp.float32)
    core = ids[1]
    core_float = core.astype(jnp.float32)
    wave_two = waves[...]
    lane = lax.broadcasted_iota(jnp.int32, (8, 128), 1)
    along_two = ((lane % 32).astype(jnp.float32) + 0.5) * (1.0 / 32)
    second_phase = along_two * wave_two

    def first_point(level_index, low_code):
        span = 2.0 ** (level_index + 1)
        code = core_float * 2.0**level_index + low_code
        return (row * span + code + 0.5) * (1.0 / (32 * span))

    def speed_row(level_index, low_code):
        return jnp.broadcast_to(speeds[pl.ds(2**level_index - 1 + low_code, 1), :], (8, 128))

    def blend(slot, target, boxes):
        rows = sums[slot].astype(jnp.bfloat16)
        both = jnp.dot(first_table[...], rows, preferred_element_type=jnp.float32)
        total = both[:128] + both[128:]
        for n, box in enumerate(boxes):
            for part in range(2):
                column = 128 * (2 * n + part)
                target[box, part] = total[:, column : column + 128].reshape(16, 8, 128)

    def put(slot, first_row, column, real, imag):
        sums[slot, pl.ds(first_row, 8), 256 * column : 256 * column + 128] = real
        sums[slot, pl.ds(first_row, 8), 256 * column + 128 : 256 * column + 256] = imag

    def first_level(pair, slot):
        point = first_point(0, 0.0)
        speed = speed_row(0, 0)
        for n in range(2):
            box = 2 * pair + n
            for source, child in ((own, core), (other, 1 - core)):
                for t1 in range(16):
                    entry = (2 * box + child) * 16 + t1
                    phase = (point * nodes[entry] + second_phase) + speed * lengths[entry]
                    cosine, sine = turn(phase)
                    real = source[box, 0, t1]
                    imag = source[box, 1, t1]
                    first_row = pl.multiple_of(child * 128 + 8 * t1, 8)
                    put(slot, first_row, n, real * cosine + imag * sine, imag * cosine - real * sine)
        blend(slot, boxes_a, [2 * pair, 2 * pair + 1])

    def later_level(level_index, source, target, index, slot):
        low_bits = level_index - 1
        stride = 2**low_bits
        parent = index // stride
        low = index % stride
        code = jnp.int32(0)
        for bit in range(low_bits):
            code = code + low // 2**bit % 2 * 2 ** (low_bits - 1 - bit)
        before = first_point(level_index - 1, code.astype(jnp.float32))
        before_speed = speed_row(level_index - 1, code)
        points = [first_point(level_index, (2 * code + b).astype(jnp.float32)) for b in range(2)]
        point_speeds = [speed_row(level_index, 2 * code + b) for b in range(2)]
        first_box = parent * (2 * stride) + low
        for child in range(2):
            for t1 in range(16):
                entry = LEVEL_ROWS[level_index] + (2 * parent + child) * 16 + t1
                length = lengths[entry]
                wave = nodes[entry]
                real = source[first_box + child * stride, 0, t1]
                imag = source[first_box + child * stride, 1, t1]
                old = (before * wave + second_phase) + before_speed * length
                for b in range(2):
                    new = (points[b] * wave + second_phase) + point_speeds[b] * length
                    cosine, sine = turn(new - old)
                    first_row = child * 128 + 8 * t1
                    put(slot, first_row, b, real * cosine + imag * sine, imag * cosine - real * sine)
        blend(slot, target, [first_box, first_box + stride])

    def in_pairs(one):
        def step(half, carry):
            for slot in range(2):
                one(2 * half + slot, slot)
            return carry

        lax.fori_loop(0, 2, step, 0)

    in_pairs(first_level)
    in_pairs(partial(later_level, 1, boxes_a, boxes_b))
    in_pairs(partial(later_level, 2, boxes_b, boxes_a))
    in_pairs(partial(later_level, 3, boxes_a, boxes_b))

    fine_two = [((lane % 32).astype(jnp.float32) * 2.0 + (e + 0.5)) * (1.0 / 64) for e in range(2)]
    fine_phase = [fine_two[e] * wave_two for e in range(2)]

    def reversed_code(box):
        return box % 2 * 4 + box // 2 % 2 * 2 + box // 4

    def fine_speed(code, e):
        return jnp.broadcast_to(speeds[pl.ds(15 + 2 * code + e, 1), :], (8, 128))

    def rotate_box(box, carry):
        code = reversed_code(box)
        point = first_point(3, code.astype(jnp.float32))
        old_speed = speed_row(3, code)
        new_speeds = [fine_speed(code, e) for e in range(2)]
        for t1 in range(16):
            entry = LEVEL_ROWS[4] + t1
            length = lengths[entry]
            across = point * nodes[entry]
            real = boxes_b[box, 0, t1]
            imag = boxes_b[box, 1, t1]
            old = (across + second_phase) + old_speed * length
            for e in range(2):
                new = (across + fine_phase[e]) + new_speeds[e] * length
                cosine, sine = turn(new - old)
                first = pl.multiple_of((e * 256 + box * 32 + t1) * 8, 8)
                turned[pl.ds(first, 8), :] = real * cosine + imag * sine
                turned[pl.ds(first + 128, 8), :] = imag * cosine - real * sine
        return carry

    lax.fori_loop(0, 8, rotate_box, 0)

    for e in range(2):
        for a in range(4):
            last_phase[e, a] = fine_two[e] * last_two[a]

    total = None
    for j in range(4):
        rows = jnp.concatenate(
            [turned[pl.ds(2 * j + k, 512, stride=8), :] for k in range(2)], axis=1
        ).astype(jnp.bfloat16)
        for part in range(2):
            term = jnp.dot(rows, second_table[part, j], preferred_element_type=jnp.float32)
            total = term if total is None else total + term
    mixed[...] = total

    def finish_box(target, out):
        box, e = target // 2, target % 2
        code = reversed_code(box)
        point = first_point(3, code.astype(jnp.float32))
        speed = fine_speed(code, e)
        for high in range(2):
            across = point * last_one[high]
            first = pl.multiple_of(e * 256 + box * 32 + high * 8, 8)
            for a in range(4):
                phase = (across + last_phase[e, a]) + speed * last_lengths[high, a]
                cosine, sine = turn(phase)
                real = mixed[pl.ds(first, 8), 128 * a : 128 * a + 128]
                imag = mixed[pl.ds(first + 16, 8), 128 * a : 128 * a + 128]
                out[high * 4 + a] = real * cosine - imag * sine
                out[8 + high * 4 + a] = real * sine + imag * cosine

    def finish_row(major, carry):
        for minor in range(4):
            finish_box(4 * major + minor, outs.at[4 * major + minor])
        return carry

    lax.fori_loop(0, 4, finish_row, 0)


def levels(chunk, ids, own, other, speeds):
    nodes, waves, lengths = node_tables()
    last_one, last_two, last_lengths = final_tables()
    tables = (waves, lengths, last_one, last_two, last_lengths, first_weights(), second_weights())
    in_vmem = pl.BlockSpec(memory_space=pltpu.VMEM)
    in_smem = pl.BlockSpec(memory_space=pltpu.SMEM)
    return pl.pallas_call(
        partial(levels_kernel, chunk),
        in_specs=[in_smem, in_smem] + [in_vmem] * 10,
        out_specs=in_vmem,
        out_shape=jax.ShapeDtypeStruct((PIECES, 16, 8, 128), jnp.float32),
        scratch_shapes=[
            pltpu.VMEM((8, 2, 16, 8, 128), jnp.float32),
            pltpu.VMEM((8, 2, 16, 8, 128), jnp.float32),
            pltpu.VMEM((2, 256, 512), jnp.float32),
            pltpu.VMEM((4096, 128), jnp.float32),
            pltpu.VMEM((512, 512), jnp.float32),
            pltpu.VMEM((2, 4, 8, 128), jnp.float32),
        ],
        compiler_params=pltpu.CompilerParams(vmem_limit_bytes=VMEM_LIMIT),
        cost_estimate=pl.CostEstimate(flops=10**8, bytes_accessed=2**23, transcendentals=0),
        name="levels",
    )(ids, jnp.asarray(nodes), own, other, speeds, *[jnp.asarray(table) for table in tables])


def unpack_rows(tiles, rows, out_ref, lanes):
    def step(block, carry):
        for a in range(4):
            values = [tiles[j, 4 * block + a] for j in range(4)]
            for b, tile in enumerate(swap_lanes(values)):
                t2 = 4 * b + a
                rows[block, 8 * t2 : 8 * t2 + 8, :] = tile
        for t1 in range(8):
            out_ref[block // 2, block % 2 * 8 + t1, :, lanes] = rows[block, pl.ds(t1, 16, stride=8), :]
        return carry

    lax.fori_loop(0, 4, step, 0)


def unpack_kernel(*refs):
    unpack_rows(refs[0], refs[-1], refs[-2], slice(None))


def unpack(received, chunk, earlier):
    operands = [received]
    in_specs = [pl.BlockSpec((4, 16, 8, 128), lambda i: (i, 0, 0, 0))]
    aliases = {}
    if earlier is not None:
        aliases = {1: 0}
        operands.append(earlier)
        in_specs.append(pl.BlockSpec(memory_space=pl.ANY))
    return pl.pallas_call(
        unpack_kernel,
        grid=(4,),
        in_specs=in_specs,
        out_specs=pl.BlockSpec((2, 16, 16, 128), lambda i: (0, 0, 0, 4 * chunk + i)),
        out_shape=jax.ShapeDtypeStruct((2, 16, 16, 1024), jnp.float32),
        scratch_shapes=[pltpu.VMEM((4, 128, 128), jnp.float32)],
        input_output_aliases=aliases,
        compiler_params=pltpu.CompilerParams(vmem_limit_bytes=VMEM_LIMIT),
        cost_estimate=pl.CostEstimate(flops=10**6, bytes_accessed=2**21, transcendentals=0),
        name="unpack",
    )(*operands)


def speed_tables(speed_modes, core):
    numerators, spans = [], []
    for level_index in range(4):
        for code in range(2**level_index):
            numerators.append(core * 2**level_index + code)
            spans.append(2 ** (level_index + 1))
    for code in range(8):
        for e in range(2):
            numerators.append(core * 8 + code)
            spans.append(16)
    codes = jnp.stack(numerators).astype(jnp.float32)
    spans = jnp.asarray(np.array(spans), jnp.float32)
    me = lax.axis_index("bx") * 2 + lax.axis_index("by")
    rows = (jnp.arange(CHUNKS) * PIECES + me).astype(jnp.float32)
    target_one = (rows[:, None] * spans + codes + 0.5) / (TGT * spans)
    columns = jnp.arange(32).astype(jnp.float32)
    coarse = jnp.broadcast_to((columns + 0.5) / TGT, (15, 32))
    fine = jnp.stack([(2 * columns + e + 0.5) / (2 * TGT) for e in range(2)])
    target_two = jnp.concatenate([coarse, jnp.tile(fine, (8, 1))])
    target_one = jnp.broadcast_to(target_one[:, :, None], (CHUNKS, 31, 32))
    target_two = jnp.broadcast_to(target_two[None], (CHUNKS, 31, 32))
    speed = speed_of(speed_modes, target_one.reshape(-1), target_two.reshape(-1))
    return jnp.tile(speed.reshape(CHUNKS, 31, 32), (1, 1, 4))


def on_device_dealt(weights, speed_modes):
    local = weights.reshape(weights.shape[2:])
    core = lax.axis_index("cores")
    me = lax.axis_index("bx") * 2 + lax.axis_index("by")
    ids = jnp.stack([me, core]).astype(jnp.int32)
    speeds = speed_tables(speed_modes, core)

    received = [deal(pack(local, chunk)) for chunk in range(CHUNKS)]
    results = []
    for chunk in range(CHUNKS):
        own = join(received[chunk])
        other = partner_2(own, "cores", 0)
        results.append(deal(levels(chunk, ids, own, other, speeds[chunk])))
    out = None
    for chunk in range(CHUNKS):
        out = unpack(results[chunk], chunk, out)
    return out.reshape(weights.shape)


def deal(pieces):
    return lax.all_to_all(pieces, ("bx", "by"), 0, 0, tiled=True)


def solution(mesh):
    sizes = dict(mesh.shape)
    spec = P(("bx", "cores"), "by", None, None, None, None)
    dealt = (sizes["bx"], sizes["by"], sizes["cores"]) == (8, 2, 2)

    def whole(weights, speed_modes):
        fits = dealt and weights.shape[2:] == (2, 16, 16, 1024)
        return jax.shard_map(
            on_device_dealt if fits else on_device,
            mesh=mesh,
            in_specs=(spec, P()),
            out_specs=spec,
            check_vma=False,
        )(weights, speed_modes)

    return whole
```

```python
from functools import partial
import math

import jax
import jax.numpy as jnp
import ml_dtypes
import numpy as np
from jax import lax
from jax.experimental import pallas as pl
from jax.experimental.pallas import tpu as pltpu
from jax.sharding import PartitionSpec as P

N = 8192
TGT = 32


def partner_2(value, axis, apart):
    mask = 2**apart
    pairs = [(source, source ^ mask) for source in range(lax.axis_size(axis))]
    return lax.ppermute(value, axis, pairs)


def cheb_nodes(degree):
    return np.cos(np.pi * (2 * np.arange(degree) + 1) / (2 * degree))


def lagrange_table(degree):
    points = cheb_nodes(degree)
    result = np.ones((degree, 2 * degree))
    for child_side in range(2):
        inside = (points + 2 * child_side - 1) / 2
        for node_row in range(degree):
            for node_other in range(degree):
                if node_other != node_row:
                    result[node_row, child_side * degree : (child_side + 1) * degree] *= (
                        inside - points[node_other]
                    ) / (points[node_row] - points[node_other])
    return result


def speed_of(speed_modes, target_one, target_two):
    mode_count = speed_modes.shape[0]
    frequencies = jnp.arange(mode_count).astype(jnp.float32) * math.pi
    along_one = jnp.cos(frequencies[:, None] * target_one[None, :])
    along_two = jnp.cos(frequencies[:, None] * target_two[None, :])
    blended = jnp.dot(
        speed_modes, along_two, preferred_element_type=jnp.float32, precision=lax.Precision.HIGHEST
    )
    return 1.0 + jnp.sum(blended * along_one, axis=0)


def rotation(target_one, target_two, speed_value, wave_one, wave_two):
    phase = (
        target_one * wave_one
        + target_two * wave_two
        + speed_value * jnp.sqrt(wave_one * wave_one + wave_two * wave_two)
    )
    phase = phase - jnp.floor(phase)
    angle = 2.0 * math.pi * phase
    return (jnp.cos(angle), jnp.sin(angle))


def node_phase(layout, speed_value, center, half_width, degree):
    target_one, target_two, merge_dim, centers, child_half, other_center, other_half = layout
    points = jnp.asarray(cheb_nodes(degree), jnp.float32)
    merged = center[None, :] + half_width * points[:, None]
    across = other_center[None, :] + other_half * points[:, None]
    if merge_dim == 0:
        return rotation(target_one, target_two, speed_value, merged[:, None, :], across[None, :, :])
    return rotation(target_one, target_two, speed_value, across[:, None, :], merged[None, :, :])


def merge_children(child_low, child_high, layout, speed_modes):
    target_one, target_two, merge_dim, centers, child_half, other_center, other_half = layout
    degree = child_low.shape[1]
    speed_value = speed_of(speed_modes, target_one, target_two)
    lagrange = jnp.asarray(lagrange_table(degree), jnp.float32)
    pieces = []
    for child, center in ((child_low, centers[0]), (child_high, centers[1])):
        cosine, sine_part = node_phase(layout, speed_value, center, child_half, degree)
        real_part = child[0] * cosine + child[1] * sine_part
        imag_part = child[1] * cosine - child[0] * sine_part
        pieces.append(jnp.stack([real_part, imag_part]))
    stacked = jnp.concatenate(pieces, axis=1 + merge_dim)
    if merge_dim == 0:
        blended = jnp.einsum("ij,rjks->riks", lagrange, stacked, precision=lax.Precision.HIGHEST)
    else:
        blended = jnp.einsum("kj,rijs->riks", lagrange, stacked, precision=lax.Precision.HIGHEST)
    cosine, sine_part = node_phase(layout, speed_value, centers[2], 2.0 * child_half, degree)
    return jnp.stack(
        [blended[0] * cosine - blended[1] * sine_part, blended[0] * sine_part + blended[1] * cosine]
    )


def reversed_bits(box_code, bit_count):
    result = jnp.zeros_like(box_code)
    for bit_place in range(bit_count):
        result = result + box_code // 2**bit_place % 2 * 2 ** (bit_count - 1 - bit_place)
    return result


def x_layout(level_index, box_code, targets, y_box, geometry):
    extent, side_count, src_x, src_y = geometry
    span_size = 2 ** (level_index + 1)
    row_index = targets // side_count * span_size + reversed_bits(box_code, level_index + 1)
    target_one = (row_index.astype(jnp.float32) + 0.5) / (side_count * span_size)
    target_two = ((targets % side_count).astype(jnp.float32) + 0.5) / side_count
    parent = (box_code // span_size).astype(jnp.float32)
    child_width = extent * 2**level_index / src_x
    low_center = -extent / 2 + (2.0 * parent + 0.5) * child_width
    high_center = low_center + child_width
    parent_center = -extent / 2 + (parent + 0.5) * (2.0 * child_width)
    other_center = jnp.zeros_like(target_one) + (
        -extent / 2 + (jnp.asarray(y_box).astype(jnp.float32) + 0.5) * (extent / src_y)
    )
    return (
        target_one,
        target_two,
        0,
        (low_center, high_center, parent_center),
        child_width / 2,
        other_center,
        extent / (2 * src_y),
    )


def y_layout(level_index, box_code, targets, x_code, x_bits, geometry):
    extent, side_count, src_x, src_y = geometry
    span_size = 2 ** (level_index + 1)
    col_index = targets % side_count * span_size + reversed_bits(box_code, level_index + 1)
    target_two = (col_index.astype(jnp.float32) + 0.5) / (side_count * span_size)
    row_index = targets // side_count * src_x + reversed_bits(x_code, x_bits)
    target_one = (row_index.astype(jnp.float32) + 0.5) / (side_count * src_x)
    parent = (box_code // span_size).astype(jnp.float32)
    child_width = extent * 2**level_index / src_y
    low_center = -extent / 2 + (2.0 * parent + 0.5) * child_width
    high_center = low_center + child_width
    parent_center = -extent / 2 + (parent + 0.5) * (2.0 * child_width)
    other_center = jnp.zeros_like(target_one)
    return (
        target_one,
        target_two,
        1,
        (low_center, high_center, parent_center),
        child_width / 2,
        other_center,
        extent / 2,
    )


def pair_level(current, partner, level_index, box_code, targets, layout_fn, speed_modes):
    own_bit = box_code // 2**level_index % 2
    child_low = jnp.where(own_bit == 0, current, partner)
    child_high = jnp.where(own_bit == 0, partner, current)
    box_codes = jnp.zeros_like(targets) + box_code
    return merge_children(
        child_low, child_high, layout_fn(level_index, box_codes, targets), speed_modes
    )


def on_device(weights, speed_modes):
    current = weights.reshape(weights.shape[2:])
    pair_count = current.shape[3]
    core_count = lax.axis_size("cores")
    src_x = lax.axis_size("bx") * core_count
    src_y = lax.axis_size("by")
    x_bits = src_x.bit_length() - 1
    y_bits = src_y.bit_length() - 1
    x_code = lax.axis_index("bx") * core_count + lax.axis_index("cores")
    y_box = lax.axis_index("by")
    geometry = (float(N), TGT, src_x, src_y)
    targets = jnp.arange(pair_count, dtype=jnp.int32)
    first_layout = partial(x_layout, y_box=y_box, geometry=geometry)
    second_layout = partial(y_layout, x_code=x_code, x_bits=x_bits, geometry=geometry)
    for level_index in range(x_bits):
        if level_index == 0:
            partner = partner_2(current, "cores", 0)
        else:
            partner = partner_2(current, "bx", level_index - 1)
        current = pair_level(
            current, partner, level_index, x_code, targets, first_layout, speed_modes
        )
    for level_index in range(y_bits):
        partner = partner_2(current, "by", level_index)
        current = pair_level(
            current, partner, level_index, y_box, targets, second_layout, speed_modes
        )
    return current.reshape(weights.shape)


SIN_HALF = (4.442879586386342, -7.3078180422392816, 3.597788667381583, -0.7912380409231197)
COS_HALF = (
    1.4142134965636117,
    -6.978850988059019,
    5.739461167077472,
    -1.883562964211867,
    0.3106981455985473,
)
CHUNKS = 2
PIECES = 16
LEVEL_ROWS = (0, 256, 384, 448, 480)
VMEM_LIMIT = 48 * 2**20


def node_tables():
    points = cheb_nodes(16).astype(np.float32)
    nodes = []
    for level_index in range(5):
        width = np.float32(N * 2**level_index / 16)
        for box in range(16 >> level_index):
            center = np.float32(-N / 2 + (box + 0.5) * width)
            nodes.append(center + (width / 2) * points)
    nodes = np.concatenate(nodes).astype(np.float32)
    sub = np.arange(8)
    lane = np.arange(128)
    half = (sub // 4)[:, None] + 0 * lane[None, :]
    second = (lane // 32 * 4)[None, :] + (sub % 4)[:, None]
    wave_two = (-N / 2 + (half + 0.5) * (N / 2)).astype(np.float32) + np.float32(N / 4) * points[second]
    wave_two = wave_two.astype(np.float32)
    lengths = np.sqrt(nodes[:, None, None] * nodes[:, None, None] + wave_two * wave_two)
    return nodes, wave_two, lengths.astype(np.float32)


def final_tables():
    points = cheb_nodes(16).astype(np.float32) * np.float32(N / 2)
    lane = np.arange(128)
    one = np.broadcast_to(points.reshape(2, 8, 1), (2, 8, 128)).astype(np.float32)
    two = np.stack([np.broadcast_to(points[lane // 32 * 4 + a], (8, 128)) for a in range(4)])
    two = two.astype(np.float32)
    lengths = np.sqrt((one * one)[:, None] + (two * two)[None, :]).astype(np.float32)
    return np.array(one), two, lengths


def in_two_parts(table):
    high = table.astype(ml_dtypes.bfloat16)
    low = (table - high.astype(np.float32)).astype(ml_dtypes.bfloat16)
    return high, low


def first_weights():
    table = lagrange_table(16).astype(np.float32)
    high, low = in_two_parts(np.kron(table, np.eye(8, dtype=np.float32)))
    return np.concatenate([high, low])


def second_weights():
    table = lagrange_table(16)
    result = np.zeros((8, 4, 32, 4, 4, 32), np.float32)
    same = np.eye(32, dtype=np.float32)
    for half in range(2):
        for a in range(4):
            for b in range(4):
                for out_a in range(4):
                    for out_b in range(4):
                        weight = table[4 * out_b + out_a, half * 16 + 4 * b + a]
                        result[half * 4 + a, b, :, out_a, out_b, :] = np.float32(weight) * same
    return np.stack(in_two_parts(result.reshape(4, 256, 512)))


def turn(phase):
    part = phase - jnp.round(phase)
    square = part * part
    sine = SIN_HALF[3]
    for coefficient in SIN_HALF[2::-1]:
        sine = sine * square + coefficient
    sine = sine * part
    cosine = COS_HALF[4]
    for coefficient in COS_HALF[3::-1]:
        cosine = cosine * square + coefficient
    return 1.0 - sine * sine, sine * cosine


def swap_lanes(values):
    lane = lax.broadcasted_iota(jnp.int32, (8, 128), 1)
    low = lane < 64
    even = lane // 32 % 2 == 0
    half = [None] * 4
    for b in range(2):
        half[b] = jnp.where(low, values[b], pltpu.roll(values[b + 2], 64, 1))
        half[b + 2] = jnp.where(low, pltpu.roll(values[b], 64, 1), values[b + 2])
    full = [None] * 4
    for j in (0, 2):
        full[j] = jnp.where(even, half[j], pltpu.roll(half[j + 1], 32, 1))
        full[j + 1] = jnp.where(even, pltpu.roll(half[j], 96, 1), half[j + 1])
    return full


def pack_rows(in_ref, lanes, tiles):
    upper = lax.broadcasted_iota(jnp.int32, (8, 128), 0) < 4
    for t1 in range(16):
        groups = [None] * 4
        for high in range(2):
            real = in_ref[0, t1, 8 * high : 8 * high + 8, lanes]
            imag = in_ref[1, t1, 8 * high : 8 * high + 8, lanes]
            groups[2 * high] = jnp.where(upper, real, pltpu.roll(imag, 4, 0))
            groups[2 * high + 1] = jnp.where(upper, pltpu.roll(real, 4, 0), imag)
        for j, tile in enumerate(swap_lanes(groups)):
            tiles[j, t1] = tile


def pack_kernel(chunk, in_ref, out_ref, held, arrived):
    group = pl.program_id(0)

    def fetch(place):
        lanes = pl.ds((4 * chunk + place) * 128, 128)
        return pltpu.make_async_copy(
            in_ref.at[:, :, :, lanes], held.at[place], arrived.at[place]
        )

    @pl.when(group == 0)
    def _():
        for place in range(4):
            fetch(place).start()

    for place in range(4):

        @pl.when(group == place)
        def _(place=place):
            fetch(place).wait()

    pack_rows(held.at[group], slice(None), out_ref)


def pack(weights, chunk):
    return pl.pallas_call(
        partial(pack_kernel, chunk),
        grid=(4,),
        in_specs=[pl.BlockSpec(memory_space=pl.ANY)],
        out_specs=pl.BlockSpec((4, 16, 8, 128), lambda i: (i, 0, 0, 0)),
        out_shape=jax.ShapeDtypeStruct((PIECES, 16, 8, 128), jnp.float32),
        scratch_shapes=[pltpu.VMEM((4, 2, 16, 16, 128), jnp.float32), pltpu.SemaphoreType.DMA((4,))],
        cost_estimate=pl.CostEstimate(flops=10**6, bytes_accessed=2**21, transcendentals=0),
        name="pack",
    )(weights)


def merge_halves(out_ref, box, t1, low, high):
    upper = lax.broadcasted_iota(jnp.int32, (8, 128), 0) < 4
    out_ref[box, 0, t1] = jnp.where(upper, low, pltpu.roll(high, 4, 0))
    out_ref[box, 1, t1] = jnp.where(upper, pltpu.roll(low, 4, 0), high)


def join_kernel(in_ref, *refs):
    out_ref = refs[-1]

    def step(box, carry):
        for t1 in range(16):
            merge_halves(out_ref, box, t1, in_ref[2 * box, t1], in_ref[2 * box + 1, t1])
        return carry

    lax.fori_loop(0, 8, step, 0)


def join(received):
    in_vmem = pl.BlockSpec(memory_space=pltpu.VMEM)
    return pl.pallas_call(
        join_kernel,
        in_specs=[in_vmem],
        out_specs=in_vmem,
        out_shape=jax.ShapeDtypeStruct((8, 2, 16, 8, 128), jnp.float32),
        compiler_params=pltpu.CompilerParams(vmem_limit_bytes=VMEM_LIMIT),
        cost_estimate=pl.CostEstimate(flops=10**6, bytes_accessed=2**21, transcendentals=0),
        name="join",
    )(received)


def levels_kernel(
    chunk, ids, nodes, own, other, speeds, waves, lengths, last_one, last_two,
    last_lengths, first_table, second_table, *refs,
):
    outs = refs[0]
    boxes_a, boxes_b, sums, turned, mixed, last_phase = refs[-6:]
    row = (chunk * PIECES + ids[0]).astype(jnp.float32)
    core = ids[1]
    core_float = core.astype(jnp.float32)
    wave_two = waves[...]
    lane = lax.broadcasted_iota(jnp.int32, (8, 128), 1)
    along_two = ((lane % 32).astype(jnp.float32) + 0.5) * (1.0 / 32)
    second_phase = along_two * wave_two

    def first_point(level_index, low_code):
        span = 2.0 ** (level_index + 1)
        code = core_float * 2.0**level_index + low_code
        return (row * span + code + 0.5) * (1.0 / (32 * span))

    def speed_row(level_index, low_code):
        return jnp.broadcast_to(speeds[pl.ds(2**level_index - 1 + low_code, 1), :], (8, 128))

    def blend(slot, target, boxes):
        rows = sums[slot].astype(jnp.bfloat16)
        both = jnp.dot(first_table[...], rows, preferred_element_type=jnp.float32)
        total = both[:128] + both[128:]
        for n, box in enumerate(boxes):
            for part in range(2):
                column = 128 * (2 * n + part)
                target[box, part] = total[:, column : column + 128].reshape(16, 8, 128)

    def put(slot, first_row, column, real, imag):
        sums[slot, pl.ds(first_row, 8), 256 * column : 256 * column + 128] = real
        sums[slot, pl.ds(first_row, 8), 256 * column + 128 : 256 * column + 256] = imag

    def first_level(pair, slot):
        point = first_point(0, 0.0)
        speed = speed_row(0, 0)
        for n in range(2):
            box = 2 * pair + n
            for source, child in ((own, core), (other, 1 - core)):
                for t1 in range(16):
                    entry = (2 * box + child) * 16 + t1
                    phase = (point * nodes[entry] + second_phase) + speed * lengths[entry]
                    cosine, sine = turn(phase)
                    real = source[box, 0, t1]
                    imag = source[box, 1, t1]
                    first_row = pl.multiple_of(child * 128 + 8 * t1, 8)
                    put(slot, first_row, n, real * cosine + imag * sine, imag * cosine - real * sine)
        blend(slot, boxes_a, [2 * pair, 2 * pair + 1])

    def later_level(level_index, source, target, index, slot):
        low_bits = level_index - 1
        stride = 2**low_bits
        parent = index // stride
        low = index % stride
        code = jnp.int32(0)
        for bit in range(low_bits):
            code = code + low // 2**bit % 2 * 2 ** (low_bits - 1 - bit)
        before = first_point(level_index - 1, code.astype(jnp.float32))
        before_speed = speed_row(level_index - 1, code)
        points = [first_point(level_index, (2 * code + b).astype(jnp.float32)) for b in range(2)]
        point_speeds = [speed_row(level_index, 2 * code + b) for b in range(2)]
        first_box = parent * (2 * stride) + low
        for child in range(2):
            for t1 in range(16):
                entry = LEVEL_ROWS[level_index] + (2 * parent + child) * 16 + t1
                length = lengths[entry]
                wave = nodes[entry]
                real = source[first_box + child * stride, 0, t1]
                imag = source[first_box + child * stride, 1, t1]
                old = (before * wave + second_phase) + before_speed * length
                for b in range(2):
                    new = (points[b] * wave + second_phase) + point_speeds[b] * length
                    cosine, sine = turn(new - old)
                    first_row = child * 128 + 8 * t1
                    put(slot, first_row, b, real * cosine + imag * sine, imag * cosine - real * sine)
        blend(slot, target, [first_box, first_box + stride])

    def in_pairs(one):
        def step(half, carry):
            for slot in range(2):
                one(2 * half + slot, slot)
            return carry

        lax.fori_loop(0, 2, step, 0)

    in_pairs(first_level)
    in_pairs(partial(later_level, 1, boxes_a, boxes_b))
    in_pairs(partial(later_level, 2, boxes_b, boxes_a))
    in_pairs(partial(later_level, 3, boxes_a, boxes_b))

    fine_two = [((lane % 32).astype(jnp.float32) * 2.0 + (e + 0.5)) * (1.0 / 64) for e in range(2)]
    fine_phase = [fine_two[e] * wave_two for e in range(2)]

    def reversed_code(box):
        return box % 2 * 4 + box // 2 % 2 * 2 + box // 4

    def fine_speed(code, e):
        return jnp.broadcast_to(speeds[pl.ds(15 + 2 * code + e, 1), :], (8, 128))

    def rotate_box(box, carry):
        code = reversed_code(box)
        point = first_point(3, code.astype(jnp.float32))
        old_speed = speed_row(3, code)
        new_speeds = [fine_speed(code, e) for e in range(2)]
        for t1 in range(16):
            entry = LEVEL_ROWS[4] + t1
            length = lengths[entry]
            across = point * nodes[entry]
            real = boxes_b[box, 0, t1]
            imag = boxes_b[box, 1, t1]
            old = (across + second_phase) + old_speed * length
            for e in range(2):
                new = (across + fine_phase[e]) + new_speeds[e] * length
                cosine, sine = turn(new - old)
                first = pl.multiple_of((e * 256 + box * 32 + t1) * 8, 8)
                turned[pl.ds(first, 8), :] = real * cosine + imag * sine
                turned[pl.ds(first + 128, 8), :] = imag * cosine - real * sine
        return carry

    lax.fori_loop(0, 8, rotate_box, 0)

    for e in range(2):
        for a in range(4):
            last_phase[e, a] = fine_two[e] * last_two[a]

    total = None
    for j in range(4):
        rows = jnp.concatenate(
            [turned[pl.ds(2 * j + k, 512, stride=8), :] for k in range(2)], axis=1
        ).astype(jnp.bfloat16)
        for part in range(2):
            term = jnp.dot(rows, second_table[part, j], preferred_element_type=jnp.float32)
            total = term if total is None else total + term
    mixed[...] = total

    def finish_box(target, out):
        box, e = target // 2, target % 2
        code = reversed_code(box)
        point = first_point(3, code.astype(jnp.float32))
        speed = fine_speed(code, e)
        for high in range(2):
            across = point * last_one[high]
            first = pl.multiple_of(e * 256 + box * 32 + high * 8, 8)
            for a in range(4):
                phase = (across + last_phase[e, a]) + speed * last_lengths[high, a]
                cosine, sine = turn(phase)
                real = mixed[pl.ds(first, 8), 128 * a : 128 * a + 128]
                imag = mixed[pl.ds(first + 16, 8), 128 * a : 128 * a + 128]
                out[high * 4 + a] = real * cosine - imag * sine
                out[8 + high * 4 + a] = real * sine + imag * cosine

    def finish_row(major, carry):
        for minor in range(4):
            finish_box(4 * major + minor, outs.at[4 * major + minor])
        return carry

    lax.fori_loop(0, 4, finish_row, 0)


def levels(chunk, ids, own, other, speeds):
    nodes, waves, lengths = node_tables()
    last_one, last_two, last_lengths = final_tables()
    tables = (waves, lengths, last_one, last_two, last_lengths, first_weights(), second_weights())
    in_vmem = pl.BlockSpec(memory_space=pltpu.VMEM)
    in_smem = pl.BlockSpec(memory_space=pltpu.SMEM)
    return pl.pallas_call(
        partial(levels_kernel, chunk),
        in_specs=[in_smem, in_smem] + [in_vmem] * 10,
        out_specs=in_vmem,
        out_shape=jax.ShapeDtypeStruct((PIECES, 16, 8, 128), jnp.float32),
        scratch_shapes=[
            pltpu.VMEM((8, 2, 16, 8, 128), jnp.float32),
            pltpu.VMEM((8, 2, 16, 8, 128), jnp.float32),
            pltpu.VMEM((2, 256, 512), jnp.float32),
            pltpu.VMEM((4096, 128), jnp.float32),
            pltpu.VMEM((512, 512), jnp.float32),
            pltpu.VMEM((2, 4, 8, 128), jnp.float32),
        ],
        compiler_params=pltpu.CompilerParams(vmem_limit_bytes=VMEM_LIMIT),
        cost_estimate=pl.CostEstimate(flops=10**8, bytes_accessed=2**23, transcendentals=0),
        name="levels",
    )(ids, jnp.asarray(nodes), own, other, speeds, *[jnp.asarray(table) for table in tables])


def unpack_rows(tiles, rows, out_ref, lanes):
    for part in range(2):
        for high in range(2):
            block = part * 2 + high
            for a in range(4):
                values = [tiles[j, part * 8 + high * 4 + a] for j in range(4)]
                for b, tile in enumerate(swap_lanes(values)):
                    t2 = 4 * b + a
                    rows[block, 8 * t2 : 8 * t2 + 8, :] = tile
            for t1 in range(8):
                out_ref[part, high * 8 + t1, :, lanes] = rows[block, pl.ds(t1, 16, stride=8), :]


def unpack_kernel(*refs):
    unpack_rows(refs[0], refs[-1], refs[-2], slice(None))


def unpack(received, chunk, earlier):
    operands = [received]
    in_specs = [pl.BlockSpec((4, 16, 8, 128), lambda i: (i, 0, 0, 0))]
    aliases = {}
    if earlier is not None:
        aliases = {1: 0}
        operands.append(earlier)
        in_specs.append(pl.BlockSpec(memory_space=pl.ANY))
    return pl.pallas_call(
        unpack_kernel,
        grid=(4,),
        in_specs=in_specs,
        out_specs=pl.BlockSpec((2, 16, 16, 128), lambda i: (0, 0, 0, 4 * chunk + i)),
        out_shape=jax.ShapeDtypeStruct((2, 16, 16, 1024), jnp.float32),
        scratch_shapes=[pltpu.VMEM((4, 128, 128), jnp.float32)],
        input_output_aliases=aliases,
        compiler_params=pltpu.CompilerParams(vmem_limit_bytes=VMEM_LIMIT),
        cost_estimate=pl.CostEstimate(flops=10**6, bytes_accessed=2**21, transcendentals=0),
        name="unpack",
    )(*operands)


def speed_tables(speed_modes, core):
    numerators, spans = [], []
    for level_index in range(4):
        for code in range(2**level_index):
            numerators.append(core * 2**level_index + code)
            spans.append(2 ** (level_index + 1))
    for code in range(8):
        for e in range(2):
            numerators.append(core * 8 + code)
            spans.append(16)
    codes = jnp.stack(numerators).astype(jnp.float32)
    spans = jnp.asarray(np.array(spans), jnp.float32)
    me = lax.axis_index("bx") * 2 + lax.axis_index("by")
    rows = (jnp.arange(CHUNKS) * PIECES + me).astype(jnp.float32)
    target_one = (rows[:, None] * spans + codes + 0.5) / (TGT * spans)
    columns = jnp.arange(32).astype(jnp.float32)
    coarse = jnp.broadcast_to((columns + 0.5) / TGT, (15, 32))
    fine = jnp.stack([(2 * columns + e + 0.5) / (2 * TGT) for e in range(2)])
    target_two = jnp.concatenate([coarse, jnp.tile(fine, (8, 1))])
    target_one = jnp.broadcast_to(target_one[:, :, None], (CHUNKS, 31, 32))
    target_two = jnp.broadcast_to(target_two[None], (CHUNKS, 31, 32))
    speed = speed_of(speed_modes, target_one.reshape(-1), target_two.reshape(-1))
    return jnp.tile(speed.reshape(CHUNKS, 31, 32), (1, 1, 4))


def on_device_dealt(weights, speed_modes):
    local = weights.reshape(weights.shape[2:])
    core = lax.axis_index("cores")
    me = lax.axis_index("bx") * 2 + lax.axis_index("by")
    ids = jnp.stack([me, core]).astype(jnp.int32)
    speeds = speed_tables(speed_modes, core)

    received = [deal(pack(local, chunk)) for chunk in range(CHUNKS)]
    results = []
    for chunk in range(CHUNKS):
        own = join(received[chunk])
        other = partner_2(own, "cores", 0)
        results.append(deal(levels(chunk, ids, own, other, speeds[chunk])))
    out = None
    for chunk in range(CHUNKS):
        out = unpack(results[chunk], chunk, out)
    return out.reshape(weights.shape)


def deal(pieces):
    return lax.all_to_all(pieces, ("bx", "by"), 0, 0, tiled=True)


def solution(mesh):
    sizes = dict(mesh.shape)
    spec = P(("bx", "cores"), "by", None, None, None, None)
    dealt = (sizes["bx"], sizes["by"], sizes["cores"]) == (8, 2, 2)

    def whole(weights, speed_modes):
        fits = dealt and weights.shape[2:] == (2, 16, 16, 1024)
        return jax.shard_map(
            on_device_dealt if fits else on_device,
            mesh=mesh,
            in_specs=(spec, P()),
            out_specs=spec,
            check_vma=False,
        )(weights, speed_modes)

    return whole
```

```python
from functools import partial
import math

import jax
import jax.numpy as jnp
import ml_dtypes
import numpy as np
from jax import lax
from jax.experimental import pallas as pl
from jax.experimental.pallas import tpu as pltpu
from jax.sharding import PartitionSpec as P

N = 8192
TGT = 32


def partner_2(value, axis, apart):
    mask = 2**apart
    pairs = [(source, source ^ mask) for source in range(lax.axis_size(axis))]
    return lax.ppermute(value, axis, pairs)


def cheb_nodes(degree):
    return np.cos(np.pi * (2 * np.arange(degree) + 1) / (2 * degree))


def lagrange_table(degree):
    points = cheb_nodes(degree)
    result = np.ones((degree, 2 * degree))
    for child_side in range(2):
        inside = (points + 2 * child_side - 1) / 2
        for node_row in range(degree):
            for node_other in range(degree):
                if node_other != node_row:
                    result[node_row, child_side * degree : (child_side + 1) * degree] *= (
                        inside - points[node_other]
                    ) / (points[node_row] - points[node_other])
    return result


def speed_of(speed_modes, target_one, target_two):
    mode_count = speed_modes.shape[0]
    frequencies = jnp.arange(mode_count).astype(jnp.float32) * math.pi
    along_one = jnp.cos(frequencies[:, None] * target_one[None, :])
    along_two = jnp.cos(frequencies[:, None] * target_two[None, :])
    blended = jnp.dot(
        speed_modes, along_two, preferred_element_type=jnp.float32, precision=lax.Precision.HIGHEST
    )
    return 1.0 + jnp.sum(blended * along_one, axis=0)


def rotation(target_one, target_two, speed_value, wave_one, wave_two):
    phase = (
        target_one * wave_one
        + target_two * wave_two
        + speed_value * jnp.sqrt(wave_one * wave_one + wave_two * wave_two)
    )
    phase = phase - jnp.floor(phase)
    angle = 2.0 * math.pi * phase
    return (jnp.cos(angle), jnp.sin(angle))


def node_phase(layout, speed_value, center, half_width, degree):
    target_one, target_two, merge_dim, centers, child_half, other_center, other_half = layout
    points = jnp.asarray(cheb_nodes(degree), jnp.float32)
    merged = center[None, :] + half_width * points[:, None]
    across = other_center[None, :] + other_half * points[:, None]
    if merge_dim == 0:
        return rotation(target_one, target_two, speed_value, merged[:, None, :], across[None, :, :])
    return rotation(target_one, target_two, speed_value, across[:, None, :], merged[None, :, :])


def merge_children(child_low, child_high, layout, speed_modes):
    target_one, target_two, merge_dim, centers, child_half, other_center, other_half = layout
    degree = child_low.shape[1]
    speed_value = speed_of(speed_modes, target_one, target_two)
    lagrange = jnp.asarray(lagrange_table(degree), jnp.float32)
    pieces = []
    for child, center in ((child_low, centers[0]), (child_high, centers[1])):
        cosine, sine_part = node_phase(layout, speed_value, center, child_half, degree)
        real_part = child[0] * cosine + child[1] * sine_part
        imag_part = child[1] * cosine - child[0] * sine_part
        pieces.append(jnp.stack([real_part, imag_part]))
    stacked = jnp.concatenate(pieces, axis=1 + merge_dim)
    if merge_dim == 0:
        blended = jnp.einsum("ij,rjks->riks", lagrange, stacked, precision=lax.Precision.HIGHEST)
    else:
        blended = jnp.einsum("kj,rijs->riks", lagrange, stacked, precision=lax.Precision.HIGHEST)
    cosine, sine_part = node_phase(layout, speed_value, centers[2], 2.0 * child_half, degree)
    return jnp.stack(
        [blended[0] * cosine - blended[1] * sine_part, blended[0] * sine_part + blended[1] * cosine]
    )


def reversed_bits(box_code, bit_count):
    result = jnp.zeros_like(box_code)
    for bit_place in range(bit_count):
        result = result + box_code // 2**bit_place % 2 * 2 ** (bit_count - 1 - bit_place)
    return result


def x_layout(level_index, box_code, targets, y_box, geometry):
    extent, side_count, src_x, src_y = geometry
    span_size = 2 ** (level_index + 1)
    row_index = targets // side_count * span_size + reversed_bits(box_code, level_index + 1)
    target_one = (row_index.astype(jnp.float32) + 0.5) / (side_count * span_size)
    target_two = ((targets % side_count).astype(jnp.float32) + 0.5) / side_count
    parent = (box_code // span_size).astype(jnp.float32)
    child_width = extent * 2**level_index / src_x
    low_center = -extent / 2 + (2.0 * parent + 0.5) * child_width
    high_center = low_center + child_width
    parent_center = -extent / 2 + (parent + 0.5) * (2.0 * child_width)
    other_center = jnp.zeros_like(target_one) + (
        -extent / 2 + (jnp.asarray(y_box).astype(jnp.float32) + 0.5) * (extent / src_y)
    )
    return (
        target_one,
        target_two,
        0,
        (low_center, high_center, parent_center),
        child_width / 2,
        other_center,
        extent / (2 * src_y),
    )


def y_layout(level_index, box_code, targets, x_code, x_bits, geometry):
    extent, side_count, src_x, src_y = geometry
    span_size = 2 ** (level_index + 1)
    col_index = targets % side_count * span_size + reversed_bits(box_code, level_index + 1)
    target_two = (col_index.astype(jnp.float32) + 0.5) / (side_count * span_size)
    row_index = targets // side_count * src_x + reversed_bits(x_code, x_bits)
    target_one = (row_index.astype(jnp.float32) + 0.5) / (side_count * src_x)
    parent = (box_code // span_size).astype(jnp.float32)
    child_width = extent * 2**level_index / src_y
    low_center = -extent / 2 + (2.0 * parent + 0.5) * child_width
    high_center = low_center + child_width
    parent_center = -extent / 2 + (parent + 0.5) * (2.0 * child_width)
    other_center = jnp.zeros_like(target_one)
    return (
        target_one,
        target_two,
        1,
        (low_center, high_center, parent_center),
        child_width / 2,
        other_center,
        extent / 2,
    )


def pair_level(current, partner, level_index, box_code, targets, layout_fn, speed_modes):
    own_bit = box_code // 2**level_index % 2
    child_low = jnp.where(own_bit == 0, current, partner)
    child_high = jnp.where(own_bit == 0, partner, current)
    box_codes = jnp.zeros_like(targets) + box_code
    return merge_children(
        child_low, child_high, layout_fn(level_index, box_codes, targets), speed_modes
    )


def on_device(weights, speed_modes):
    current = weights.reshape(weights.shape[2:])
    pair_count = current.shape[3]
    core_count = lax.axis_size("cores")
    src_x = lax.axis_size("bx") * core_count
    src_y = lax.axis_size("by")
    x_bits = src_x.bit_length() - 1
    y_bits = src_y.bit_length() - 1
    x_code = lax.axis_index("bx") * core_count + lax.axis_index("cores")
    y_box = lax.axis_index("by")
    geometry = (float(N), TGT, src_x, src_y)
    targets = jnp.arange(pair_count, dtype=jnp.int32)
    first_layout = partial(x_layout, y_box=y_box, geometry=geometry)
    second_layout = partial(y_layout, x_code=x_code, x_bits=x_bits, geometry=geometry)
    for level_index in range(x_bits):
        if level_index == 0:
            partner = partner_2(current, "cores", 0)
        else:
            partner = partner_2(current, "bx", level_index - 1)
        current = pair_level(
            current, partner, level_index, x_code, targets, first_layout, speed_modes
        )
    for level_index in range(y_bits):
        partner = partner_2(current, "by", level_index)
        current = pair_level(
            current, partner, level_index, y_box, targets, second_layout, speed_modes
        )
    return current.reshape(weights.shape)


SIN_HALF = (4.442879586386342, -7.3078180422392816, 3.597788667381583, -0.7912380409231197)
COS_HALF = (
    1.4142134965636117,
    -6.978850988059019,
    5.739461167077472,
    -1.883562964211867,
    0.3106981455985473,
)
CHUNKS = 2
PIECES = 16
LEVEL_ROWS = (0, 256, 384, 448, 480)
VMEM_LIMIT = 48 * 2**20


def node_tables():
    points = cheb_nodes(16).astype(np.float32)
    nodes = []
    for level_index in range(5):
        width = np.float32(N * 2**level_index / 16)
        for box in range(16 >> level_index):
            center = np.float32(-N / 2 + (box + 0.5) * width)
            nodes.append(center + (width / 2) * points)
    nodes = np.concatenate(nodes).astype(np.float32)
    sub = np.arange(8)
    lane = np.arange(128)
    half = (sub // 4)[:, None] + 0 * lane[None, :]
    second = (lane // 32 * 4)[None, :] + (sub % 4)[:, None]
    wave_two = (-N / 2 + (half + 0.5) * (N / 2)).astype(np.float32) + np.float32(N / 4) * points[second]
    wave_two = wave_two.astype(np.float32)
    lengths = np.sqrt(nodes[:, None, None] * nodes[:, None, None] + wave_two * wave_two)
    return nodes, wave_two, lengths.astype(np.float32)


def final_tables():
    points = cheb_nodes(16).astype(np.float32) * np.float32(N / 2)
    lane = np.arange(128)
    one = np.broadcast_to(points.reshape(2, 8, 1), (2, 8, 128)).astype(np.float32)
    two = np.stack([np.broadcast_to(points[lane // 32 * 4 + a], (8, 128)) for a in range(4)])
    two = two.astype(np.float32)
    lengths = np.sqrt((one * one)[:, None] + (two * two)[None, :]).astype(np.float32)
    return np.array(one), two, lengths


def in_two_parts(table):
    high = table.astype(ml_dtypes.bfloat16)
    low = (table - high.astype(np.float32)).astype(ml_dtypes.bfloat16)
    return high, low


def first_weights():
    table = lagrange_table(16).astype(np.float32)
    high, low = in_two_parts(np.kron(table, np.eye(8, dtype=np.float32)))
    return np.concatenate([high, low])


def second_weights():
    table = lagrange_table(16)
    result = np.zeros((8, 4, 32, 4, 4, 32), np.float32)
    same = np.eye(32, dtype=np.float32)
    for half in range(2):
        for a in range(4):
            for b in range(4):
                for out_a in range(4):
                    for out_b in range(4):
                        weight = table[4 * out_b + out_a, half * 16 + 4 * b + a]
                        result[half * 4 + a, b, :, out_a, out_b, :] = np.float32(weight) * same
    return np.stack(in_two_parts(result.reshape(4, 256, 512)))


def turn(phase):
    part = phase - jnp.round(phase)
    square = part * part
    sine = SIN_HALF[3]
    for coefficient in SIN_HALF[2::-1]:
        sine = sine * square + coefficient
    sine = sine * part
    cosine = COS_HALF[4]
    for coefficient in COS_HALF[3::-1]:
        cosine = cosine * square + coefficient
    return 1.0 - sine * sine, sine * cosine


def swap_lanes(values):
    lane = lax.broadcasted_iota(jnp.int32, (8, 128), 1)
    low = lane < 64
    even = lane // 32 % 2 == 0
    half = [None] * 4
    for b in range(2):
        half[b] = jnp.where(low, values[b], pltpu.roll(values[b + 2], 64, 1))
        half[b + 2] = jnp.where(low, pltpu.roll(values[b], 64, 1), values[b + 2])
    full = [None] * 4
    for j in (0, 2):
        full[j] = jnp.where(even, half[j], pltpu.roll(half[j + 1], 32, 1))
        full[j + 1] = jnp.where(even, pltpu.roll(half[j], 96, 1), half[j + 1])
    return full


def pack_rows(in_ref, lanes, tiles):
    upper = lax.broadcasted_iota(jnp.int32, (8, 128), 0) < 4
    for t1 in range(16):
        groups = [None] * 4
        for high in range(2):
            real = in_ref[0, t1, 8 * high : 8 * high + 8, lanes]
            imag = in_ref[1, t1, 8 * high : 8 * high + 8, lanes]
            groups[2 * high] = jnp.where(upper, real, pltpu.roll(imag, 4, 0))
            groups[2 * high + 1] = jnp.where(upper, pltpu.roll(real, 4, 0), imag)
        for j, tile in enumerate(swap_lanes(groups)):
            tiles[j, t1] = tile


def pack_kernel(chunk, in_ref, out_ref, held, packed, arrived, left):
    def fetch(group):
        lanes = pl.ds(pl.multiple_of((4 * chunk + group) * 128, 128), 128)
        return pltpu.make_async_copy(
            in_ref.at[:, :, :, lanes], held.at[group], arrived.at[group]
        )

    def send(group):
        return pltpu.make_async_copy(
            packed.at[group], out_ref.at[pl.ds(4 * group, 4)], left.at[group]
        )

    for group in range(4):
        fetch(group).start()

    def step(group, carry):
        fetch(group).wait()
        pack_rows(held.at[group], slice(None), packed.at[group])
        send(group).start()
        return carry

    lax.fori_loop(0, 4, step, 0)
    for group in range(4):
        send(group).wait()


def pack(weights, chunk):
    return pl.pallas_call(
        partial(pack_kernel, chunk),
        in_specs=[pl.BlockSpec(memory_space=pl.ANY)],
        out_specs=pl.BlockSpec(memory_space=pl.ANY),
        out_shape=jax.ShapeDtypeStruct((PIECES, 16, 8, 128), jnp.float32),
        scratch_shapes=[
            pltpu.VMEM((4, 2, 16, 16, 128), jnp.float32),
            pltpu.VMEM((4, 4, 16, 8, 128), jnp.float32),
            pltpu.SemaphoreType.DMA((4,)),
            pltpu.SemaphoreType.DMA((4,)),
        ],
        cost_estimate=pl.CostEstimate(flops=10**6, bytes_accessed=2**21, transcendentals=0),
        name="pack",
    )(weights)


def merge_halves(out_ref, box, t1, low, high):
    upper = lax.broadcasted_iota(jnp.int32, (8, 128), 0) < 4
    out_ref[box, 0, t1] = jnp.where(upper, low, pltpu.roll(high, 4, 0))
    out_ref[box, 1, t1] = jnp.where(upper, pltpu.roll(low, 4, 0), high)


def join_kernel(in_ref, *refs):
    out_ref = refs[-1]

    def step(box, carry):
        for t1 in range(16):
            merge_halves(out_ref, box, t1, in_ref[2 * box, t1], in_ref[2 * box + 1, t1])
        return carry

    lax.fori_loop(0, 8, step, 0)


def join(received):
    in_vmem = pl.BlockSpec(memory_space=pltpu.VMEM)
    return pl.pallas_call(
        join_kernel,
        in_specs=[in_vmem],
        out_specs=in_vmem,
        out_shape=jax.ShapeDtypeStruct((8, 2, 16, 8, 128), jnp.float32),
        compiler_params=pltpu.CompilerParams(vmem_limit_bytes=VMEM_LIMIT),
        cost_estimate=pl.CostEstimate(flops=10**6, bytes_accessed=2**21, transcendentals=0),
        name="join",
    )(received)


def levels_kernel(
    chunk, ids, nodes, own, other, speeds, waves, lengths, last_one, last_two,
    last_lengths, first_table, second_table, *refs,
):
    outs = refs[0]
    boxes_a, boxes_b, sums, turned, mixed, last_phase = refs[-6:]
    row = (chunk * PIECES + ids[0]).astype(jnp.float32)
    core = ids[1]
    core_float = core.astype(jnp.float32)
    wave_two = waves[...]
    lane = lax.broadcasted_iota(jnp.int32, (8, 128), 1)
    along_two = ((lane % 32).astype(jnp.float32) + 0.5) * (1.0 / 32)
    second_phase = along_two * wave_two

    def first_point(level_index, low_code):
        span = 2.0 ** (level_index + 1)
        code = core_float * 2.0**level_index + low_code
        return (row * span + code + 0.5) * (1.0 / (32 * span))

    def speed_row(level_index, low_code):
        return jnp.broadcast_to(speeds[pl.ds(2**level_index - 1 + low_code, 1), :], (8, 128))

    def blend(slot, target, boxes):
        rows = sums[slot].astype(jnp.bfloat16)
        both = jnp.dot(first_table[...], rows, preferred_element_type=jnp.float32)
        total = both[:128] + both[128:]
        for n, box in enumerate(boxes):
            for part in range(2):
                column = 128 * (2 * n + part)
                target[box, part] = total[:, column : column + 128].reshape(16, 8, 128)

    def put(slot, first_row, column, real, imag):
        sums[slot, pl.ds(first_row, 8), 256 * column : 256 * column + 128] = real
        sums[slot, pl.ds(first_row, 8), 256 * column + 128 : 256 * column + 256] = imag

    def first_level(pair, slot):
        point = first_point(0, 0.0)
        speed = speed_row(0, 0)
        for n in range(2):
            box = 2 * pair + n
            for source, child in ((own, core), (other, 1 - core)):
                for t1 in range(16):
                    entry = (2 * box + child) * 16 + t1
                    phase = (point * nodes[entry] + second_phase) + speed * lengths[entry]
                    cosine, sine = turn(phase)
                    real = source[box, 0, t1]
                    imag = source[box, 1, t1]
                    first_row = pl.multiple_of(child * 128 + 8 * t1, 8)
                    put(slot, first_row, n, real * cosine + imag * sine, imag * cosine - real * sine)
        blend(slot, boxes_a, [2 * pair, 2 * pair + 1])

    def later_level(level_index, source, target, index, slot):
        low_bits = level_index - 1
        stride = 2**low_bits
        parent = index // stride
        low = index % stride
        code = jnp.int32(0)
        for bit in range(low_bits):
            code = code + low // 2**bit % 2 * 2 ** (low_bits - 1 - bit)
        before = first_point(level_index - 1, code.astype(jnp.float32))
        before_speed = speed_row(level_index - 1, code)
        points = [first_point(level_index, (2 * code + b).astype(jnp.float32)) for b in range(2)]
        point_speeds = [speed_row(level_index, 2 * code + b) for b in range(2)]
        first_box = parent * (2 * stride) + low
        for child in range(2):
            for t1 in range(16):
                entry = LEVEL_ROWS[level_index] + (2 * parent + child) * 16 + t1
                length = lengths[entry]
                wave = nodes[entry]
                real = source[first_box + child * stride, 0, t1]
                imag = source[first_box + child * stride, 1, t1]
                old = (before * wave + second_phase) + before_speed * length
                for b in range(2):
                    new = (points[b] * wave + second_phase) + point_speeds[b] * length
                    cosine, sine = turn(new - old)
                    first_row = child * 128 + 8 * t1
                    put(slot, first_row, b, real * cosine + imag * sine, imag * cosine - real * sine)
        blend(slot, target, [first_box, first_box + stride])

    def in_pairs(one):
        def step(half, carry):
            for slot in range(2):
                one(2 * half + slot, slot)
            return carry

        lax.fori_loop(0, 2, step, 0)

    in_pairs(first_level)
    in_pairs(partial(later_level, 1, boxes_a, boxes_b))
    in_pairs(partial(later_level, 2, boxes_b, boxes_a))
    in_pairs(partial(later_level, 3, boxes_a, boxes_b))

    fine_two = [((lane % 32).astype(jnp.float32) * 2.0 + (e + 0.5)) * (1.0 / 64) for e in range(2)]
    fine_phase = [fine_two[e] * wave_two for e in range(2)]

    def reversed_code(box):
        return box % 2 * 4 + box // 2 % 2 * 2 + box // 4

    def fine_speed(code, e):
        return jnp.broadcast_to(speeds[pl.ds(15 + 2 * code + e, 1), :], (8, 128))

    def rotate_box(box, carry):
        code = reversed_code(box)
        point = first_point(3, code.astype(jnp.float32))
        old_speed = speed_row(3, code)
        new_speeds = [fine_speed(code, e) for e in range(2)]
        for t1 in range(16):
            entry = LEVEL_ROWS[4] + t1
            length = lengths[entry]
            across = point * nodes[entry]
            real = boxes_b[box, 0, t1]
            imag = boxes_b[box, 1, t1]
            old = (across + second_phase) + old_speed * length
            for e in range(2):
                new = (across + fine_phase[e]) + new_speeds[e] * length
                cosine, sine = turn(new - old)
                first = pl.multiple_of((e * 256 + box * 32 + t1) * 8, 8)
                turned[pl.ds(first, 8), :] = real * cosine + imag * sine
                turned[pl.ds(first + 128, 8), :] = imag * cosine - real * sine
        return carry

    lax.fori_loop(0, 8, rotate_box, 0)

    for e in range(2):
        for a in range(4):
            last_phase[e, a] = fine_two[e] * last_two[a]

    total = None
    for j in range(4):
        rows = jnp.concatenate(
            [turned[pl.ds(2 * j + k, 512, stride=8), :] for k in range(2)], axis=1
        ).astype(jnp.bfloat16)
        for part in range(2):
            term = jnp.dot(rows, second_table[part, j], preferred_element_type=jnp.float32)
            total = term if total is None else total + term
    mixed[...] = total

    def finish_box(target, out):
        box, e = target // 2, target % 2
        code = reversed_code(box)
        point = first_point(3, code.astype(jnp.float32))
        speed = fine_speed(code, e)
        for high in range(2):
            across = point * last_one[high]
            first = pl.multiple_of(e * 256 + box * 32 + high * 8, 8)
            for a in range(4):
                phase = (across + last_phase[e, a]) + speed * last_lengths[high, a]
                cosine, sine = turn(phase)
                real = mixed[pl.ds(first, 8), 128 * a : 128 * a + 128]
                imag = mixed[pl.ds(first + 16, 8), 128 * a : 128 * a + 128]
                out[high * 4 + a] = real * cosine - imag * sine
                out[8 + high * 4 + a] = real * sine + imag * cosine

    def finish_row(major, carry):
        for minor in range(4):
            finish_box(4 * major + minor, outs.at[4 * major + minor])
        return carry

    lax.fori_loop(0, 4, finish_row, 0)


def levels(chunk, ids, own, other, speeds):
    nodes, waves, lengths = node_tables()
    last_one, last_two, last_lengths = final_tables()
    tables = (waves, lengths, last_one, last_two, last_lengths, first_weights(), second_weights())
    in_vmem = pl.BlockSpec(memory_space=pltpu.VMEM)
    in_smem = pl.BlockSpec(memory_space=pltpu.SMEM)
    return pl.pallas_call(
        partial(levels_kernel, chunk),
        in_specs=[in_smem, in_smem] + [in_vmem] * 10,
        out_specs=in_vmem,
        out_shape=jax.ShapeDtypeStruct((PIECES, 16, 8, 128), jnp.float32),
        scratch_shapes=[
            pltpu.VMEM((8, 2, 16, 8, 128), jnp.float32),
            pltpu.VMEM((8, 2, 16, 8, 128), jnp.float32),
            pltpu.VMEM((2, 256, 512), jnp.float32),
            pltpu.VMEM((4096, 128), jnp.float32),
            pltpu.VMEM((512, 512), jnp.float32),
            pltpu.VMEM((2, 4, 8, 128), jnp.float32),
        ],
        compiler_params=pltpu.CompilerParams(vmem_limit_bytes=VMEM_LIMIT),
        cost_estimate=pl.CostEstimate(flops=10**8, bytes_accessed=2**23, transcendentals=0),
        name="levels",
    )(ids, jnp.asarray(nodes), own, other, speeds, *[jnp.asarray(table) for table in tables])


def unpack_rows(tiles, rows, out_ref, lanes):
    for part in range(2):
        for high in range(2):
            block = part * 2 + high
            for a in range(4):
                values = [tiles[j, part * 8 + high * 4 + a] for j in range(4)]
                for b, tile in enumerate(swap_lanes(values)):
                    t2 = 4 * b + a
                    rows[block, 8 * t2 : 8 * t2 + 8, :] = tile
            for t1 in range(8):
                out_ref[part, high * 8 + t1, :, lanes] = rows[block, pl.ds(t1, 16, stride=8), :]


def unpack_kernel(*refs):
    unpack_rows(refs[0], refs[-1], refs[-2], slice(None))


def unpack(received, chunk, earlier):
    operands = [received]
    in_specs = [pl.BlockSpec((4, 16, 8, 128), lambda i: (i, 0, 0, 0))]
    aliases = {}
    if earlier is not None:
        aliases = {1: 0}
        operands.append(earlier)
        in_specs.append(pl.BlockSpec(memory_space=pl.ANY))
    return pl.pallas_call(
        unpack_kernel,
        grid=(4,),
        in_specs=in_specs,
        out_specs=pl.BlockSpec((2, 16, 16, 128), lambda i: (0, 0, 0, 4 * chunk + i)),
        out_shape=jax.ShapeDtypeStruct((2, 16, 16, 1024), jnp.float32),
        scratch_shapes=[pltpu.VMEM((4, 128, 128), jnp.float32)],
        input_output_aliases=aliases,
        compiler_params=pltpu.CompilerParams(vmem_limit_bytes=VMEM_LIMIT),
        cost_estimate=pl.CostEstimate(flops=10**6, bytes_accessed=2**21, transcendentals=0),
        name="unpack",
    )(*operands)


def speed_tables(speed_modes, core):
    numerators, spans = [], []
    for level_index in range(4):
        for code in range(2**level_index):
            numerators.append(core * 2**level_index + code)
            spans.append(2 ** (level_index + 1))
    for code in range(8):
        for e in range(2):
            numerators.append(core * 8 + code)
            spans.append(16)
    codes = jnp.stack(numerators).astype(jnp.float32)
    spans = jnp.asarray(np.array(spans), jnp.float32)
    me = lax.axis_index("bx") * 2 + lax.axis_index("by")
    rows = (jnp.arange(CHUNKS) * PIECES + me).astype(jnp.float32)
    target_one = (rows[:, None] * spans + codes + 0.5) / (TGT * spans)
    columns = jnp.arange(32).astype(jnp.float32)
    coarse = jnp.broadcast_to((columns + 0.5) / TGT, (15, 32))
    fine = jnp.stack([(2 * columns + e + 0.5) / (2 * TGT) for e in range(2)])
    target_two = jnp.concatenate([coarse, jnp.tile(fine, (8, 1))])
    target_one = jnp.broadcast_to(target_one[:, :, None], (CHUNKS, 31, 32))
    target_two = jnp.broadcast_to(target_two[None], (CHUNKS, 31, 32))
    speed = speed_of(speed_modes, target_one.reshape(-1), target_two.reshape(-1))
    return jnp.tile(speed.reshape(CHUNKS, 31, 32), (1, 1, 4))


def on_device_dealt(weights, speed_modes):
    local = weights.reshape(weights.shape[2:])
    core = lax.axis_index("cores")
    me = lax.axis_index("bx") * 2 + lax.axis_index("by")
    ids = jnp.stack([me, core]).astype(jnp.int32)
    speeds = speed_tables(speed_modes, core)

    received = [deal(pack(local, chunk)) for chunk in range(CHUNKS)]
    results = []
    for chunk in range(CHUNKS):
        own = join(received[chunk])
        other = partner_2(own, "cores", 0)
        results.append(deal(levels(chunk, ids, own, other, speeds[chunk])))
    out = None
    for chunk in range(CHUNKS):
        out = unpack(results[chunk], chunk, out)
    return out.reshape(weights.shape)


def deal(pieces):
    return lax.all_to_all(pieces, ("bx", "by"), 0, 0, tiled=True)


def solution(mesh):
    sizes = dict(mesh.shape)
    spec = P(("bx", "cores"), "by", None, None, None, None)
    dealt = (sizes["bx"], sizes["by"], sizes["cores"]) == (8, 2, 2)

    def whole(weights, speed_modes):
        fits = dealt and weights.shape[2:] == (2, 16, 16, 1024)
        return jax.shard_map(
            on_device_dealt if fits else on_device,
            mesh=mesh,
            in_specs=(spec, P()),
            out_specs=spec,
            check_vma=False,
        )(weights, speed_modes)

    return whole
```
